32 devices in a mesh: fsdp: 4 (over z), ctx: 8 (over y, x, core).
Axes of the slice: x: 2, y: 2, z: 4, core: 2. Of those that a mesh axis runs over, the one named last changes fastest.
Arguments:
- inputs: bfloat16 [4096, 2048], P(('fsdp', 'ctx')), may hold values from -6 to 6
- doc_lengths: int32 [4, 8], P('fsdp'), may hold values from 1 to 897, 1024 in all within a row
- gain_attn: bfloat16 [2048], P('fsdp'), may hold values from 0.25 to 1.75
- w_query: bfloat16 [2048, 2048], P('fsdp'), may hold values from -0.0625 to 0.0625
- w_key: bfloat16 [2048, 2048], P('fsdp'), may hold values from -0.0625 to 0.0625
- w_value: bfloat16 [2048, 2048], P('fsdp'), may hold values from -0.125 to 0.125
- w_out: bfloat16 [2048, 2048], P('fsdp'), may hold values from -0.5 to 0.5
- bias_table: bfloat16 [32, 32], replicated, may hold values from -4 to 4
- gain_ff: bfloat16 [2048], P('fsdp'), may hold values from 0.25 to 1.75
- w_gate: bfloat16 [2048, 5120], P('fsdp'), may hold values from -0.125 to 0.125
- w_up: bfloat16 [2048, 5120], P('fsdp'), may hold values from -0.125 to 0.125
- w_down: bfloat16 [5120, 2048], P('fsdp'), may hold values from -0.078125 to 0.078125
- cotangent: bfloat16 [4096, 2048], P(('fsdp', 'ctx')), may hold values from -6 to 6
Outputs:
- output: bfloat16 [4096, 2048], P(('fsdp', 'ctx'))
- input_grad: bfloat16 [4096, 2048], P(('fsdp', 'ctx'))
- attn_gain_grad: float32 [2048], P(('fsdp', 'ctx'))
- ff_gain_grad: float32 [2048], P(('fsdp', 'ctx'))
- query_weight_grad: float32 [2048, 2048], P(('fsdp', 'ctx'))
- key_weight_grad: float32 [2048, 2048], P(('fsdp', 'ctx'))
- value_weight_grad: float32 [2048, 2048], P(('fsdp', 'ctx'))
- out_weight_grad: float32 [2048, 2048], P(('fsdp', 'ctx'))
- bias_grad: float32 [1024], P(('fsdp', 'ctx'))
- gate_weight_grad: float32 [2048, 5120], P(('fsdp', 'ctx'))
- up_weight_grad: float32 [2048, 5120], P(('fsdp', 'ctx'))
- down_weight_grad: float32 [5120, 2048], P(('fsdp', 'ctx'))
The draws below stay inside these ranges and needn't reach their ends.
Inputs may be any that keep to these rules, and one draw needn't show every extreme that they name: `doc_lengths`: each row lists the lengths of the documents packed in order into one sequence; they sum to 1024, and the longest is exactly 897 tokens.
All inputs are finite; a program needn't handle non-finite values.
Results may differ from the reference program's by a relative error of at most 0.019.
Values may be sent and summed in bfloat16 or wider, within the bound.
No kernel may reach another device: no remote copies, remote signals or barrier semaphores. Data moves between devices by JAX's collectives and lax.ppermute only.
A program may use at most 448 MiB of HBM per device.

```python
import math
from functools import partial
import jax
import jax.numpy as jnp
import numpy as np
from jax import lax

D = 2048
H = 32
DH = 64
FF = 5120
BUCKETS = 32
NDOCS = 8
BLK = 128
LEN = 1024
SEQS = 4
TOKENS = 4096


def block_levels(rng, extent, shards, smallest, top_value):
    gain = 1.0
    for position, parts in shards:
        heights = jax.random.uniform(jax.random.fold_in(jax.random.fold_in(rng, 6), position), (parts,), jnp.float32, smallest / len(shards), top_value / len(shards))
        gain = gain * jnp.repeat(jnp.exp(heights), extent[position] // parts).reshape((-1,) + (1,) * (len(extent) - 1 - position))
    return gain


def profile(number_of, total, most, slope):
    portions = [(1 << 20) // math.isqrt(standing ** slope) + 1 for standing in range(2, number_of + 1)]
    rest, holding = total - most - (number_of - 1), [1] * (number_of - 1)
    while rest > 0:
        movable = [i for i in range(number_of - 1) if holding[i] < most]
        mass, budget = sum([portions[i] for i in movable]), rest
        for i in movable:
            addition = min(most - holding[i], max(1, budget * portions[i] // mass), rest)
            holding[i] = holding[i] + addition
            rest = rest - addition
    return np.array([most] + holding)


def ragged_sizes(own_key, number_of, total, reach, skew):
    if number_of == 2:
        one = jax.random.randint(own_key, (), max(1, total - reach), min(reach, total - 1) + 1)
        return jnp.stack([one, total - one])
    tallies = jnp.asarray(profile(number_of, total, reach, skew), jnp.int32)
    pairs = (number_of - 1) // 2
    source_of, receiver = tallies[1:1 + 2 * pairs:2], tallies[2:2 + 2 * pairs:2]
    slack = jnp.minimum(source_of - 1, reach - receiver)
    passed = jax.random.randint(jax.random.fold_in(own_key, 1), (pairs,), 0, 1 << 20) % (slack + 1)
    tallies = tallies.at[1:1 + 2 * pairs:2].set(source_of - passed).at[2:2 + 2 * pairs:2].set(receiver + passed)
    return tallies[jax.random.permutation(jax.random.fold_in(own_key, 2), number_of)]


def bell_draw(stream_key, dims, scale, bound, pieces=(), kind=jnp.bfloat16):
    values = scale * jax.random.normal(stream_key, dims, jnp.float32)
    if pieces:
        values = values * block_levels(stream_key, dims, pieces, -0.22, 0.18)
    return jnp.clip(values, -bound, bound).astype(kind)


def setup_inputs(seed: int = 0) -> dict:
    seeds = jax.random.split(jax.random.key(seed), 14)
    inputs = bell_draw(seeds[0], (TOKENS, D), 1.0, 6.0, ((0, 32),))
    doc_lengths = jax.vmap(lambda own: ragged_sizes(own, NDOCS, LEN, LEN - BLK + 1, 2))(jax.random.split(seeds[1], SEQS)).reshape((SEQS, NDOCS)).astype(jnp.int32)
    gain_attn = jnp.clip(1.0 + 0.15 * jax.random.normal(seeds[2], (D,), jnp.float32), 0.25, 1.75).astype(jnp.bfloat16)
    w_query = bell_draw(seeds[3], (D, D), (4 * D) ** -0.5, 0.0625, ((0, 4),))
    w_key = bell_draw(seeds[4], (D, D), (4 * D) ** -0.5, 0.0625, ((0, 4),))
    w_value = bell_draw(seeds[5], (D, D), D ** -0.5, 0.125, ((0, 4),))
    w_out = bell_draw(seeds[6], (D, D), (D // 16) ** -0.5, 0.5, ((0, 4),))
    bias_table = bell_draw(seeds[7], (BUCKETS, H), 1.0, 4.0)
    gain_ff = jnp.clip(1.0 + 0.15 * jax.random.normal(seeds[8], (D,), jnp.float32), 0.25, 1.75).astype(jnp.bfloat16)
    w_gate = bell_draw(seeds[9], (D, FF), D ** -0.5, 0.125, ((0, 4),))
    w_up = bell_draw(seeds[10], (D, FF), D ** -0.5, 0.125, ((0, 4),))
    w_down = bell_draw(seeds[11], (FF, D), FF ** -0.5, 0.078125, ((0, 4),))
    cotangent = bell_draw(seeds[12], (TOKENS, D), 1.0, 6.0, ((0, 32),))
    return dict(inputs=inputs, doc_lengths=doc_lengths, gain_attn=gain_attn, w_query=w_query, w_key=w_key, w_value=w_value, w_out=w_out, bias_table=bias_table, gain_ff=gain_ff, w_gate=w_gate, w_up=w_up, w_down=w_down, cotangent=cotangent)


epsilon = 1e-06
score_masked_rows = -1000000000.0
bucket_edges = (12, 16, 23, 32, 46, 64, 91)
highest = lax.Precision.HIGHEST

@jax.custom_vjp
def low(v):
    return lax.optimization_barrier(v.astype(jnp.bfloat16)).astype(jnp.float32)

@jax.custom_vjp
def low_back(v):
    return v

def low_keep(v):
    return (low(v), None)

def low_pass(kept, grad):
    return (grad,)

def back_keep(v):
    return (v, None)

def back_low(kept, grad):
    return (low(grad),)
low.defvjp(low_keep, low_pass)
low_back.defvjp(back_keep, back_low)

def bucket_index(offset):
    distance = jnp.abs(offset)
    far_bucket = BUCKETS // 4 + sum(((distance >= boundary).astype(jnp.int32) for boundary in bucket_edges))
    within = jnp.where(distance < BUCKETS // 4, distance, far_bucket)
    return within + BUCKETS // 2 * (offset > 0).astype(jnp.int32)

def rms_scale(values, gain_row):
    mean_square = lax.optimization_barrier(jnp.mean(values * values, axis=-1, keepdims=True))
    return values * lax.rsqrt(mean_square + epsilon) * gain_row

def gated_mix(gate_part, up_part):
    return jax.nn.gelu(gate_part, approximate=True) * up_part

def segment_table(doc_row, total_rows):
    doc_ends = jnp.cumsum(doc_row)
    positions = jnp.arange(total_rows, dtype=jnp.int32)
    return lax.optimization_barrier(jnp.sum((positions[:, None] >= doc_ends[None, :]).astype(jnp.int32), axis=1)).astype(jnp.int32)

def product(left_side, right_side):
    return jnp.dot(left_side, right_side, precision=highest)

def attend_heads(queries, key_heads, value_heads, bucket_table_entries, segment_row):
    length = queries.shape[0]
    block_rows = 512 if length % 512 == 0 else length
    key_index = jnp.arange(length, dtype=jnp.int32)

    def one_block(first_row):
        query_part = lax.dynamic_slice_in_dim(queries, first_row, block_rows, 0)
        query_index = first_row + jnp.arange(block_rows, dtype=jnp.int32)
        query_segment = lax.dynamic_slice_in_dim(segment_row, first_row, block_rows, 0)
        buckets = bucket_index(key_index[None, :] - query_index[:, None])
        bias_portion = jnp.transpose(bucket_table_entries[buckets], (2, 0, 1))
        raw_scores = jnp.einsum('qhd,khd->hqk', query_part, key_heads, precision=highest)
        raw_scores = low_back(raw_scores + bias_portion)
        same_doc = query_segment[:, None] == segment_row[None, :]
        masked = jnp.where(same_doc[None], raw_scores, score_masked_rows)
        probabilities = jax.nn.softmax(masked, axis=-1)
        return jnp.einsum('hqk,khd->qhd', low(probabilities), value_heads, precision=highest)
    starts = jnp.arange(length // block_rows, dtype=jnp.int32) * block_rows
    blocks = lax.map(jax.checkpoint(one_block), starts)
    return blocks.reshape(length, H * DH)

def sequence_layer(seq_rows, segment_row, gain_first, query_weight, key_weight, value_weight, output_weight, bucket_table_entries, gain_second, gate_weight, up_weight, down_weight):
    normed = low(rms_scale(seq_rows, gain_first))
    queries = low(low_back(product(normed, query_weight))).reshape(-1, H, DH)
    key_heads = low(low_back(product(normed, key_weight))).reshape(-1, H, DH)
    value_heads = low(low_back(product(normed, value_weight))).reshape(-1, H, DH)
    context = low(low_back(attend_heads(queries, key_heads, value_heads, bucket_table_entries, segment_row)))
    residual = seq_rows + low_back(product(context, output_weight))
    normed_ff = low(rms_scale(residual, gain_second))
    gate_pre = low_back(product(normed_ff, gate_weight))
    up_pre = low_back(product(normed_ff, up_weight))
    active = low(gated_mix(gate_pre, up_pre))
    return residual + low_back(product(active, down_weight))

def reference(inputs, doc_lengths, gain_attn, w_query, w_key, w_value, w_out, bias_table, gain_ff, w_gate, w_up, w_down, cotangent):
    segments = jax.vmap(partial(segment_table, total_rows=LEN))(doc_lengths)

    def whole_layer(source, gain_first, query_weight, key_weight, value_weight, output_weight, bucket_table_entries, gain_second, gate_weight, up_weight, down_weight):
        sequences = source.reshape(SEQS, LEN, D)

        def per_sequence(carried, seq_item):
            seq_rows, segment_row = seq_item
            return (carried, sequence_layer(seq_rows, segment_row, gain_first, query_weight, key_weight, value_weight, output_weight, bucket_table_entries, gain_second, gate_weight, up_weight, down_weight))
        _, results = lax.scan(per_sequence, jnp.zeros((), jnp.int32), (sequences, segments))
        return results.reshape(SEQS * LEN, D)
    floats = tuple((array_in.astype(jnp.float32) for array_in in (inputs, gain_attn, w_query, w_key, w_value, w_out, bias_table, gain_ff, w_gate, w_up, w_down)))
    result_rows, pullback = jax.vjp(whole_layer, *floats)
    gradients = pullback(cotangent.astype(jnp.float32))
    input_grad, attn_gain_grad, query_grad, key_grad, value_grad, out_grad, table_grad, ff_gain_grad, gate_grad, up_grad, down_grad = gradients
    return (result_rows.astype(jnp.bfloat16), input_grad.astype(jnp.bfloat16), attn_gain_grad, ff_gain_grad, query_grad, key_grad, value_grad, out_grad, table_grad.reshape(BUCKETS * H), gate_grad, up_grad, down_grad)
```

```python
import functools

import jax
import jax.numpy as jnp
from jax import lax
from jax.experimental import pallas as pl
from jax.experimental.pallas import tpu as pltpu
from jax.sharding import PartitionSpec as P

H = 32
DH = 64
BUCKETS = 32
TILE = 128
PAIR = 2
CLASSES = 5

epsilon = 1e-06
score_masked_rows = -1000000000.0
bucket_edges = (12, 16, 23, 32, 46, 64, 91)
f32 = jnp.float32
bf16 = jnp.bfloat16
NT = (((1,), (1,)), ((), ()))
VMEM_BYTES = 56 * 1024 * 1024


def bucket_index(offset):
    distance = jnp.abs(offset)
    far_bucket = BUCKETS // 4 + sum(
        ((distance >= boundary).astype(jnp.int32) for boundary in bucket_edges)
    )
    within = jnp.where(distance < BUCKETS // 4, distance, far_bucket)
    return within + BUCKETS // 2 * (offset > 0).astype(jnp.int32)


def rms_scale(values, gain_row):
    mean_square = jnp.mean(values * values, axis=-1, keepdims=True)
    return values * lax.rsqrt(mean_square + epsilon) * gain_row


def gated_mix(gate_part, up_part):
    return jax.nn.gelu(gate_part, approximate=True) * up_part


def segment_table(doc_row, total_rows):
    doc_ends = jnp.cumsum(doc_row)
    positions = jnp.arange(total_rows, dtype=jnp.int32)
    return jnp.sum((positions[:, None] >= doc_ends[None, :]).astype(jnp.int32), axis=1)


def dot(left, right, contract=((1,), (0,))):
    return lax.dot_general(left, right, (contract, ((), ())), preferred_element_type=f32)


def swap(block, mask):
    return lax.ppermute(block, "ctx", [(i, i ^ mask) for i in range(lax.axis_size("ctx"))])


def by_exchange():
    return lax.axis_size("ctx") == 8


def plane_gather(block):
    if not by_exchange():
        return lax.all_gather(block, "ctx", axis=0, tiled=True)
    half = block.shape[0] // 2
    from_x, from_y, from_core = swap(block, 2), swap(block, 4), swap(block, 1)
    diagonal = jnp.concatenate([swap(from_x[:half], 4), swap(from_y[half:], 2)], axis=0)
    x_core, y_core = swap(from_x, 1), swap(from_y, 1)
    return jnp.concatenate(
        [block, from_core, from_x, x_core, from_y, y_core, diagonal, swap(diagonal, 1)], axis=0
    )


def plane_scatter(partial):
    if not by_exchange():
        return lax.psum_scatter(partial, "ctx", scatter_dimension=0, tiled=True).astype(f32)
    rows = partial.shape[0] // 8
    half = rows // 2

    def slot(m):
        return partial[m * rows : (m + 1) * rows]

    def chip(m):
        return slot(m).astype(f32) + swap(slot(m + 1), 1).astype(f32)

    diagonal = chip(6).astype(bf16)
    via_x, via_y = swap(diagonal[:half], 2), swap(diagonal[half:], 4)
    y_sum, x_sum = chip(4), chip(2)
    y_sum = jnp.concatenate([y_sum[:half] + via_x.astype(f32), y_sum[half:]], axis=0)
    x_sum = jnp.concatenate([x_sum[:half], x_sum[half:] + via_y.astype(f32)], axis=0)
    return chip(0) + swap(x_sum.astype(bf16), 2).astype(f32) + swap(y_sum.astype(bf16), 4).astype(f32)


def line_gather(small):
    parts = lax.axis_size("fsdp")
    own = lax.axis_index("fsdp")
    whole = jnp.zeros((parts,) + small.shape, small.dtype)
    for step in range(parts):
        piece = (
            small
            if step == 0
            else lax.ppermute(small, "fsdp", [(i, (i + step) % parts) for i in range(parts)])
        )
        whole = lax.dynamic_update_index_in_dim(whole, piece, (own - step) % parts, 0)
    return jnp.transpose(whole, (1, 0, 2)).reshape(small.shape[0], -1)


def tiles_kernel(table_ref, out_ref):
    heads = out_ref.shape[0]
    row = lax.broadcasted_iota(jnp.int32, (TILE, TILE), 0)
    column = lax.broadcasted_iota(jnp.int32, (TILE, TILE), 1)

    def one_head(h, _):
        for kind in range(CLASSES):
            bucket = bucket_index(row - column + (kind - 2) * TILE)
            first, last = (0, BUCKETS // 2) if kind < 2 else (BUCKETS // 2, BUCKETS)
            if kind == 2:
                first = 0
            tile = jnp.zeros((TILE, TILE), f32)
            for b in range(first, last):
                tile = jnp.where(bucket == b, table_ref[b, h], tile)
            out_ref[h, kind] = tile
        return 0

    lax.fori_loop(0, heads, one_head, 0)


def bias_tiles(table):
    heads = table.shape[1]
    return pl.pallas_call(
        tiles_kernel,
        out_shape=jax.ShapeDtypeStruct((heads, CLASSES, TILE, TILE), f32),
        in_specs=[pl.BlockSpec(memory_space=pltpu.SMEM)],
        out_specs=pl.BlockSpec(memory_space=pltpu.VMEM),
        name="bias_tiles",
    )(table)


def fold(tile, reduce):
    return reduce(tile.reshape(TILE // 8, 8, TILE), axis=0)


def tile_class(base, key_slot, query_slot):
    difference = lax.bitwise_xor(base, key_slot) - lax.bitwise_xor(base, query_slot)
    return jnp.clip(difference, -2, 2) + 2


def score_tile(base, h, a, i, q_i, k_ref, seg_keys, seg_i, tiles_ref):
    s = lax.dot_general(
        k_ref[a * TILE : (a + 1) * TILE, h * DH : (h + 1) * DH], q_i, NT, preferred_element_type=f32
    )
    kind = tile_class(base, jnp.int32(a), i)
    s = s + tiles_ref[h, kind]
    return jnp.where(seg_keys[a * TILE : (a + 1) * TILE, :] == seg_i, s, score_masked_rows), kind


def forward_kernel(base_ref, q_ref, k_ref, v_ref, segk_ref, segq_ref, tiles_ref, ctx_ref, log_ref, s_scr, p_scr):
    blocks = q_ref.shape[0] // TILE
    base = base_ref[0]
    for h in range(PAIR):
        v_t = v_ref[:, h * DH : (h + 1) * DH].astype(f32).T.astype(bf16)

        def one_block(i, _, h=h, v_t=v_t):
            start = pl.multiple_of(i * TILE, TILE)
            q_i = q_ref[pl.ds(start, TILE), h * DH : (h + 1) * DH]
            seg_i = segq_ref[pl.ds(i, 1), :]
            top = jnp.full((8, TILE), -jnp.inf, f32)
            for a in range(blocks):
                s, _ = score_tile(base, h, a, i, q_i, k_ref, segk_ref, seg_i, tiles_ref)
                s_scr[a * TILE : (a + 1) * TILE, :] = s
                top = jnp.maximum(top, fold(s, jnp.max))
            top = jnp.max(top, axis=0, keepdims=True)
            total = jnp.zeros((8, TILE), f32)
            for a in range(blocks):
                e = jnp.exp(s_scr[a * TILE : (a + 1) * TILE, :] - top)
                p_scr[a * TILE : (a + 1) * TILE, :] = e.astype(bf16)
                total = total + fold(e, jnp.sum)
            total = jnp.sum(total, axis=0, keepdims=True)
            context = lax.dot_general(
                v_t, p_scr[...], (((1,), (0,)), ((), ())), preferred_element_type=f32
            )
            ctx_ref[h * DH : (h + 1) * DH, pl.ds(start, TILE)] = (context / total).astype(bf16)
            log_ref[0, h, pl.ds(i, 1), :] = top + jnp.log(total)
            return 0

        lax.fori_loop(0, blocks, one_block, 0)


def attend(base, q, k, v, seg_keys, seg_queries, tiles):
    rows, width = q.shape
    pairs, blocks = width // (PAIR * DH), rows // TILE
    one_pair = pl.BlockSpec((rows, PAIR * DH), lambda j: (0, j))
    return pl.pallas_call(
        forward_kernel,
        grid=(pairs,),
        out_shape=(
            jax.ShapeDtypeStruct((width, rows), bf16),
            jax.ShapeDtypeStruct((pairs, PAIR, blocks, TILE), f32),
        ),
        in_specs=[
            pl.BlockSpec(memory_space=pltpu.SMEM),
            one_pair,
            one_pair,
            one_pair,
            pl.BlockSpec((rows, TILE), lambda j: (0, 0)),
            pl.BlockSpec((blocks, TILE), lambda j: (0, 0)),
            pl.BlockSpec((PAIR, CLASSES, TILE, TILE), lambda j: (j, 0, 0, 0)),
        ],
        out_specs=(
            pl.BlockSpec((PAIR * DH, rows), lambda j: (j, 0)),
            pl.BlockSpec((1, PAIR, blocks, TILE), lambda j: (j, 0, 0, 0)),
        ),
        scratch_shapes=[pltpu.VMEM((rows, TILE), f32), pltpu.VMEM((rows, TILE), bf16)],
        compiler_params=pltpu.CompilerParams(vmem_limit_bytes=VMEM_BYTES),
        name="attend_forward",
    )(base, q, k, v, seg_keys, seg_queries, tiles)


def backward_kernel(
    base_ref, q_ref, k_ref, v_ref, do_ref, log_ref, segk_ref, segq_ref, tiles_ref,
    dq_ref, dk_ref, dv_ref, bias_ref,
    p_scr, dp_scr, p_all, ds_all, near,
):
    rows = q_ref.shape[0]
    blocks = rows // TILE
    base = base_ref[0]
    row = lax.broadcasted_iota(jnp.int32, (TILE, TILE), 0)
    column = lax.broadcasted_iota(jnp.int32, (TILE, TILE), 1)
    for h in range(PAIR):
        lanes = slice(h * DH, (h + 1) * DH)
        near[...] = jnp.zeros_like(near)

        def one_block(i, _, h=h, lanes=lanes):
            start = pl.multiple_of(i * TILE, TILE)
            q_i = q_ref[pl.ds(start, TILE), lanes]
            do_i = do_ref[pl.ds(start, TILE), lanes]
            seg_i = segq_ref[pl.ds(i, 1), :]
            log_i = log_ref[0, h, pl.ds(i, 1), :]
            delta = jnp.zeros((8, TILE), f32)
            for a in range(blocks):
                here = slice(a * TILE, (a + 1) * TILE)
                s, _ = score_tile(base, h, a, i, q_i, k_ref, segk_ref, seg_i, tiles_ref)
                p = jnp.exp(s - log_i)
                dp = lax.dot_general(v_ref[here, lanes], do_i, NT, preferred_element_type=f32)
                delta = delta + fold(p * dp, jnp.sum)
                p_scr[here, :] = p
                dp_scr[here, :] = dp
                p_all[here, pl.ds(start, TILE)] = p.astype(bf16)
            delta = jnp.sum(delta, axis=0, keepdims=True)
            for a in range(blocks):
                here = slice(a * TILE, (a + 1) * TILE)
                ds = (p_scr[here, :] * (dp_scr[here, :] - delta)).astype(bf16)
                ds_all[here, pl.ds(start, TILE)] = ds
                kind = tile_class(base, jnp.int32(a), i)
                near[kind] = near[kind] + ds.astype(f32)
            return 0

        lax.fori_loop(0, blocks, one_block, 0)
        q_h, do_h = q_ref[:, lanes], do_ref[:, lanes]
        k_t = k_ref[:, lanes].astype(f32).T.astype(bf16)

        def products(a, _, lanes=lanes, q_h=q_h, do_h=do_h, k_t=k_t, h=h):
            here = pl.ds(pl.multiple_of(a * 2 * TILE, 2 * TILE), 2 * TILE)
            dv_ref[here, lanes] = jnp.dot(p_all[here, :], do_h, preferred_element_type=f32).astype(bf16)
            dk_ref[here, lanes] = jnp.dot(ds_all[here, :], q_h, preferred_element_type=f32).astype(bf16)
            dq_ref[lanes, here] = jnp.dot(k_t, ds_all[:, here], preferred_element_type=f32).astype(bf16)
            return 0

        lax.fori_loop(0, blocks // 2, products, 0)
        for b in range(BUCKETS):
            part = jnp.zeros((8, TILE), f32)
            low = b < BUCKETS // 2
            for kind in (1, 2) if low else (2, 3):
                bucket = bucket_index(row - column + (kind - 2) * TILE)
                part = part + fold(jnp.where(bucket == b, near[kind], 0.0), jnp.sum)
            if b == BUCKETS // 2 - 1:
                part = part + fold(near[0], jnp.sum)
            if b == BUCKETS - 1:
                part = part + fold(near[4], jnp.sum)
            bias_ref[h, b] = part


def attend_back(base, q, k, v, context_grad, log_total, seg_keys, seg_queries, tiles):
    rows, width = q.shape
    pairs, blocks = width // (PAIR * DH), rows // TILE
    one_pair = pl.BlockSpec((rows, PAIR * DH), lambda j: (0, j))
    return pl.pallas_call(
        backward_kernel,
        grid=(pairs,),
        out_shape=(
            jax.ShapeDtypeStruct((width, rows), bf16),
            jax.ShapeDtypeStruct((rows, width), bf16),
            jax.ShapeDtypeStruct((rows, width), bf16),
            jax.ShapeDtypeStruct((pairs * PAIR, BUCKETS, 8, TILE), f32),
        ),
        in_specs=[
            pl.BlockSpec(memory_space=pltpu.SMEM),
            one_pair,
            one_pair,
            one_pair,
            one_pair,
            pl.BlockSpec((1, PAIR, blocks, TILE), lambda j: (j, 0, 0, 0)),
            pl.BlockSpec((rows, TILE), lambda j: (0, 0)),
            pl.BlockSpec((blocks, TILE), lambda j: (0, 0)),
            pl.BlockSpec((PAIR, CLASSES, TILE, TILE), lambda j: (j, 0, 0, 0)),
        ],
        out_specs=(
            pl.BlockSpec((PAIR * DH, rows), lambda j: (j, 0)),
            one_pair,
            one_pair,
            pl.BlockSpec((PAIR, BUCKETS, 8, TILE), lambda j: (j, 0, 0, 0)),
        ),
        scratch_shapes=[
            pltpu.VMEM((rows, TILE), f32),
            pltpu.VMEM((rows, TILE), f32),
            pltpu.VMEM((rows, rows), bf16),
            pltpu.VMEM((rows, rows), bf16),
            pltpu.VMEM((CLASSES, TILE, TILE), f32),
        ],
        compiler_params=pltpu.CompilerParams(vmem_limit_bytes=VMEM_BYTES),
        name="attend_backward",
    )(base, q, k, v, context_grad, log_total, seg_keys, seg_queries, tiles)


def per_device(
    inputs,
    doc_lengths,
    gain_attn,
    w_query,
    w_key,
    w_value,
    w_out,
    bias_table,
    gain_ff,
    w_gate,
    w_up,
    w_down,
    cotangent,
):
    rows, width = inputs.shape
    planes, members = lax.axis_size("fsdp"), lax.axis_size("ctx")
    me = lax.axis_index("ctx")
    length = rows * members
    heads = H // members
    hidden = w_gate.shape[1] // members
    model = heads * DH
    striped = H % (planes * members) == 0

    def columns(weight, pieces):
        cut = weight.shape[1] // (pieces * members)
        split = weight.reshape(weight.shape[0], pieces, members, cut)
        return lax.dynamic_index_in_dim(split, me, 2, False).reshape(weight.shape[0], pieces * cut)

    def own_rows(weight):
        count = weight.shape[0] // members
        return lax.dynamic_slice_in_dim(weight, me * count, count, 0)

    def over_planes(weight):
        return lax.all_gather(weight, "fsdp", axis=0, tiled=True)

    head_pieces = planes if striped else 1
    w_qkv = over_planes(
        jnp.concatenate([columns(w, head_pieces) for w in (w_query, w_key, w_value)], axis=1)
    )
    if striped:
        out_rows = over_planes(own_rows(w_out))
    else:
        out_rows = lax.dynamic_slice_in_dim(over_planes(w_out), me * model, model, 0)
    w_mix = over_planes(jnp.concatenate([columns(w_gate, planes), columns(w_up, planes)], axis=1))
    down_rows = over_planes(own_rows(w_down))
    gains = line_gather(jnp.stack([gain_attn, gain_ff])).astype(f32)
    gain_first, gain_second = gains[0], gains[1]

    base = me if by_exchange() else jnp.zeros_like(me)
    slots = jnp.arange(members, dtype=jnp.int32)
    segments = segment_table(doc_lengths[0], length).reshape(members, rows)
    seg_queries = jnp.take(segments, lax.bitwise_xor(base, slots), axis=0)
    seg_queries = seg_queries.reshape(length // TILE, TILE)
    seg_keys = jnp.broadcast_to(seg_queries.reshape(length, 1), (length, TILE))
    base_block = jnp.reshape(base, (1,)).astype(jnp.int32)
    if striped:
        unit = H // (planes * members)
        order = jnp.arange(heads, dtype=jnp.int32)
        own_heads = order // unit * (H // planes) + me * unit + order % unit
    else:
        own_heads = me * heads + jnp.arange(heads, dtype=jnp.int32)
    pick = (jnp.arange(H, dtype=jnp.int32)[:, None] == own_heads[None, :]).astype(f32)
    table = jnp.dot(bias_table.astype(f32), pick, precision=lax.Precision.HIGHEST)
    tiles = bias_tiles(table)

    source_all = plane_gather(inputs)
    normed = rms_scale(source_all.astype(f32), gain_first).astype(bf16)
    qkv = dot(normed, w_qkv).astype(bf16)
    q, k, v = qkv[:, :model], qkv[:, model : 2 * model], qkv[:, 2 * model :]
    context_t, log_total = attend(base_block, q, k, v, seg_keys, seg_queries, tiles)
    grad_all = plane_gather(cotangent)
    source = inputs.astype(f32)
    residual = source + plane_scatter(dot(context_t, out_rows, ((0,), (0,))).astype(bf16))

    normed_ff = plane_gather(rms_scale(residual, gain_second).astype(bf16))
    mix = dot(normed_ff, w_mix)
    gate_pre, up_pre = mix[:, :hidden], mix[:, hidden:]
    active_f, mix_back = jax.vjp(gated_mix, gate_pre, up_pre)
    active = active_f.astype(bf16)
    down_grad = dot(active, grad_all, ((0,), (0,))).astype(bf16)
    active_grad = dot(grad_all, down_rows, ((1,), (1,)))
    gate_grad, up_grad = mix_back(active_grad)
    mix_grad = jnp.concatenate([gate_grad.astype(bf16), up_grad.astype(bf16)], axis=1)
    normed_ff_grad = plane_scatter(dot(mix_grad, w_mix, ((1,), (1,))).astype(bf16))
    output_sum = plane_scatter(dot(active, down_rows).astype(bf16))
    output = (residual + output_sum).astype(bf16)
    mix_weight_grad = dot(normed_ff, mix_grad, ((0,), (0,))).astype(bf16)
    norm_back = jax.vjp(rms_scale, residual, gain_second)[1]
    residual_part, ff_gain_grad = norm_back(normed_ff_grad)
    residual_grad = cotangent.astype(f32) + residual_part

    residual_low = plane_gather(residual_grad.astype(bf16))
    context_grad = dot(residual_low, out_rows, ((1,), (1,))).astype(bf16)
    out_weight_grad = dot(context_t, residual_low).astype(bf16)
    query_grad_t, key_grad, value_grad, bias_parts = attend_back(
        base_block, q, k, v, context_grad, log_total, seg_keys, seg_queries, tiles
    )
    w_q, w_kv = w_qkv[:, :model], w_qkv[:, model:]
    kv_grad = jnp.concatenate([key_grad, value_grad], axis=1)
    normed_grad = plane_scatter(
        (dot(query_grad_t, w_q, ((0,), (1,))) + dot(kv_grad, w_kv, ((1,), (1,)))).astype(bf16)
    )
    qkv_weight_grad = jnp.concatenate(
        [dot(normed, query_grad_t, ((0,), (1,))), dot(normed, kv_grad, ((0,), (0,)))], axis=1
    ).astype(bf16)
    first_back = jax.vjp(rms_scale, source, gain_first)[1]
    source_part, attn_gain_grad = first_back(normed_grad)
    input_grad = (residual_grad + source_part).astype(bf16)

    def sum_planes(partial):
        return lax.psum_scatter(partial, "fsdp", scatter_dimension=0, tiled=True)

    def to_rows(partial, kinds, pieces):
        summed = sum_planes(partial)
        cut = summed.shape[1] // (kinds * pieces)
        moved = lax.all_to_all(summed, "ctx", 0, 0, tiled=True)
        moved = moved.reshape(members, summed.shape[0] // members, kinds, pieces, cut)
        moved = jnp.transpose(moved, (2, 1, 3, 0, 4))
        return moved.reshape(kinds, moved.shape[1], pieces * members * cut).astype(f32)

    down_shard = sum_planes(down_grad).astype(f32)
    gate_shard, up_shard = to_rows(mix_weight_grad, 2, planes)
    if striped:
        out_shard = sum_planes(out_weight_grad).astype(f32)
    else:
        placed = jnp.zeros((H * DH, width), f32)
        placed = lax.dynamic_update_slice_in_dim(placed, out_weight_grad.astype(f32), me * model, 0)
        out_shard = lax.psum_scatter(placed, ("fsdp", "ctx"), scatter_dimension=0, tiled=True)
    query_shard, key_shard, value_shard = to_rows(qkv_weight_grad, 3, head_pieces)
    bias_own = jnp.sum(bias_parts, axis=(2, 3))
    bias_rows = jnp.dot(bias_own.T, pick.T, precision=lax.Precision.HIGHEST)
    small = [attn_gain_grad, ff_gain_grad, bias_rows.reshape(BUCKETS * H)]
    small = [lax.psum_scatter(s, ("fsdp", "ctx"), scatter_dimension=0, tiled=True) for s in small]
    return (
        output,
        input_grad,
        small[0],
        small[1],
        query_shard,
        key_shard,
        value_shard,
        out_shard,
        small[2],
        gate_shard,
        up_shard,
        down_shard,
    )


def solution(mesh):
    rows = P(("fsdp", "ctx"), None)
    vector = P(("fsdp", "ctx"))
    weight = P("fsdp", None)
    return jax.shard_map(
        per_device,
        mesh=mesh,
        in_specs=(
            rows,
            P("fsdp", None),
            P("fsdp"),
            weight,
            weight,
            weight,
            weight,
            P(),
            P("fsdp"),
            weight,
            weight,
            weight,
            rows,
        ),
        out_specs=(rows, rows, vector, vector, rows, rows, rows, rows, vector, rows, rows, rows),
        check_vma=False,
    )
```

```python
import functools

import jax
import jax.numpy as jnp
from jax import lax
from jax.experimental import pallas as pl
from jax.experimental.pallas import tpu as pltpu
from jax.sharding import PartitionSpec as P

H = 32
DH = 64
BUCKETS = 32
TILE = 128
PAIR = 2
CLASSES = 5

epsilon = 1e-06
score_masked_rows = -1000000000.0
bucket_edges = (12, 16, 23, 32, 46, 64, 91)
f32 = jnp.float32
bf16 = jnp.bfloat16
NT = (((1,), (1,)), ((), ()))
VMEM_BYTES = 56 * 1024 * 1024


def bucket_index(offset):
    distance = jnp.abs(offset)
    far_bucket = BUCKETS // 4 + sum(
        ((distance >= boundary).astype(jnp.int32) for boundary in bucket_edges)
    )
    within = jnp.where(distance < BUCKETS // 4, distance, far_bucket)
    return within + BUCKETS // 2 * (offset > 0).astype(jnp.int32)


def rms_scale(values, gain_row):
    mean_square = jnp.mean(values * values, axis=-1, keepdims=True)
    return values * lax.rsqrt(mean_square + epsilon) * gain_row


def gated_mix(gate_part, up_part):
    return jax.nn.gelu(gate_part, approximate=True) * up_part


def segment_table(doc_row, total_rows):
    doc_ends = jnp.cumsum(doc_row)
    positions = jnp.arange(total_rows, dtype=jnp.int32)
    return jnp.sum((positions[:, None] >= doc_ends[None, :]).astype(jnp.int32), axis=1)


def dot(left, right, contract=((1,), (0,))):
    return lax.dot_general(left, right, (contract, ((), ())), preferred_element_type=f32)


def swap(block, mask):
    return lax.ppermute(block, "ctx", [(i, i ^ mask) for i in range(lax.axis_size("ctx"))])


def by_exchange():
    return lax.axis_size("ctx") == 8


def plane_gather(block):
    if not by_exchange():
        return lax.all_gather(block, "ctx", axis=0, tiled=True)
    half = block.shape[0] // 2
    from_x, from_y, from_core = swap(block, 2), swap(block, 4), swap(block, 1)
    diagonal = jnp.concatenate([swap(from_x[:half], 4), swap(from_y[half:], 2)], axis=0)
    x_core, y_core = swap(from_x, 1), swap(from_y, 1)
    return jnp.concatenate(
        [block, from_core, from_x, x_core, from_y, y_core, diagonal, swap(diagonal, 1)], axis=0
    )


def scatter_chips(partial):
    if not by_exchange():
        return partial
    rows = partial.shape[0] // 8

    def chip(m):
        mine, other = partial[m * rows : (m + 1) * rows], partial[(m + 1) * rows : (m + 2) * rows]
        return mine.astype(f32) + swap(other, 1).astype(f32)

    diagonal = chip(6).astype(bf16)
    return [chip(0), chip(2), chip(4), diagonal]


def scatter_corner(sums):
    if not by_exchange():
        return sums
    own, x_sum, y_sum, diagonal = sums
    half = own.shape[0] // 2
    via_x, via_y = swap(diagonal[:half], 2), swap(diagonal[half:], 4)
    y_sum = jnp.concatenate([y_sum[:half] + via_x.astype(f32), y_sum[half:]], axis=0)
    x_sum = jnp.concatenate([x_sum[:half], x_sum[half:] + via_y.astype(f32)], axis=0)
    return [own, x_sum.astype(bf16), y_sum.astype(bf16)]


def scatter_sides(sums):
    if not by_exchange():
        return lax.psum_scatter(sums, "ctx", scatter_dimension=0, tiled=True).astype(f32)
    own, x_sum, y_sum = sums
    return own + swap(x_sum, 2).astype(f32) + swap(y_sum, 4).astype(f32)


def plane_scatter(partial):
    return scatter_sides(scatter_corner(scatter_chips(partial)))


def line_gather(small):
    parts = lax.axis_size("fsdp")
    own = lax.axis_index("fsdp")
    whole = jnp.zeros((parts,) + small.shape, small.dtype)
    for step in range(parts):
        piece = (
            small
            if step == 0
            else lax.ppermute(small, "fsdp", [(i, (i + step) % parts) for i in range(parts)])
        )
        whole = lax.dynamic_update_index_in_dim(whole, piece, (own - step) % parts, 0)
    return jnp.transpose(whole, (1, 0, 2)).reshape(small.shape[0], -1)


def cut_plan(cut, members):
    window = max(-(-((cut * p) % TILE + cut) // TILE) for p in range(members))
    return window, members * cut // TILE - window


def cut_kernel(start_ref, *refs, pieces, window, cut, moves, along):
    out_ref = refs[-1]
    if along:
        rows_ref = refs[-2]
        count, groups = rows_ref.shape[0], rows_ref.shape[1] // along
        for group in range(groups):
            part = rows_ref[:, group * along : (group + 1) * along]
            out_ref[group * count : (group + 1) * count, out_ref.shape[1] - along :] = part
    shift = start_ref[1]
    held = {}
    for source, piece, first, length, target in moves:
        if (source, piece) not in held:
            at = (source * pieces + piece) * window
            span = jnp.concatenate([r[...].astype(f32) for r in refs[at : at + window]], axis=1)
            held[source, piece] = pltpu.roll(span, shift, 1)
        part = held[source, piece][:, first : first + length]
        out_ref[:, target : target + length] = part.astype(bf16)


def cut_columns(weights, pieces, me, members, moves, name, along=None):
    rows, width = weights[0].shape
    cut = width // (pieces * members)
    window, most = cut_plan(cut, members)
    blocks = width // pieces // TILE
    start = jnp.minimum(cut * me // TILE, most)
    shift = (window * TILE - (cut * me - start * TILE)) % (window * TILE)
    step = min(rows, 256)
    specs = []
    for _ in weights:
        for piece in range(pieces):
            for w in range(window):
                place = piece * blocks + w
                specs.append(pl.BlockSpec((step, TILE), lambda r, s, place=place: (r, place + s[0])))
    columns = sum(move[3] for move in moves)
    operands = [w for w in weights for _ in range(pieces * window)]
    extra = 0
    if along is not None:
        count = along.shape[0] // members
        extra = count * along.shape[1] // rows
        columns += extra
        specs.append(pl.BlockSpec((count, step // count * extra), lambda r, s: (s[2], r)))
        operands.append(along)
    return pl.pallas_call(
        functools.partial(
            cut_kernel, pieces=pieces, window=window, cut=cut, moves=moves, along=extra
        ),
        grid_spec=pltpu.PrefetchScalarGridSpec(
            num_scalar_prefetch=1,
            grid=(rows // step,),
            in_specs=specs,
            out_specs=pl.BlockSpec((step, columns), lambda r, s: (r, 0)),
        ),
        out_shape=jax.ShapeDtypeStruct((rows, columns), bf16),
        name=name,
    )(jnp.stack([start, shift, me]).astype(jnp.int32), *operands)


def join_kernel(in_ref, *out_refs, pieces, cut, moves):
    members = in_ref.shape[0]
    for kind, piece, first, length, source in moves:
        for p in range(members):
            target = (piece * members + p) * cut + first
            out_refs[kind][:, target : target + length] = in_ref[p, :, source : source + length].astype(f32)


def join_columns(moved, kinds, pieces, moves, name):
    members, rows, columns = moved.shape
    cut = columns // (kinds * pieces)
    step = min(rows, 32)
    width = members * pieces * cut
    return pl.pallas_call(
        functools.partial(join_kernel, pieces=pieces, cut=cut, moves=moves),
        grid=(rows // step,),
        out_shape=[jax.ShapeDtypeStruct((rows, width), f32)] * kinds,
        in_specs=[pl.BlockSpec((members, step, columns), lambda r: (0, r, 0))],
        out_specs=[pl.BlockSpec((step, width), lambda r: (r, 0))] * kinds,
        name=name,
    )(moved)


def head_moves(pieces, heads):
    each = heads // pieces
    return [
        (kind, t // each, t % each * DH, DH, (t // PAIR * 3 + kind) * PAIR * DH + t % PAIR * DH)
        for t in range(heads)
        for kind in range(3)
    ]


def block_moves(kinds, pieces, cut):
    return [
        (kind, piece, 0, cut, (kind * pieces + piece) * cut)
        for kind in range(kinds)
        for piece in range(pieces)
    ]


def after_all(values, *others):
    return lax.optimization_barrier((values,) + others)[0]


def after(value, *others):
    return lax.optimization_barrier((value,) + others)[0]


def tiles_kernel(table_ref, out_ref):
    heads = out_ref.shape[0]
    row = lax.broadcasted_iota(jnp.int32, (TILE, TILE), 0)
    column = lax.broadcasted_iota(jnp.int32, (TILE, TILE), 1)

    def one_head(h, _):
        for kind in range(CLASSES):
            bucket = bucket_index(row - column + (kind - 2) * TILE)
            first, last = (0, BUCKETS // 2) if kind < 2 else (BUCKETS // 2, BUCKETS)
            if kind == 2:
                first = 0
            tile = jnp.zeros((TILE, TILE), f32)
            for b in range(first, last):
                tile = jnp.where(bucket == b, table_ref[b, h], tile)
            out_ref[h, kind] = tile
        return 0

    lax.fori_loop(0, heads, one_head, 0)


def bias_tiles(table):
    heads = table.shape[1]
    return pl.pallas_call(
        tiles_kernel,
        out_shape=jax.ShapeDtypeStruct((heads, CLASSES, TILE, TILE), f32),
        in_specs=[pl.BlockSpec(memory_space=pltpu.SMEM)],
        out_specs=pl.BlockSpec(memory_space=pltpu.VMEM),
        name="bias_tiles",
    )(table)


def fold(tile, reduce):
    return reduce(tile.reshape(TILE // 8, 8, TILE), axis=0)


def tile_class(base, key_slot, query_slot):
    difference = lax.bitwise_xor(base, key_slot) - lax.bitwise_xor(base, query_slot)
    return jnp.clip(difference, -2, 2) + 2


def score_tile(base, h, a, i, q_i, k_ref, seg_keys, seg_i, tiles_ref):
    s = lax.dot_general(
        k_ref[a * TILE : (a + 1) * TILE, h * DH : (h + 1) * DH], q_i, NT, preferred_element_type=f32
    )
    kind = tile_class(base, jnp.int32(a), i)
    s = s + tiles_ref[h, kind]
    return jnp.where(seg_keys[a * TILE : (a + 1) * TILE, :] == seg_i, s, score_masked_rows), kind


def forward_kernel(base_ref, q_ref, k_ref, v_ref, segk_ref, segq_ref, tiles_ref, ctx_ref, log_ref, s_scr, p_scr):
    blocks = q_ref.shape[0] // TILE
    base = base_ref[0]
    for h in range(PAIR):
        v_t = v_ref[:, h * DH : (h + 1) * DH].astype(f32).T.astype(bf16)

        def one_block(i, _, h=h, v_t=v_t):
            start = pl.multiple_of(i * TILE, TILE)
            q_i = q_ref[pl.ds(start, TILE), h * DH : (h + 1) * DH]
            seg_i = segq_ref[pl.ds(i, 1), :]
            top = jnp.full((8, TILE), -jnp.inf, f32)
            for a in range(blocks):
                s, _ = score_tile(base, h, a, i, q_i, k_ref, segk_ref, seg_i, tiles_ref)
                s_scr[a * TILE : (a + 1) * TILE, :] = s
                top = jnp.maximum(top, fold(s, jnp.max))
            top = jnp.max(top, axis=0, keepdims=True)
            total = jnp.zeros((8, TILE), f32)
            for a in range(blocks):
                e = jnp.exp(s_scr[a * TILE : (a + 1) * TILE, :] - top)
                p_scr[a * TILE : (a + 1) * TILE, :] = e.astype(bf16)
                total = total + fold(e, jnp.sum)
            total = jnp.sum(total, axis=0, keepdims=True)
            context = lax.dot_general(
                v_t, p_scr[...], (((1,), (0,)), ((), ())), preferred_element_type=f32
            )
            ctx_ref[h * DH : (h + 1) * DH, pl.ds(start, TILE)] = (context / total).astype(bf16)
            log_ref[0, h, pl.ds(i, 1), :] = top + jnp.log(total)
            return 0

        lax.fori_loop(0, blocks, one_block, 0)


def of_pair(rows, kind):
    return pl.BlockSpec((rows, PAIR * DH), lambda j: (0, 3 * j + kind))


def attend(base, qkv, seg_keys, seg_queries, tiles):
    rows, width = qkv.shape[0], qkv.shape[1] // 3
    pairs, blocks = width // (PAIR * DH), rows // TILE
    return pl.pallas_call(
        forward_kernel,
        grid=(pairs,),
        out_shape=(
            jax.ShapeDtypeStruct((width, rows), bf16),
            jax.ShapeDtypeStruct((pairs, PAIR, blocks, TILE), f32),
        ),
        in_specs=[
            pl.BlockSpec(memory_space=pltpu.SMEM),
            of_pair(rows, 0),
            of_pair(rows, 1),
            of_pair(rows, 2),
            pl.BlockSpec((rows, TILE), lambda j: (0, 0)),
            pl.BlockSpec((blocks, TILE), lambda j: (0, 0)),
            pl.BlockSpec((PAIR, CLASSES, TILE, TILE), lambda j: (j, 0, 0, 0)),
        ],
        out_specs=(
            pl.BlockSpec((PAIR * DH, rows), lambda j: (j, 0)),
            pl.BlockSpec((1, PAIR, blocks, TILE), lambda j: (j, 0, 0, 0)),
        ),
        scratch_shapes=[pltpu.VMEM((rows, TILE), f32), pltpu.VMEM((rows, TILE), bf16)],
        compiler_params=pltpu.CompilerParams(vmem_limit_bytes=VMEM_BYTES),
        name="attend_forward",
    )(base, qkv, qkv, qkv, seg_keys, seg_queries, tiles)


def backward_kernel(
    base_ref, q_ref, k_ref, v_ref, do_ref, log_ref, segk_ref, segq_ref, tiles_ref,
    *rest, kept,
):
    grad_ref, bias_ref, p_scr, dp_scr, p_all, ds_all, near = rest[kept:]
    rows = q_ref.shape[0]
    blocks = rows // TILE
    base = base_ref[0]
    row = lax.broadcasted_iota(jnp.int32, (TILE, TILE), 0)
    column = lax.broadcasted_iota(jnp.int32, (TILE, TILE), 1)
    for h in range(PAIR):
        lanes = slice(h * DH, (h + 1) * DH)
        near[...] = jnp.zeros_like(near)

        def one_block(i, _, h=h, lanes=lanes):
            start = pl.multiple_of(i * TILE, TILE)
            q_i = q_ref[pl.ds(start, TILE), lanes]
            do_i = do_ref[pl.ds(start, TILE), lanes]
            seg_i = segq_ref[pl.ds(i, 1), :]
            log_i = log_ref[0, h, pl.ds(i, 1), :]
            delta = jnp.zeros((8, TILE), f32)
            for a in range(blocks):
                here = slice(a * TILE, (a + 1) * TILE)
                s, _ = score_tile(base, h, a, i, q_i, k_ref, segk_ref, seg_i, tiles_ref)
                p = jnp.exp(s - log_i)
                dp = lax.dot_general(v_ref[here, lanes], do_i, NT, preferred_element_type=f32)
                delta = delta + fold(p * dp, jnp.sum)
                p_scr[here, :] = p
                dp_scr[here, :] = dp
                p_all[here, pl.ds(start, TILE)] = p.astype(bf16)
            delta = jnp.sum(delta, axis=0, keepdims=True)
            for a in range(blocks):
                here = slice(a * TILE, (a + 1) * TILE)
                ds = (p_scr[here, :] * (dp_scr[here, :] - delta)).astype(bf16)
                ds_all[here, pl.ds(start, TILE)] = ds
                kind = tile_class(base, jnp.int32(a), i)
                near[kind] = near[kind] + ds.astype(f32)
            return 0

        lax.fori_loop(0, blocks, one_block, 0)
        q_h, do_h = q_ref[:, lanes], do_ref[:, lanes]
        k_t = k_ref[:, lanes].astype(f32).T.astype(bf16)

        def products(a, _, lanes=lanes, q_h=q_h, do_h=do_h, k_t=k_t, h=h):
            here = pl.ds(pl.multiple_of(a * 2 * TILE, 2 * TILE), 2 * TILE)
            dv = jnp.dot(p_all[here, :], do_h, preferred_element_type=f32)
            dk = jnp.dot(ds_all[here, :], q_h, preferred_element_type=f32)
            dq = jnp.dot(k_t, ds_all[:, here], preferred_element_type=f32).T
            for kind, grad in enumerate((dq, dk, dv)):
                first = kind * PAIR * DH + h * DH
                grad_ref[here, first : first + DH] = grad.astype(bf16)
            return 0

        lax.fori_loop(0, blocks // 2, products, 0)
        for b in range(BUCKETS):
            part = jnp.zeros((8, TILE), f32)
            low = b < BUCKETS // 2
            for kind in (1, 2) if low else (2, 3):
                bucket = bucket_index(row - column + (kind - 2) * TILE)
                part = part + fold(jnp.where(bucket == b, near[kind], 0.0), jnp.sum)
            if b == BUCKETS // 2 - 1:
                part = part + fold(near[0], jnp.sum)
            if b == BUCKETS - 1:
                part = part + fold(near[4], jnp.sum)
            bias_ref[h, b] = part


def attend_back(base, pair, qkv, context_grad, log_total, seg_keys, seg_queries, tiles, earlier=None):
    rows, width = context_grad.shape
    blocks = rows // TILE

    def part(kind):
        return pl.BlockSpec((rows, PAIR * DH), lambda j: (0, 3 * pair + kind))

    specs = [
        pl.BlockSpec(memory_space=pltpu.SMEM),
        part(0),
        part(1),
        part(2),
        pl.BlockSpec((rows, PAIR * DH), lambda j: (0, pair)),
        pl.BlockSpec((1, PAIR, blocks, TILE), lambda j: (pair, 0, 0, 0)),
        pl.BlockSpec((rows, TILE), lambda j: (0, 0)),
        pl.BlockSpec((blocks, TILE), lambda j: (0, 0)),
        pl.BlockSpec((PAIR, CLASSES, TILE, TILE), lambda j: (pair, 0, 0, 0)),
    ]
    operands = [base, qkv, qkv, qkv, context_grad, log_total, seg_keys, seg_queries, tiles]
    aliases = {}
    if earlier is not None:
        specs.append(pl.BlockSpec(memory_space=pl.ANY))
        operands.append(earlier)
        aliases = {len(operands) - 1: 0}
    return pl.pallas_call(
        functools.partial(backward_kernel, kept=len(aliases)),
        grid=(1,),
        out_shape=(
            jax.ShapeDtypeStruct((rows, 3 * width), bf16),
            jax.ShapeDtypeStruct((PAIR, BUCKETS, 8, TILE), f32),
        ),
        in_specs=specs,
        out_specs=(
            pl.BlockSpec((rows, 3 * PAIR * DH), lambda j: (0, pair)),
            pl.BlockSpec((PAIR, BUCKETS, 8, TILE), lambda j: (0, 0, 0, 0)),
        ),
        scratch_shapes=[
            pltpu.VMEM((rows, TILE), f32),
            pltpu.VMEM((rows, TILE), f32),
            pltpu.VMEM((rows, rows), bf16),
            pltpu.VMEM((rows, rows), bf16),
            pltpu.VMEM((CLASSES, TILE, TILE), f32),
        ],
        input_output_aliases=aliases,
        compiler_params=pltpu.CompilerParams(vmem_limit_bytes=VMEM_BYTES),
        name="attend_backward",
    )(*operands)


def per_device(
    inputs,
    doc_lengths,
    gain_attn,
    w_query,
    w_key,
    w_value,
    w_out,
    bias_table,
    gain_ff,
    w_gate,
    w_up,
    w_down,
    cotangent,
):
    rows, width = inputs.shape
    planes, members = lax.axis_size("fsdp"), lax.axis_size("ctx")
    me = lax.axis_index("ctx")
    length = rows * members
    heads = H // members
    hidden = w_gate.shape[1] // members
    model = heads * DH
    striped = H % (planes * members) == 0

    def own_rows(weight):
        count = weight.shape[0] // members
        return lax.dynamic_slice_in_dim(weight, me * count, count, 0)

    def over_planes(weight):
        return lax.all_gather(weight, "fsdp", axis=0, tiled=True)

    def sum_planes(partial):
        return lax.psum_scatter(partial, "fsdp", scatter_dimension=0, tiled=True)

    def trade(summed):
        moved = summed.reshape(members, -1, summed.shape[1])
        return lax.all_to_all(moved, "ctx", 0, 0, tiled=True)

    head_pieces = planes if striped else 1
    of_heads = head_moves(head_pieces, heads)
    of_hidden = block_moves(2, planes, hidden // planes)
    own_qkv = cut_columns(
        [w_query, w_key, w_value], head_pieces, me, members, of_heads, "cut_heads",
        w_out if striped else None,
    )
    if striped:
        gathered = over_planes(own_qkv)
        w_qkv = gathered[:, : 3 * model]
        lanes = gathered.shape[1] - 3 * model
        out_rows = gathered[:, 3 * model :].reshape(planes, width // lanes, -1, lanes)
        out_rows = jnp.transpose(out_rows, (0, 2, 1, 3)).reshape(model, width)
    else:
        w_qkv = over_planes(own_qkv)
        out_rows = lax.dynamic_slice_in_dim(over_planes(w_out), me * model, model, 0)
    w_mix = over_planes(cut_columns([w_gate, w_up], planes, me, members, of_hidden, "cut_hidden"))
    down_rows = over_planes(own_rows(w_down))
    gains = line_gather(after(jnp.stack([gain_attn, gain_ff]), own_qkv)).astype(f32)
    gain_first, gain_second = gains[0], gains[1]

    base = me if by_exchange() else jnp.zeros_like(me)
    slots = jnp.arange(members, dtype=jnp.int32)
    segments = segment_table(doc_lengths[0], length).reshape(members, rows)
    seg_queries = jnp.take(segments, lax.bitwise_xor(base, slots), axis=0)
    seg_queries = seg_queries.reshape(length // TILE, TILE)
    seg_keys = jnp.broadcast_to(seg_queries.reshape(length, 1), (length, TILE))
    base_block = jnp.reshape(base, (1,)).astype(jnp.int32)
    if striped:
        unit = H // (planes * members)
        order = jnp.arange(heads, dtype=jnp.int32)
        own_heads = order // unit * (H // planes) + me * unit + order % unit
    else:
        own_heads = me * heads + jnp.arange(heads, dtype=jnp.int32)
    pick = (jnp.arange(H, dtype=jnp.int32)[:, None] == own_heads[None, :]).astype(f32)
    table = jnp.dot(bias_table.astype(f32), pick, precision=lax.Precision.HIGHEST)
    tiles = bias_tiles(table)

    inputs, cotangent = lax.optimization_barrier((inputs, cotangent, own_qkv))[:2]
    source_all = plane_gather(inputs)
    normed = rms_scale(source_all.astype(f32), gain_first).astype(bf16)
    grad_all = plane_gather(after(cotangent, source_all))
    normed = after(normed, grad_all, tiles)
    qkv = dot(normed, w_qkv).astype(bf16)
    context_t, log_total = attend(base_block, qkv, seg_keys, seg_queries, tiles)
    source = inputs.astype(f32)
    residual = source + plane_scatter(dot(context_t, out_rows, ((0,), (0,))).astype(bf16))

    normed_ff = plane_gather(rms_scale(residual, gain_second).astype(bf16))
    mix = dot(normed_ff, w_mix)
    gate_pre, up_pre = mix[:, :hidden], mix[:, hidden:]
    active_f, mix_back = jax.vjp(gated_mix, gate_pre, up_pre)
    active = active_f.astype(bf16)
    down_grad = dot(active, grad_all, ((0,), (0,))).astype(bf16)
    down_sum = sum_planes(down_grad)
    active_grad = dot(after(grad_all, down_grad), down_rows, ((1,), (1,)))
    gate_grad, up_grad = mix_back(active_grad)
    mix_grad = jnp.concatenate([gate_grad.astype(bf16), up_grad.astype(bf16)], axis=1)
    normed_ff_part = dot(mix_grad, w_mix, ((1,), (1,))).astype(bf16)
    normed_ff_grad = plane_scatter(normed_ff_part)
    mix_grad = after(mix_grad, normed_ff_part)
    mix_weight_grad = dot(normed_ff, mix_grad, ((0,), (0,))).astype(bf16)
    mix_sum = sum_planes(mix_weight_grad)
    norm_back = jax.vjp(lambda v: rms_scale(v, gain_second), residual)[1]
    residual_grad = cotangent.astype(f32) + norm_back(normed_ff_grad)[0]

    residual_low = plane_gather(after(residual_grad.astype(bf16), down_sum, mix_weight_grad))
    output_part = dot(after(active, mix_weight_grad), down_rows).astype(bf16)
    context_grad = dot(after(residual_low, output_part), out_rows, ((1,), (1,))).astype(bf16)
    output_sums = scatter_chips(after(output_part, residual_low))

    def back(pair, grad, earlier=None):
        return attend_back(
            base_block, pair, qkv, grad, log_total, seg_keys, seg_queries, tiles, earlier
        )

    qkv_grad, bias_parts = back(0, context_grad)
    bias_parts = [bias_parts]
    for pair in range(1, heads // PAIR):
        context_grad = after(context_grad, qkv_grad, output_sums)
        qkv_grad, more = back(pair, context_grad, qkv_grad)
        bias_parts.append(more)
    bias_parts = jnp.concatenate(bias_parts, axis=0)
    qkv_weight_grad = dot(normed, qkv_grad, ((0,), (0,))).astype(bf16)
    qkv_sum = sum_planes(qkv_weight_grad)
    normed_part = dot(after(qkv_grad, qkv_weight_grad), w_qkv, ((1,), (1,))).astype(bf16)
    moved_mix = trade(mix_sum)
    normed_sums, moved_mix = lax.optimization_barrier((scatter_chips(normed_part), moved_mix))
    out_weight_grad = dot(context_t, after(residual_low, moved_mix)).astype(bf16)
    bias_own = jnp.sum(after(bias_parts, moved_mix), axis=(2, 3))
    bias_rows = jnp.dot(bias_own.T, pick.T, precision=lax.Precision.HIGHEST)
    bias_rows = jnp.transpose(bias_rows.reshape(planes, members, -1), (1, 0, 2))
    bias_rows = jnp.sum(lax.all_to_all(bias_rows, "ctx", 0, 0, tiled=True), axis=0)
    normed_sums, bias_rows = lax.optimization_barrier((scatter_corner(normed_sums), bias_rows))
    bias_shard = jnp.sum(lax.all_to_all(bias_rows, "fsdp", 0, 0, tiled=True), axis=0)
    gate_shard, up_shard = join_columns(moved_mix, 2, planes, of_hidden, "join_hidden")
    normed_grad, bias_shard, gate_shard, up_shard, output_sums = lax.optimization_barrier(
        (scatter_sides(normed_sums), bias_shard, gate_shard, up_shard, output_sums)
    )
    moved_qkv = trade(after(qkv_sum, normed_grad))
    output = (residual + scatter_sides(scatter_corner(output_sums))).astype(bf16)
    first_back = jax.vjp(lambda v: rms_scale(v, gain_first), source)[1]
    input_grad = (residual_grad + first_back(normed_grad)[0]).astype(bf16)

    def gain_grad(gain, pairs):
        return sum(jnp.sum(own_rows(w).astype(f32) * g, axis=1) for w, g in pairs) / own_rows(
            gain
        ).astype(f32)

    down_shard = down_sum.astype(f32)
    ff_gain_shard = gain_grad(gain_ff, ((w_gate, gate_shard), (w_up, up_shard)))
    query_shard, key_shard, value_shard = join_columns(
        moved_qkv, 3, head_pieces, of_heads, "join_heads"
    )
    attn_gain_shard = gain_grad(
        gain_attn, ((w_query, query_shard), (w_key, key_shard), (w_value, value_shard))
    )
    if striped:
        out_shard = after(sum_planes(out_weight_grad), attn_gain_shard).astype(f32)
    else:
        placed = jnp.zeros((H * DH, width), f32)
        placed = lax.dynamic_update_slice_in_dim(placed, out_weight_grad.astype(f32), me * model, 0)
        out_shard = lax.psum_scatter(placed, ("fsdp", "ctx"), scatter_dimension=0, tiled=True)
    return (
        output,
        input_grad,
        attn_gain_shard,
        ff_gain_shard,
        query_shard,
        key_shard,
        value_shard,
        out_shard,
        bias_shard,
        gate_shard,
        up_shard,
        down_shard,
    )


def solution(mesh):
    rows = P(("fsdp", "ctx"), None)
    vector = P(("fsdp", "ctx"))
    weight = P("fsdp", None)
    return jax.shard_map(
        per_device,
        mesh=mesh,
        in_specs=(
            rows,
            P("fsdp", None),
            P("fsdp"),
            weight,
            weight,
            weight,
            weight,
            P(),
            P("fsdp"),
            weight,
            weight,
            weight,
            rows,
        ),
        out_specs=(rows, rows, vector, vector, rows, rows, rows, rows, vector, rows, rows, rows),
        check_vma=False,
    )
```

```python
import functools

import jax
import jax.numpy as jnp
from jax import lax
from jax.experimental import pallas as pl
from jax.experimental.pallas import tpu as pltpu
from jax.sharding import PartitionSpec as P

H = 32
DH = 64
BUCKETS = 32
TILE = 128
PAIR = 2
CLASSES = 5

epsilon = 1e-06
score_masked_rows = -1000000000.0
bucket_edges = (12, 16, 23, 32, 46, 64, 91)
f32 = jnp.float32
bf16 = jnp.bfloat16
NT = (((1,), (1,)), ((), ()))
VMEM_BYTES = 56 * 1024 * 1024


def bucket_index(offset):
    distance = jnp.abs(offset)
    far_bucket = BUCKETS // 4 + sum(
        ((distance >= boundary).astype(jnp.int32) for boundary in bucket_edges)
    )
    within = jnp.where(distance < BUCKETS // 4, distance, far_bucket)
    return within + BUCKETS // 2 * (offset > 0).astype(jnp.int32)


def rms_scale(values, gain_row):
    mean_square = jnp.mean(values * values, axis=-1, keepdims=True)
    return values * lax.rsqrt(mean_square + epsilon) * gain_row


def gated_mix(gate_part, up_part):
    return jax.nn.gelu(gate_part, approximate=True) * up_part


def segment_table(doc_row, total_rows):
    doc_ends = jnp.cumsum(doc_row)
    positions = jnp.arange(total_rows, dtype=jnp.int32)
    return jnp.sum((positions[:, None] >= doc_ends[None, :]).astype(jnp.int32), axis=1)


def dot(left, right, contract=((1,), (0,))):
    return lax.dot_general(left, right, (contract, ((), ())), preferred_element_type=f32)


def swap(block, mask):
    return lax.ppermute(block, "ctx", [(i, i ^ mask) for i in range(lax.axis_size("ctx"))])


def by_exchange():
    return lax.axis_size("ctx") == 8


def plane_gather(block):
    if not by_exchange():
        return lax.all_gather(block, "ctx", axis=0, tiled=True)
    half = block.shape[0] // 2
    from_x, from_y, from_core = swap(block, 2), swap(block, 4), swap(block, 1)
    diagonal = jnp.concatenate([swap(from_x[:half], 4), swap(from_y[half:], 2)], axis=0)
    x_core, y_core = swap(from_x, 1), swap(from_y, 1)
    return jnp.concatenate(
        [block, from_core, from_x, x_core, from_y, y_core, diagonal, swap(diagonal, 1)], axis=0
    )


def scatter_chips(partial):
    if not by_exchange():
        return partial
    rows = partial.shape[0] // 8

    def chip(m):
        mine, other = partial[m * rows : (m + 1) * rows], partial[(m + 1) * rows : (m + 2) * rows]
        return mine.astype(f32) + swap(other, 1).astype(f32)

    diagonal = chip(6).astype(bf16)
    return [chip(0), chip(2), chip(4), diagonal]


def scatter_corner(sums):
    if not by_exchange():
        return sums
    own, x_sum, y_sum, diagonal = sums
    half = own.shape[0] // 2
    via_x, via_y = swap(diagonal[:half], 2), swap(diagonal[half:], 4)
    y_sum = jnp.concatenate([y_sum[:half] + via_x.astype(f32), y_sum[half:]], axis=0)
    x_sum = jnp.concatenate([x_sum[:half], x_sum[half:] + via_y.astype(f32)], axis=0)
    return [own, x_sum.astype(bf16), y_sum.astype(bf16)]


def scatter_sides(sums):
    if not by_exchange():
        return lax.psum_scatter(sums, "ctx", scatter_dimension=0, tiled=True).astype(f32)
    own, x_sum, y_sum = sums
    return own + swap(x_sum, 2).astype(f32) + swap(y_sum, 4).astype(f32)


def plane_scatter(partial):
    return scatter_sides(scatter_corner(scatter_chips(partial)))


def line_gather(small):
    parts = lax.axis_size("fsdp")
    own = lax.axis_index("fsdp")
    whole = jnp.zeros((parts,) + small.shape, small.dtype)
    for step in range(parts):
        piece = (
            small
            if step == 0
            else lax.ppermute(small, "fsdp", [(i, (i + step) % parts) for i in range(parts)])
        )
        whole = lax.dynamic_update_index_in_dim(whole, piece, (own - step) % parts, 0)
    return jnp.transpose(whole, (1, 0, 2)).reshape(small.shape[0], -1)


def cut_plan(cut, members):
    window = max(-(-((cut * p) % TILE + cut) // TILE) for p in range(members))
    return window, members * cut // TILE - window


def cut_kernel(start_ref, *refs, pieces, window, cut, moves, along):
    out_ref = refs[-1]
    if along:
        rows_ref = refs[-2]
        count, groups = rows_ref.shape[0], rows_ref.shape[1] // along
        for group in range(groups):
            part = rows_ref[:, group * along : (group + 1) * along]
            out_ref[group * count : (group + 1) * count, out_ref.shape[1] - along :] = part
    shift = start_ref[1]
    held = {}
    for source, piece, first, length, target in moves:
        if (source, piece) not in held:
            at = (source * pieces + piece) * window
            span = jnp.concatenate([r[...].astype(f32) for r in refs[at : at + window]], axis=1)
            held[source, piece] = pltpu.roll(span, shift, 1)
        part = held[source, piece][:, first : first + length]
        out_ref[:, target : target + length] = part.astype(bf16)


def cut_columns(weights, pieces, me, members, moves, name, along=None):
    rows, width = weights[0].shape
    cut = width // (pieces * members)
    window, most = cut_plan(cut, members)
    blocks = width // pieces // TILE
    start = jnp.minimum(cut * me // TILE, most)
    shift = (window * TILE - (cut * me - start * TILE)) % (window * TILE)
    step = min(rows, 256)
    specs = []
    for _ in weights:
        for piece in range(pieces):
            for w in range(window):
                place = piece * blocks + w
                specs.append(pl.BlockSpec((step, TILE), lambda r, s, place=place: (r, place + s[0])))
    columns = sum(move[3] for move in moves)
    operands = [w for w in weights for _ in range(pieces * window)]
    extra = 0
    if along is not None:
        count = along.shape[0] // members
        extra = count * along.shape[1] // rows
        columns += extra
        specs.append(pl.BlockSpec((count, step // count * extra), lambda r, s: (s[2], r)))
        operands.append(along)
    return pl.pallas_call(
        functools.partial(
            cut_kernel, pieces=pieces, window=window, cut=cut, moves=moves, along=extra
        ),
        grid_spec=pltpu.PrefetchScalarGridSpec(
            num_scalar_prefetch=1,
            grid=(rows // step,),
            in_specs=specs,
            out_specs=pl.BlockSpec((step, columns), lambda r, s: (r, 0)),
        ),
        out_shape=jax.ShapeDtypeStruct((rows, columns), bf16),
        name=name,
    )(jnp.stack([start, shift, me]).astype(jnp.int32), *operands)


def join_kernel(in_ref, *out_refs, pieces, cut, moves):
    members = in_ref.shape[0]
    for kind, piece, first, length, source in moves:
        for p in range(members):
            target = (piece * members + p) * cut + first
            out_refs[kind][:, target : target + length] = in_ref[p, :, source : source + length].astype(f32)


def join_columns(moved, kinds, pieces, moves, name):
    members, rows, columns = moved.shape
    cut = columns // (kinds * pieces)
    step = min(rows, 32)
    width = members * pieces * cut
    return pl.pallas_call(
        functools.partial(join_kernel, pieces=pieces, cut=cut, moves=moves),
        grid=(rows // step,),
        out_shape=[jax.ShapeDtypeStruct((rows, width), f32)] * kinds,
        in_specs=[pl.BlockSpec((members, step, columns), lambda r: (0, r, 0))],
        out_specs=[pl.BlockSpec((step, width), lambda r: (r, 0))] * kinds,
        name=name,
    )(moved)


def head_moves(pieces, heads):
    each = heads // pieces
    return [
        (kind, t // each, t % each * DH, DH, (t // PAIR * 3 + kind) * PAIR * DH + t % PAIR * DH)
        for t in range(heads)
        for kind in range(3)
    ]


def block_moves(kinds, pieces, cut):
    return [
        (kind, piece, 0, cut, (kind * pieces + piece) * cut)
        for kind in range(kinds)
        for piece in range(pieces)
    ]


def after_all(values, *others):
    return lax.optimization_barrier((values,) + others)[0]


def after(value, *others):
    return lax.optimization_barrier((value,) + others)[0]


def tiles_kernel(table_ref, out_ref):
    heads = out_ref.shape[0]
    row = lax.broadcasted_iota(jnp.int32, (TILE, TILE), 0)
    column = lax.broadcasted_iota(jnp.int32, (TILE, TILE), 1)

    def one_head(h, _):
        for kind in range(CLASSES):
            bucket = bucket_index(row - column + (kind - 2) * TILE)
            first, last = (0, BUCKETS // 2) if kind < 2 else (BUCKETS // 2, BUCKETS)
            if kind == 2:
                first = 0
            tile = jnp.zeros((TILE, TILE), f32)
            for b in range(first, last):
                tile = jnp.where(bucket == b, table_ref[b, h], tile)
            out_ref[h, kind] = tile
        return 0

    lax.fori_loop(0, heads, one_head, 0)


def bias_tiles(table):
    heads = table.shape[1]
    return pl.pallas_call(
        tiles_kernel,
        out_shape=jax.ShapeDtypeStruct((heads, CLASSES, TILE, TILE), f32),
        in_specs=[pl.BlockSpec(memory_space=pltpu.SMEM)],
        out_specs=pl.BlockSpec(memory_space=pltpu.VMEM),
        name="bias_tiles",
    )(table)


def fold(tile, reduce):
    return reduce(tile.reshape(TILE // 8, 8, TILE), axis=0)


def tile_class(base, key_slot, query_slot):
    difference = lax.bitwise_xor(base, key_slot) - lax.bitwise_xor(base, query_slot)
    return jnp.clip(difference, -2, 2) + 2


def score_tile(base, h, a, i, q_i, k_ref, seg_keys, seg_i, tiles_ref):
    s = lax.dot_general(
        k_ref[a * TILE : (a + 1) * TILE, h * DH : (h + 1) * DH], q_i, NT, preferred_element_type=f32
    )
    kind = tile_class(base, jnp.int32(a), i)
    s = s + tiles_ref[h, kind]
    return jnp.where(seg_keys[a * TILE : (a + 1) * TILE, :] == seg_i, s, score_masked_rows), kind


def forward_kernel(base_ref, q_ref, k_ref, v_ref, segk_ref, segq_ref, tiles_ref, ctx_ref, log_ref, s_scr, p_scr):
    blocks = q_ref.shape[0] // TILE
    base = base_ref[0]
    for h in range(PAIR):
        v_t = v_ref[:, h * DH : (h + 1) * DH].astype(f32).T.astype(bf16)

        def one_block(i, _, h=h, v_t=v_t):
            start = pl.multiple_of(i * TILE, TILE)
            q_i = q_ref[pl.ds(start, TILE), h * DH : (h + 1) * DH]
            seg_i = segq_ref[pl.ds(i, 1), :]
            top = jnp.full((8, TILE), -jnp.inf, f32)
            for a in range(blocks):
                s, _ = score_tile(base, h, a, i, q_i, k_ref, segk_ref, seg_i, tiles_ref)
                s_scr[a * TILE : (a + 1) * TILE, :] = s
                top = jnp.maximum(top, fold(s, jnp.max))
            top = jnp.max(top, axis=0, keepdims=True)
            total = jnp.zeros((8, TILE), f32)
            for a in range(blocks):
                e = jnp.exp(s_scr[a * TILE : (a + 1) * TILE, :] - top)
                p_scr[a * TILE : (a + 1) * TILE, :] = e.astype(bf16)
                total = total + fold(e, jnp.sum)
            total = jnp.sum(total, axis=0, keepdims=True)
            context = lax.dot_general(
                v_t, p_scr[...], (((1,), (0,)), ((), ())), preferred_element_type=f32
            )
            ctx_ref[h * DH : (h + 1) * DH, pl.ds(start, TILE)] = (context / total).astype(bf16)
            log_ref[0, h, pl.ds(i, 1), :] = top + jnp.log(total)
            return 0

        lax.fori_loop(0, blocks, one_block, 0)


def of_pair(rows, kind):
    return pl.BlockSpec((rows, PAIR * DH), lambda j: (0, 3 * j + kind))


def attend(base, qkv, seg_keys, seg_queries, tiles):
    rows, width = qkv.shape[0], qkv.shape[1] // 3
    pairs, blocks = width // (PAIR * DH), rows // TILE
    return pl.pallas_call(
        forward_kernel,
        grid=(pairs,),
        out_shape=(
            jax.ShapeDtypeStruct((width, rows), bf16),
            jax.ShapeDtypeStruct((pairs, PAIR, blocks, TILE), f32),
        ),
        in_specs=[
            pl.BlockSpec(memory_space=pltpu.SMEM),
            of_pair(rows, 0),
            of_pair(rows, 1),
            of_pair(rows, 2),
            pl.BlockSpec((rows, TILE), lambda j: (0, 0)),
            pl.BlockSpec((blocks, TILE), lambda j: (0, 0)),
            pl.BlockSpec((PAIR, CLASSES, TILE, TILE), lambda j: (j, 0, 0, 0)),
        ],
        out_specs=(
            pl.BlockSpec((PAIR * DH, rows), lambda j: (j, 0)),
            pl.BlockSpec((1, PAIR, blocks, TILE), lambda j: (j, 0, 0, 0)),
        ),
        scratch_shapes=[pltpu.VMEM((rows, TILE), f32), pltpu.VMEM((rows, TILE), bf16)],
        compiler_params=pltpu.CompilerParams(vmem_limit_bytes=VMEM_BYTES),
        name="attend_forward",
    )(base, qkv, qkv, qkv, seg_keys, seg_queries, tiles)


def backward_kernel(
    base_ref, q_ref, k_ref, v_ref, do_ref, log_ref, segk_ref, segq_ref, tiles_ref,
    *rest, kept,
):
    grad_ref, bias_ref, p_scr, dp_scr, p_all, ds_all, near = rest[kept:]
    rows = q_ref.shape[0]
    blocks = rows // TILE
    base = base_ref[0]
    row = lax.broadcasted_iota(jnp.int32, (TILE, TILE), 0)
    column = lax.broadcasted_iota(jnp.int32, (TILE, TILE), 1)
    for h in range(PAIR):
        lanes = slice(h * DH, (h + 1) * DH)
        near[...] = jnp.zeros_like(near)

        def one_block(i, _, h=h, lanes=lanes):
            start = pl.multiple_of(i * TILE, TILE)
            q_i = q_ref[pl.ds(start, TILE), lanes]
            do_i = do_ref[pl.ds(start, TILE), lanes]
            seg_i = segq_ref[pl.ds(i, 1), :]
            log_i = log_ref[0, h, pl.ds(i, 1), :]
            delta = jnp.zeros((8, TILE), f32)
            for a in range(blocks):
                here = slice(a * TILE, (a + 1) * TILE)
                s, _ = score_tile(base, h, a, i, q_i, k_ref, segk_ref, seg_i, tiles_ref)
                p = jnp.exp(s - log_i)
                dp = lax.dot_general(v_ref[here, lanes], do_i, NT, preferred_element_type=f32)
                delta = delta + fold(p * dp, jnp.sum)
                p_scr[here, :] = p
                dp_scr[here, :] = dp
                p_all[here, pl.ds(start, TILE)] = p.astype(bf16)
            delta = jnp.sum(delta, axis=0, keepdims=True)
            for a in range(blocks):
                here = slice(a * TILE, (a + 1) * TILE)
                ds = (p_scr[here, :] * (dp_scr[here, :] - delta)).astype(bf16)
                ds_all[here, pl.ds(start, TILE)] = ds
                kind = tile_class(base, jnp.int32(a), i)
                near[kind] = near[kind] + ds.astype(f32)
            return 0

        lax.fori_loop(0, blocks, one_block, 0)
        q_h, do_h = q_ref[:, lanes], do_ref[:, lanes]
        k_t = k_ref[:, lanes].astype(f32).T.astype(bf16)

        def products(a, _, lanes=lanes, q_h=q_h, do_h=do_h, k_t=k_t, h=h):
            here = pl.ds(pl.multiple_of(a * 2 * TILE, 2 * TILE), 2 * TILE)
            dv = jnp.dot(p_all[here, :], do_h, preferred_element_type=f32)
            dk = jnp.dot(ds_all[here, :], q_h, preferred_element_type=f32)
            dq = jnp.dot(k_t, ds_all[:, here], preferred_element_type=f32).T
            for kind, grad in enumerate((dq, dk, dv)):
                first = kind * PAIR * DH + h * DH
                grad_ref[here, first : first + DH] = grad.astype(bf16)
            return 0

        lax.fori_loop(0, blocks // 2, products, 0)
        for b in range(BUCKETS):
            part = jnp.zeros((8, TILE), f32)
            low = b < BUCKETS // 2
            for kind in (1, 2) if low else (2, 3):
                bucket = bucket_index(row - column + (kind - 2) * TILE)
                part = part + fold(jnp.where(bucket == b, near[kind], 0.0), jnp.sum)
            if b == BUCKETS // 2 - 1:
                part = part + fold(near[0], jnp.sum)
            if b == BUCKETS - 1:
                part = part + fold(near[4], jnp.sum)
            bias_ref[h, b] = part


def attend_back(base, pair, qkv, context_grad, log_total, seg_keys, seg_queries, tiles, earlier=None):
    rows, width = context_grad.shape
    blocks = rows // TILE

    def part(kind):
        return pl.BlockSpec((rows, PAIR * DH), lambda j: (0, 3 * pair + kind))

    specs = [
        pl.BlockSpec(memory_space=pltpu.SMEM),
        part(0),
        part(1),
        part(2),
        pl.BlockSpec((rows, PAIR * DH), lambda j: (0, pair)),
        pl.BlockSpec((1, PAIR, blocks, TILE), lambda j: (pair, 0, 0, 0)),
        pl.BlockSpec((rows, TILE), lambda j: (0, 0)),
        pl.BlockSpec((blocks, TILE), lambda j: (0, 0)),
        pl.BlockSpec((PAIR, CLASSES, TILE, TILE), lambda j: (pair, 0, 0, 0)),
    ]
    operands = [base, qkv, qkv, qkv, context_grad, log_total, seg_keys, seg_queries, tiles]
    aliases = {}
    if earlier is not None:
        specs.append(pl.BlockSpec(memory_space=pl.ANY))
        operands.append(earlier)
        aliases = {len(operands) - 1: 0}
    return pl.pallas_call(
        functools.partial(backward_kernel, kept=len(aliases)),
        grid=(1,),
        out_shape=(
            jax.ShapeDtypeStruct((rows, 3 * width), bf16),
            jax.ShapeDtypeStruct((PAIR, BUCKETS, 8, TILE), f32),
        ),
        in_specs=specs,
        out_specs=(
            pl.BlockSpec((rows, 3 * PAIR * DH), lambda j: (0, pair)),
            pl.BlockSpec((PAIR, BUCKETS, 8, TILE), lambda j: (0, 0, 0, 0)),
        ),
        scratch_shapes=[
            pltpu.VMEM((rows, TILE), f32),
            pltpu.VMEM((rows, TILE), f32),
            pltpu.VMEM((rows, rows), bf16),
            pltpu.VMEM((rows, rows), bf16),
            pltpu.VMEM((CLASSES, TILE, TILE), f32),
        ],
        input_output_aliases=aliases,
        compiler_params=pltpu.CompilerParams(vmem_limit_bytes=VMEM_BYTES),
        name="attend_backward",
    )(*operands)


def per_device(
    inputs,
    doc_lengths,
    gain_attn,
    w_query,
    w_key,
    w_value,
    w_out,
    bias_table,
    gain_ff,
    w_gate,
    w_up,
    w_down,
    cotangent,
):
    rows, width = inputs.shape
    planes, members = lax.axis_size("fsdp"), lax.axis_size("ctx")
    me = lax.axis_index("ctx")
    length = rows * members
    heads = H // members
    hidden = w_gate.shape[1] // members
    model = heads * DH
    striped = H == planes * members == BUCKETS

    def own_rows(weight):
        count = weight.shape[0] // members
        return lax.dynamic_slice_in_dim(weight, me * count, count, 0)

    def over_planes(weight):
        return lax.all_gather(weight, "fsdp", axis=0, tiled=True)

    def sum_planes(partial):
        return lax.psum_scatter(partial, "fsdp", scatter_dimension=0, tiled=True)

    def trade(summed):
        moved = summed.reshape(members, -1, summed.shape[1])
        return lax.all_to_all(moved, "ctx", 0, 0, tiled=True)

    head_pieces = planes if striped else 1
    of_heads = head_moves(head_pieces, heads)
    of_hidden = block_moves(2, planes, hidden // planes)
    own_qkv = cut_columns(
        [w_query, w_key, w_value], head_pieces, me, members, of_heads, "cut_heads",
        w_out if striped else None,
    )
    if striped:
        gathered = over_planes(own_qkv)
        w_qkv = gathered[:, : 3 * model]
        lanes = gathered.shape[1] - 3 * model
        out_rows = gathered[:, 3 * model :].reshape(planes, width // lanes, -1, lanes)
        out_rows = jnp.transpose(out_rows, (0, 2, 1, 3)).reshape(model, width)
    else:
        w_qkv = over_planes(own_qkv)
        out_rows = lax.dynamic_slice_in_dim(over_planes(w_out), me * model, model, 0)
    w_mix = over_planes(cut_columns([w_gate, w_up], planes, me, members, of_hidden, "cut_hidden"))
    down_rows = over_planes(own_rows(w_down))
    gains = line_gather(after(jnp.stack([gain_attn, gain_ff]), own_qkv)).astype(f32)
    gain_first, gain_second = gains[0], gains[1]

    base = me if by_exchange() else jnp.zeros_like(me)
    slots = jnp.arange(members, dtype=jnp.int32)
    segments = segment_table(doc_lengths[0], length).reshape(members, rows)
    seg_queries = jnp.take(segments, lax.bitwise_xor(base, slots), axis=0)
    seg_queries = seg_queries.reshape(length // TILE, TILE)
    seg_keys = jnp.broadcast_to(seg_queries.reshape(length, 1), (length, TILE))
    base_block = jnp.reshape(base, (1,)).astype(jnp.int32)
    if striped:
        unit = H // (planes * members)
        order = jnp.arange(heads, dtype=jnp.int32)
        own_heads = order // unit * (H // planes) + me * unit + order % unit
    else:
        own_heads = me * heads + jnp.arange(heads, dtype=jnp.int32)
    pick = (jnp.arange(H, dtype=jnp.int32)[:, None] == own_heads[None, :]).astype(f32)
    table = jnp.dot(bias_table.astype(f32), pick, precision=lax.Precision.HIGHEST)
    tiles = bias_tiles(table)

    inputs, cotangent = lax.optimization_barrier((inputs, cotangent, own_qkv))[:2]
    source_all = plane_gather(inputs)
    normed = rms_scale(source_all.astype(f32), gain_first).astype(bf16)
    grad_all = plane_gather(after(cotangent, source_all))
    normed = after(normed, grad_all, tiles)
    qkv = dot(normed, w_qkv).astype(bf16)
    context_t, log_total = attend(base_block, qkv, seg_keys, seg_queries, tiles)
    source = inputs.astype(f32)
    residual = source + plane_scatter(dot(context_t, out_rows, ((0,), (0,))).astype(bf16))

    normed_ff = plane_gather(rms_scale(residual, gain_second).astype(bf16))
    mix = dot(normed_ff, w_mix)
    gate_pre, up_pre = mix[:, :hidden], mix[:, hidden:]
    active_f, mix_back = jax.vjp(gated_mix, gate_pre, up_pre)
    active = active_f.astype(bf16)
    down_grad = dot(active, grad_all, ((0,), (0,))).astype(bf16)
    down_sum = sum_planes(down_grad)
    active_grad = dot(after(grad_all, down_grad), down_rows, ((1,), (1,)))
    gate_grad, up_grad = mix_back(active_grad)
    mix_grad = jnp.concatenate([gate_grad.astype(bf16), up_grad.astype(bf16)], axis=1)
    normed_ff_part = dot(mix_grad, w_mix, ((1,), (1,))).astype(bf16)
    normed_ff_grad = plane_scatter(normed_ff_part)
    mix_grad = after(mix_grad, normed_ff_part)
    mix_weight_grad = dot(normed_ff, mix_grad, ((0,), (0,))).astype(bf16)
    mix_sum = sum_planes(mix_weight_grad)
    norm_back = jax.vjp(lambda v: rms_scale(v, gain_second), residual)[1]
    residual_grad = cotangent.astype(f32) + norm_back(normed_ff_grad)[0]

    residual_low = plane_gather(after(residual_grad.astype(bf16), down_sum, mix_weight_grad))
    output_part = dot(after(active, mix_weight_grad), down_rows).astype(bf16)
    context_grad = dot(after(residual_low, output_part), out_rows, ((1,), (1,))).astype(bf16)
    output_sums = scatter_chips(after(output_part, residual_low))

    def back(pair, grad, earlier=None):
        return attend_back(
            base_block, pair, qkv, grad, log_total, seg_keys, seg_queries, tiles, earlier
        )

    qkv_grad, bias_parts = back(0, context_grad)
    bias_parts = [bias_parts]
    for pair in range(1, heads // PAIR):
        context_grad = after(context_grad, qkv_grad, output_sums)
        qkv_grad, more = back(pair, context_grad, qkv_grad)
        bias_parts.append(more)
    bias_parts = jnp.concatenate(bias_parts, axis=0)
    qkv_weight_grad = dot(normed, qkv_grad, ((0,), (0,))).astype(bf16)
    bias_own = jnp.sum(bias_parts, axis=(2, 3))
    qkv_sent = qkv_weight_grad
    if striped:
        bias_own = bias_own.T.astype(bf16).reshape(planes, members, heads)
        bias_own = jnp.pad(bias_own, ((0, 0), (0, 0), (0, 3 * model - heads)))
        qkv_sent = qkv_sent.reshape(planes, -1, 3 * model)
        qkv_sent = jnp.concatenate([qkv_sent, bias_own], axis=1).reshape(-1, 3 * model)
    qkv_sum = sum_planes(qkv_sent)
    normed_part = dot(after(qkv_grad, qkv_weight_grad), w_qkv, ((1,), (1,))).astype(bf16)
    normed_sums, mix_sum, output_sums = lax.optimization_barrier(
        (scatter_corner(scatter_chips(normed_part)), mix_sum, scatter_corner(output_sums))
    )
    out_weight_grad = dot(context_t, after_all((residual_low,), normed_sums)[0]).astype(bf16)
    moved_mix = trade(mix_sum)
    normed_grad, moved_mix, output_sum = lax.optimization_barrier(
        (scatter_sides(normed_sums), moved_mix, scatter_sides(output_sums))
    )
    output = (residual + output_sum).astype(bf16)
    gate_shard, up_shard = join_columns(moved_mix, 2, planes, of_hidden, "join_hidden")
    qkv_sum = after(qkv_sum, normed_grad)
    if striped:
        own = width // planes
        moved_qkv = [qkv_sum[:own].reshape(members, -1, 3 * model), qkv_sum[own:][:, None]]
        moved_qkv = jnp.concatenate(moved_qkv, axis=1)
        moved_qkv = lax.all_to_all(moved_qkv, "ctx", 0, 0, tiled=True)
        bias_shard = moved_qkv[:, -1, :heads].astype(f32).T.reshape(-1)
        moved_qkv = moved_qkv[:, :-1]
    else:
        moved_qkv = trade(qkv_sum)
        bias_rows = jnp.dot(bias_own.T, pick.T, precision=lax.Precision.HIGHEST).reshape(-1)
        bias_shard = lax.psum_scatter(bias_rows, ("fsdp", "ctx"), scatter_dimension=0, tiled=True)
    first_back = jax.vjp(lambda v: rms_scale(v, gain_first), source)[1]
    input_grad = (residual_grad + first_back(normed_grad)[0]).astype(bf16)

    def gain_grad(gain, pairs):
        return sum(jnp.sum(own_rows(w).astype(f32) * g, axis=1) for w, g in pairs) / own_rows(
            gain
        ).astype(f32)

    down_shard = down_sum.astype(f32)
    ff_gain_shard = gain_grad(gain_ff, ((w_gate, gate_shard), (w_up, up_shard)))
    query_shard, key_shard, value_shard = join_columns(
        moved_qkv, 3, head_pieces, of_heads, "join_heads"
    )
    attn_gain_shard = gain_grad(
        gain_attn, ((w_query, query_shard), (w_key, key_shard), (w_value, value_shard))
    )
    if striped:
        out_shard = after(sum_planes(out_weight_grad), attn_gain_shard).astype(f32)
    else:
        placed = jnp.zeros((H * DH, width), f32)
        placed = lax.dynamic_update_slice_in_dim(placed, out_weight_grad.astype(f32), me * model, 0)
        out_shard = lax.psum_scatter(placed, ("fsdp", "ctx"), scatter_dimension=0, tiled=True)
    return (
        output,
        input_grad,
        attn_gain_shard,
        ff_gain_shard,
        query_shard,
        key_shard,
        value_shard,
        out_shard,
        bias_shard,
        gate_shard,
        up_shard,
        down_shard,
    )


def solution(mesh):
    rows = P(("fsdp", "ctx"), None)
    vector = P(("fsdp", "ctx"))
    weight = P("fsdp", None)
    return jax.shard_map(
        per_device,
        mesh=mesh,
        in_specs=(
            rows,
            P("fsdp", None),
            P("fsdp"),
            weight,
            weight,
            weight,
            weight,
            P(),
            P("fsdp"),
            weight,
            weight,
            weight,
            rows,
        ),
        out_specs=(rows, rows, vector, vector, rows, rows, rows, rows, vector, rows, rows, rows),
        check_vma=False,
    )
```

```python
import functools

import jax
import jax.numpy as jnp
from jax import lax
from jax.experimental import pallas as pl
from jax.experimental.pallas import tpu as pltpu
from jax.sharding import PartitionSpec as P

H = 32
DH = 64
BUCKETS = 32
TILE = 128
PAIR = 2
CLASSES = 5

epsilon = 1e-06
score_masked_rows = -1000000000.0
bucket_edges = (12, 16, 23, 32, 46, 64, 91)
f32 = jnp.float32
bf16 = jnp.bfloat16
NT = (((1,), (1,)), ((), ()))
VMEM_BYTES = 56 * 1024 * 1024


def bucket_index(offset):
    distance = jnp.abs(offset)
    far_bucket = BUCKETS // 4 + sum(
        ((distance >= boundary).astype(jnp.int32) for boundary in bucket_edges)
    )
    within = jnp.where(distance < BUCKETS // 4, distance, far_bucket)
    return within + BUCKETS // 2 * (offset > 0).astype(jnp.int32)


def rms_scale(values, gain_row):
    mean_square = jnp.mean(values * values, axis=-1, keepdims=True)
    return values * lax.rsqrt(mean_square + epsilon) * gain_row


def gated_mix(gate_part, up_part):
    return jax.nn.gelu(gate_part, approximate=True) * up_part


def segment_table(doc_row, total_rows):
    doc_ends = jnp.cumsum(doc_row)
    positions = jnp.arange(total_rows, dtype=jnp.int32)
    return jnp.sum((positions[:, None] >= doc_ends[None, :]).astype(jnp.int32), axis=1)


def dot(left, right, contract=((1,), (0,))):
    return lax.dot_general(left, right, (contract, ((), ())), preferred_element_type=f32)


def swap(block, mask):
    return lax.ppermute(block, "ctx", [(i, i ^ mask) for i in range(lax.axis_size("ctx"))])


def by_exchange():
    return lax.axis_size("ctx") == 8


def plane_gather(block):
    if not by_exchange():
        return lax.all_gather(block, "ctx", axis=0, tiled=True)
    half = block.shape[0] // 2
    from_x, from_y, from_core = swap(block, 2), swap(block, 4), swap(block, 1)
    diagonal = jnp.concatenate([swap(from_x[:half], 4), swap(from_y[half:], 2)], axis=0)
    x_core, y_core = swap(from_x, 1), swap(from_y, 1)
    return jnp.concatenate(
        [block, from_core, from_x, x_core, from_y, y_core, diagonal, swap(diagonal, 1)], axis=0
    )


def scatter_chips(partial):
    if not by_exchange():
        return partial
    rows = partial.shape[0] // 8

    def chip(m):
        mine, other = partial[m * rows : (m + 1) * rows], partial[(m + 1) * rows : (m + 2) * rows]
        return mine.astype(f32) + swap(other, 1).astype(f32)

    diagonal = chip(6).astype(bf16)
    return [chip(0), chip(2), chip(4), diagonal]


def scatter_corner(sums):
    if not by_exchange():
        return sums
    own, x_sum, y_sum, diagonal = sums
    half = own.shape[0] // 2
    via_x, via_y = swap(diagonal[:half], 2), swap(diagonal[half:], 4)
    y_sum = jnp.concatenate([y_sum[:half] + via_x.astype(f32), y_sum[half:]], axis=0)
    x_sum = jnp.concatenate([x_sum[:half], x_sum[half:] + via_y.astype(f32)], axis=0)
    return [own, x_sum.astype(bf16), y_sum.astype(bf16)]


def scatter_sides(sums):
    if not by_exchange():
        return lax.psum_scatter(sums, "ctx", scatter_dimension=0, tiled=True).astype(f32)
    own, x_sum, y_sum = sums
    return own + swap(x_sum, 2).astype(f32) + swap(y_sum, 4).astype(f32)


def plane_scatter(partial):
    return scatter_sides(scatter_corner(scatter_chips(partial)))


def line_gather(small):
    parts = lax.axis_size("fsdp")
    own = lax.axis_index("fsdp")
    whole = jnp.zeros((parts,) + small.shape, small.dtype)
    for step in range(parts):
        piece = (
            small
            if step == 0
            else lax.ppermute(small, "fsdp", [(i, (i + step) % parts) for i in range(parts)])
        )
        whole = lax.dynamic_update_index_in_dim(whole, piece, (own - step) % parts, 0)
    return jnp.transpose(whole, (1, 0, 2)).reshape(small.shape[0], -1)


def cut_plan(cut, members):
    window = max(-(-((cut * p) % TILE + cut) // TILE) for p in range(members))
    return window, members * cut // TILE - window


def cut_kernel(start_ref, *refs, pieces, window, cut, moves, along):
    out_ref = refs[-1]
    if along:
        rows_ref = refs[-2]
        count, groups = rows_ref.shape[0], rows_ref.shape[1] // along
        for group in range(groups):
            part = rows_ref[:, group * along : (group + 1) * along]
            out_ref[group * count : (group + 1) * count, out_ref.shape[1] - along :] = part
    shift = start_ref[1]
    held = {}
    for source, piece, first, length, target in moves:
        if (source, piece) not in held:
            at = (source * pieces + piece) * window
            span = jnp.concatenate([r[...].astype(f32) for r in refs[at : at + window]], axis=1)
            held[source, piece] = pltpu.roll(span, shift, 1)
        part = held[source, piece][:, first : first + length]
        out_ref[:, target : target + length] = part.astype(bf16)


def cut_columns(weights, pieces, me, members, moves, name, along=None):
    rows, width = weights[0].shape
    cut = width // (pieces * members)
    window, most = cut_plan(cut, members)
    blocks = width // pieces // TILE
    start = jnp.minimum(cut * me // TILE, most)
    shift = (window * TILE - (cut * me - start * TILE)) % (window * TILE)
    step = min(rows, 256)
    specs = []
    for _ in weights:
        for piece in range(pieces):
            for w in range(window):
                place = piece * blocks + w
                specs.append(pl.BlockSpec((step, TILE), lambda r, s, place=place: (r, place + s[0])))
    columns = sum(move[3] for move in moves)
    operands = [w for w in weights for _ in range(pieces * window)]
    extra = 0
    if along is not None:
        count = along.shape[0] // members
        extra = count * along.shape[1] // rows
        columns += extra
        specs.append(pl.BlockSpec((count, step // count * extra), lambda r, s: (s[2], r)))
        operands.append(along)
    return pl.pallas_call(
        functools.partial(
            cut_kernel, pieces=pieces, window=window, cut=cut, moves=moves, along=extra
        ),
        grid_spec=pltpu.PrefetchScalarGridSpec(
            num_scalar_prefetch=1,
            grid=(rows // step,),
            in_specs=specs,
            out_specs=pl.BlockSpec((step, columns), lambda r, s: (r, 0)),
        ),
        out_shape=jax.ShapeDtypeStruct((rows, columns), bf16),
        name=name,
    )(jnp.stack([start, shift, me]).astype(jnp.int32), *operands)


def cut_heads_kernel(q_ref, k_ref, v_ref, rows_ref, out_ref, held, held_rows, sems, *, pieces, members):
    me = lax.axis_index("ctx")
    tiles = members * DH // TILE
    weights = (q_ref, k_ref, v_ref)
    count = held_rows.shape[0]
    copies = []
    for source, weight in enumerate(weights):
        for piece in range(pieces):
            first = pl.multiple_of((piece * tiles + me * DH // TILE) * TILE, TILE)
            at = source * pieces + piece
            copies.append(
                pltpu.make_async_copy(weight.at[:, pl.ds(first, TILE)], held.at[at], sems.at[at])
            )
    first = pl.multiple_of(me * count, count)
    copies.append(
        pltpu.make_async_copy(
            rows_ref.at[pl.ds(first, count), :], held_rows, sems.at[len(weights) * pieces]
        )
    )
    for copy in copies:
        copy.start()
    row = lax.broadcasted_iota(jnp.int32, (TILE, TILE), 0)
    column = lax.broadcasted_iota(jnp.int32, (TILE, TILE), 1)
    same = row - lax.rem(me * DH, TILE) == lax.rem(column, DH)
    pick = [(same & (column // DH == side)).astype(bf16) for side in range(2)]
    for source in range(len(weights)):
        for pair in range(pieces // 2):
            at = source * pieces + 2 * pair
            copies[at].wait()
            copies[at + 1].wait()
            both = jnp.dot(held[at], pick[0], preferred_element_type=f32)
            both = both + jnp.dot(held[at + 1], pick[1], preferred_element_type=f32)
            target = (pair * 3 + source) * TILE
            out_ref[:, target : target + TILE] = both.astype(bf16)
    copies[-1].wait()
    along = out_ref.shape[1] - len(weights) * pieces * DH
    for group in range(held_rows.shape[1] // along):
        part = held_rows[:, group * along : (group + 1) * along]
        out_ref[group * count : (group + 1) * count, out_ref.shape[1] - along :] = part


def cut_heads_at_once(w_query, w_key, w_value, w_out, pieces, members):
    rows, width = w_query.shape
    count = w_out.shape[0] // members
    columns = 3 * pieces * DH + count * width // rows
    return pl.pallas_call(
        functools.partial(cut_heads_kernel, pieces=pieces, members=members),
        out_shape=jax.ShapeDtypeStruct((rows, columns), bf16),
        in_specs=[pl.BlockSpec(memory_space=pl.ANY)] * 4,
        out_specs=pl.BlockSpec(memory_space=pltpu.VMEM),
        scratch_shapes=[
            pltpu.VMEM((3 * pieces, rows, TILE), bf16),
            pltpu.VMEM((count, width), bf16),
            pltpu.SemaphoreType.DMA((3 * pieces + 1,)),
        ],
        compiler_params=pltpu.CompilerParams(vmem_limit_bytes=VMEM_BYTES),
        name="cut_heads",
    )(w_query, w_key, w_value, w_out)


def join_kernel(in_ref, *out_refs, pieces, cut, moves):
    members = in_ref.shape[0]
    for kind, piece, first, length, source in moves:
        for p in range(members):
            target = (piece * members + p) * cut + first
            out_refs[kind][:, target : target + length] = in_ref[p, :, source : source + length].astype(f32)


def join_columns(moved, kinds, pieces, moves, name):
    members, rows, columns = moved.shape
    cut = columns // (kinds * pieces)
    step = min(rows, 32)
    width = members * pieces * cut
    return pl.pallas_call(
        functools.partial(join_kernel, pieces=pieces, cut=cut, moves=moves),
        grid=(rows // step,),
        out_shape=[jax.ShapeDtypeStruct((rows, width), f32)] * kinds,
        in_specs=[pl.BlockSpec((members, step, columns), lambda r: (0, r, 0))],
        out_specs=[pl.BlockSpec((step, width), lambda r: (r, 0))] * kinds,
        name=name,
    )(moved)


def head_moves(pieces, heads):
    each = heads // pieces
    return [
        (kind, t // each, t % each * DH, DH, (t // PAIR * 3 + kind) * PAIR * DH + t % PAIR * DH)
        for t in range(heads)
        for kind in range(3)
    ]


def block_moves(kinds, pieces, cut):
    return [
        (kind, piece, 0, cut, (kind * pieces + piece) * cut)
        for kind in range(kinds)
        for piece in range(pieces)
    ]


def after_all(values, *others):
    return lax.optimization_barrier((values,) + others)[0]


def after(value, *others):
    return lax.optimization_barrier((value,) + others)[0]


def tiles_kernel(table_ref, out_ref):
    heads = out_ref.shape[0]
    row = lax.broadcasted_iota(jnp.int32, (TILE, TILE), 0)
    column = lax.broadcasted_iota(jnp.int32, (TILE, TILE), 1)

    def one_head(h, _):
        for kind in range(CLASSES):
            bucket = bucket_index(row - column + (kind - 2) * TILE)
            first, last = (0, BUCKETS // 2) if kind < 2 else (BUCKETS // 2, BUCKETS)
            if kind == 2:
                first = 0
            tile = jnp.zeros((TILE, TILE), f32)
            for b in range(first, last):
                tile = jnp.where(bucket == b, table_ref[b, h], tile)
            out_ref[h, kind] = tile
        return 0

    lax.fori_loop(0, heads, one_head, 0)


def bias_tiles(table):
    heads = table.shape[1]
    return pl.pallas_call(
        tiles_kernel,
        out_shape=jax.ShapeDtypeStruct((heads, CLASSES, TILE, TILE), f32),
        in_specs=[pl.BlockSpec(memory_space=pltpu.SMEM)],
        out_specs=pl.BlockSpec(memory_space=pltpu.VMEM),
        name="bias_tiles",
    )(table)


def fold(tile, reduce):
    return reduce(tile.reshape(TILE // 8, 8, TILE), axis=0)


def tile_class(base, key_slot, query_slot):
    difference = lax.bitwise_xor(base, key_slot) - lax.bitwise_xor(base, query_slot)
    return jnp.clip(difference, -2, 2) + 2


def score_tile(base, h, a, i, q_i, k_ref, seg_keys, seg_i, tiles_ref):
    s = lax.dot_general(
        k_ref[a * TILE : (a + 1) * TILE, h * DH : (h + 1) * DH], q_i, NT, preferred_element_type=f32
    )
    kind = tile_class(base, jnp.int32(a), i)
    s = s + tiles_ref[h, kind]
    return jnp.where(seg_keys[a * TILE : (a + 1) * TILE, :] == seg_i, s, score_masked_rows), kind


def forward_kernel(base_ref, q_ref, k_ref, v_ref, segk_ref, segq_ref, tiles_ref, ctx_ref, log_ref, s_scr, p_scr):
    blocks = q_ref.shape[0] // TILE
    base = base_ref[0]
    for h in range(PAIR):
        v_t = v_ref[:, h * DH : (h + 1) * DH].astype(f32).T.astype(bf16)

        def one_block(i, _, h=h, v_t=v_t):
            start = pl.multiple_of(i * TILE, TILE)
            q_i = q_ref[pl.ds(start, TILE), h * DH : (h + 1) * DH]
            seg_i = segq_ref[pl.ds(i, 1), :]
            top = jnp.full((8, TILE), -jnp.inf, f32)
            for a in range(blocks):
                s, _ = score_tile(base, h, a, i, q_i, k_ref, segk_ref, seg_i, tiles_ref)
                s_scr[a * TILE : (a + 1) * TILE, :] = s
                top = jnp.maximum(top, fold(s, jnp.max))
            top = jnp.max(top, axis=0, keepdims=True)
            total = jnp.zeros((8, TILE), f32)
            for a in range(blocks):
                e = jnp.exp(s_scr[a * TILE : (a + 1) * TILE, :] - top)
                p_scr[a * TILE : (a + 1) * TILE, :] = e.astype(bf16)
                total = total + fold(e, jnp.sum)
            total = jnp.sum(total, axis=0, keepdims=True)
            context = lax.dot_general(
                v_t, p_scr[...], (((1,), (0,)), ((), ())), preferred_element_type=f32
            )
            ctx_ref[h * DH : (h + 1) * DH, pl.ds(start, TILE)] = (context / total).astype(bf16)
            log_ref[0, h, pl.ds(i, 1), :] = top + jnp.log(total)
            return 0

        lax.fori_loop(0, blocks, one_block, 0)


def of_pair(rows, kind):
    return pl.BlockSpec((rows, PAIR * DH), lambda j: (0, 3 * j + kind))


def attend(base, qkv, seg_keys, seg_queries, tiles):
    rows, width = qkv.shape[0], qkv.shape[1] // 3
    pairs, blocks = width // (PAIR * DH), rows // TILE
    return pl.pallas_call(
        forward_kernel,
        grid=(pairs,),
        out_shape=(
            jax.ShapeDtypeStruct((width, rows), bf16),
            jax.ShapeDtypeStruct((pairs, PAIR, blocks, TILE), f32),
        ),
        in_specs=[
            pl.BlockSpec(memory_space=pltpu.SMEM),
            of_pair(rows, 0),
            of_pair(rows, 1),
            of_pair(rows, 2),
            pl.BlockSpec((rows, TILE), lambda j: (0, 0)),
            pl.BlockSpec((blocks, TILE), lambda j: (0, 0)),
            pl.BlockSpec((PAIR, CLASSES, TILE, TILE), lambda j: (j, 0, 0, 0)),
        ],
        out_specs=(
            pl.BlockSpec((PAIR * DH, rows), lambda j: (j, 0)),
            pl.BlockSpec((1, PAIR, blocks, TILE), lambda j: (j, 0, 0, 0)),
        ),
        scratch_shapes=[pltpu.VMEM((rows, TILE), f32), pltpu.VMEM((rows, TILE), bf16)],
        compiler_params=pltpu.CompilerParams(vmem_limit_bytes=VMEM_BYTES),
        name="attend_forward",
    )(base, qkv, qkv, qkv, seg_keys, seg_queries, tiles)


def backward_kernel(
    base_ref, q_ref, k_ref, v_ref, do_ref, log_ref, segk_ref, segq_ref, tiles_ref,
    *rest, kept,
):
    grad_ref, bias_ref, p_scr, dp_scr, p_all, ds_all, near = rest[kept:]
    rows = q_ref.shape[0]
    blocks = rows // TILE
    base = base_ref[0]
    row = lax.broadcasted_iota(jnp.int32, (TILE, TILE), 0)
    column = lax.broadcasted_iota(jnp.int32, (TILE, TILE), 1)
    for h in range(PAIR):
        lanes = slice(h * DH, (h + 1) * DH)
        near[...] = jnp.zeros_like(near)

        def one_block(i, _, h=h, lanes=lanes):
            start = pl.multiple_of(i * TILE, TILE)
            q_i = q_ref[pl.ds(start, TILE), lanes]
            do_i = do_ref[pl.ds(start, TILE), lanes]
            seg_i = segq_ref[pl.ds(i, 1), :]
            log_i = log_ref[0, h, pl.ds(i, 1), :]
            delta = jnp.zeros((8, TILE), f32)
            for a in range(blocks):
                here = slice(a * TILE, (a + 1) * TILE)
                s, _ = score_tile(base, h, a, i, q_i, k_ref, segk_ref, seg_i, tiles_ref)
                p = jnp.exp(s - log_i)
                dp = lax.dot_general(v_ref[here, lanes], do_i, NT, preferred_element_type=f32)
                delta = delta + fold(p * dp, jnp.sum)
                p_scr[here, :] = p
                dp_scr[here, :] = dp
                p_all[here, pl.ds(start, TILE)] = p.astype(bf16)
            delta = jnp.sum(delta, axis=0, keepdims=True)
            for a in range(blocks):
                here = slice(a * TILE, (a + 1) * TILE)
                ds = (p_scr[here, :] * (dp_scr[here, :] - delta)).astype(bf16)
                ds_all[here, pl.ds(start, TILE)] = ds
                kind = tile_class(base, jnp.int32(a), i)
                near[kind] = near[kind] + ds.astype(f32)
            return 0

        lax.fori_loop(0, blocks, one_block, 0)
        q_h, do_h = q_ref[:, lanes], do_ref[:, lanes]
        k_t = k_ref[:, lanes].astype(f32).T.astype(bf16)

        def products(a, _, lanes=lanes, q_h=q_h, do_h=do_h, k_t=k_t, h=h):
            here = pl.ds(pl.multiple_of(a * 2 * TILE, 2 * TILE), 2 * TILE)
            dv = jnp.dot(p_all[here, :], do_h, preferred_element_type=f32)
            dk = jnp.dot(ds_all[here, :], q_h, preferred_element_type=f32)
            dq = jnp.dot(k_t, ds_all[:, here], preferred_element_type=f32).T
            for kind, grad in enumerate((dq, dk, dv)):
                first = kind * PAIR * DH + h * DH
                grad_ref[here, first : first + DH] = grad.astype(bf16)
            return 0

        lax.fori_loop(0, blocks // 2, products, 0)
        for b in range(BUCKETS):
            part = jnp.zeros((8, TILE), f32)
            low = b < BUCKETS // 2
            for kind in (1, 2) if low else (2, 3):
                bucket = bucket_index(row - column + (kind - 2) * TILE)
                part = part + fold(jnp.where(bucket == b, near[kind], 0.0), jnp.sum)
            if b == BUCKETS // 2 - 1:
                part = part + fold(near[0], jnp.sum)
            if b == BUCKETS - 1:
                part = part + fold(near[4], jnp.sum)
            bias_ref[h, b] = part


def attend_back(base, pair, qkv, context_grad, log_total, seg_keys, seg_queries, tiles, earlier=None):
    rows, width = context_grad.shape
    blocks = rows // TILE

    def part(kind):
        return pl.BlockSpec((rows, PAIR * DH), lambda j: (0, 3 * pair + kind))

    specs = [
        pl.BlockSpec(memory_space=pltpu.SMEM),
        part(0),
        part(1),
        part(2),
        pl.BlockSpec((rows, PAIR * DH), lambda j: (0, pair)),
        pl.BlockSpec((1, PAIR, blocks, TILE), lambda j: (pair, 0, 0, 0)),
        pl.BlockSpec((rows, TILE), lambda j: (0, 0)),
        pl.BlockSpec((blocks, TILE), lambda j: (0, 0)),
        pl.BlockSpec((PAIR, CLASSES, TILE, TILE), lambda j: (pair, 0, 0, 0)),
    ]
    operands = [base, qkv, qkv, qkv, context_grad, log_total, seg_keys, seg_queries, tiles]
    aliases = {}
    if earlier is not None:
        specs.append(pl.BlockSpec(memory_space=pl.ANY))
        operands.append(earlier)
        aliases = {len(operands) - 1: 0}
    return pl.pallas_call(
        functools.partial(backward_kernel, kept=len(aliases)),
        grid=(1,),
        out_shape=(
            jax.ShapeDtypeStruct((rows, 3 * width), bf16),
            jax.ShapeDtypeStruct((PAIR, BUCKETS, 8, TILE), f32),
        ),
        in_specs=specs,
        out_specs=(
            pl.BlockSpec((rows, 3 * PAIR * DH), lambda j: (0, pair)),
            pl.BlockSpec((PAIR, BUCKETS, 8, TILE), lambda j: (0, 0, 0, 0)),
        ),
        scratch_shapes=[
            pltpu.VMEM((rows, TILE), f32),
            pltpu.VMEM((rows, TILE), f32),
            pltpu.VMEM((rows, rows), bf16),
            pltpu.VMEM((rows, rows), bf16),
            pltpu.VMEM((CLASSES, TILE, TILE), f32),
        ],
        input_output_aliases=aliases,
        compiler_params=pltpu.CompilerParams(vmem_limit_bytes=VMEM_BYTES),
        name="attend_backward",
    )(*operands)


def per_device(
    inputs,
    doc_lengths,
    gain_attn,
    w_query,
    w_key,
    w_value,
    w_out,
    bias_table,
    gain_ff,
    w_gate,
    w_up,
    w_down,
    cotangent,
):
    rows, width = inputs.shape
    planes, members = lax.axis_size("fsdp"), lax.axis_size("ctx")
    me = lax.axis_index("ctx")
    length = rows * members
    heads = H // members
    hidden = w_gate.shape[1] // members
    model = heads * DH
    striped = H == planes * members == BUCKETS

    def own_rows(weight):
        count = weight.shape[0] // members
        return lax.dynamic_slice_in_dim(weight, me * count, count, 0)

    def over_planes(weight):
        return lax.all_gather(weight, "fsdp", axis=0, tiled=True)

    def sum_planes(partial):
        return lax.psum_scatter(partial, "fsdp", scatter_dimension=0, tiled=True)

    def trade(summed):
        moved = summed.reshape(members, -1, summed.shape[1])
        return lax.all_to_all(moved, "ctx", 0, 0, tiled=True)

    head_pieces = planes if striped else 1
    of_heads = head_moves(head_pieces, heads)
    of_hidden = block_moves(2, planes, hidden // planes)
    if striped:
        own_qkv = cut_heads_at_once(w_query, w_key, w_value, w_out, planes, members)
    else:
        own_qkv = cut_columns(
            [w_query, w_key, w_value], head_pieces, me, members, of_heads, "cut_heads"
        )
    if striped:
        gathered = over_planes(own_qkv)
        w_qkv = gathered[:, : 3 * model]
        lanes = gathered.shape[1] - 3 * model
        out_rows = gathered[:, 3 * model :].reshape(planes, width // lanes, -1, lanes)
        out_rows = jnp.transpose(out_rows, (0, 2, 1, 3)).reshape(model, width)
    else:
        w_qkv = over_planes(own_qkv)
        out_rows = lax.dynamic_slice_in_dim(over_planes(w_out), me * model, model, 0)
    w_mix = over_planes(cut_columns([w_gate, w_up], planes, me, members, of_hidden, "cut_hidden"))
    down_rows = over_planes(own_rows(w_down))
    gains = line_gather(after(jnp.stack([gain_attn, gain_ff]), own_qkv)).astype(f32)
    gain_first, gain_second = gains[0], gains[1]

    base = me if by_exchange() else jnp.zeros_like(me)
    slots = jnp.arange(members, dtype=jnp.int32)
    segments = segment_table(doc_lengths[0], length).reshape(members, rows)
    seg_queries = jnp.take(segments, lax.bitwise_xor(base, slots), axis=0)
    seg_queries = seg_queries.reshape(length // TILE, TILE)
    seg_keys = jnp.broadcast_to(seg_queries.reshape(length, 1), (length, TILE))
    base_block = jnp.reshape(base, (1,)).astype(jnp.int32)
    if striped:
        unit = H // (planes * members)
        order = jnp.arange(heads, dtype=jnp.int32)
        own_heads = order // unit * (H // planes) + me * unit + order % unit
    else:
        own_heads = me * heads + jnp.arange(heads, dtype=jnp.int32)
    pick = (jnp.arange(H, dtype=jnp.int32)[:, None] == own_heads[None, :]).astype(f32)
    table = jnp.dot(bias_table.astype(f32), pick, precision=lax.Precision.HIGHEST)
    tiles = bias_tiles(table)

    inputs, cotangent = lax.optimization_barrier((inputs, cotangent, own_qkv))[:2]
    source_all = plane_gather(inputs)
    normed = rms_scale(source_all.astype(f32), gain_first).astype(bf16)
    grad_all = plane_gather(after(cotangent, source_all))
    normed = after(normed, grad_all, tiles)
    qkv = dot(normed, w_qkv).astype(bf16)
    context_t, log_total = attend(base_block, qkv, seg_keys, seg_queries, tiles)
    source = inputs.astype(f32)
    residual = source + plane_scatter(dot(context_t, out_rows, ((0,), (0,))).astype(bf16))

    normed_ff = plane_gather(rms_scale(residual, gain_second).astype(bf16))
    mix = dot(normed_ff, w_mix)
    gate_pre, up_pre = mix[:, :hidden], mix[:, hidden:]
    active_f, mix_back = jax.vjp(gated_mix, gate_pre, up_pre)
    active = active_f.astype(bf16)
    down_grad = dot(active, grad_all, ((0,), (0,))).astype(bf16)
    down_sum = sum_planes(down_grad)
    active_grad = dot(after(grad_all, down_grad), down_rows, ((1,), (1,)))
    gate_grad, up_grad = mix_back(active_grad)
    mix_grad = jnp.concatenate([gate_grad.astype(bf16), up_grad.astype(bf16)], axis=1)
    normed_ff_part = dot(mix_grad, w_mix, ((1,), (1,))).astype(bf16)
    normed_ff_grad = plane_scatter(normed_ff_part)
    mix_grad = after(mix_grad, normed_ff_part)
    mix_weight_grad = dot(normed_ff, mix_grad, ((0,), (0,))).astype(bf16)
    mix_sum = sum_planes(mix_weight_grad)
    norm_back = jax.vjp(lambda v: rms_scale(v, gain_second), residual)[1]
    residual_grad = cotangent.astype(f32) + norm_back(normed_ff_grad)[0]

    residual_low = plane_gather(after(residual_grad.astype(bf16), down_sum, mix_weight_grad))
    output_part = dot(after(active, mix_weight_grad), down_rows).astype(bf16)
    context_grad = dot(after(residual_low, output_part), out_rows, ((1,), (1,))).astype(bf16)
    output_sums = scatter_chips(after(output_part, residual_low))

    def back(pair, grad, earlier=None):
        return attend_back(
            base_block, pair, qkv, grad, log_total, seg_keys, seg_queries, tiles, earlier
        )

    qkv_grad, bias_parts = back(0, context_grad)
    bias_parts = [bias_parts]
    for pair in range(1, heads // PAIR):
        context_grad = after(context_grad, qkv_grad, output_sums)
        qkv_grad, more = back(pair, context_grad, qkv_grad)
        bias_parts.append(more)
    bias_parts = jnp.concatenate(bias_parts, axis=0)
    qkv_weight_grad = dot(normed, qkv_grad, ((0,), (0,))).astype(bf16)
    bias_own = jnp.sum(bias_parts, axis=(2, 3))
    qkv_sent = qkv_weight_grad
    if striped:
        bias_own = bias_own.T.astype(bf16).reshape(planes, members, heads)
        bias_own = jnp.pad(bias_own, ((0, 0), (0, 0), (0, 3 * model - heads)))
        qkv_sent = qkv_sent.reshape(planes, -1, 3 * model)
        qkv_sent = jnp.concatenate([qkv_sent, bias_own], axis=1).reshape(-1, 3 * model)
    qkv_sum = sum_planes(qkv_sent)
    normed_part = dot(after(qkv_grad, qkv_weight_grad), w_qkv, ((1,), (1,))).astype(bf16)
    normed_sums, mix_sum, output_sums = lax.optimization_barrier(
        (scatter_corner(scatter_chips(normed_part)), mix_sum, scatter_corner(output_sums))
    )
    out_weight_grad = dot(context_t, after_all((residual_low,), normed_sums)[0]).astype(bf16)
    moved_mix = trade(mix_sum)
    normed_grad, moved_mix, output_sum = lax.optimization_barrier(
        (scatter_sides(normed_sums), moved_mix, scatter_sides(output_sums))
    )
    output = (residual + output_sum).astype(bf16)
    gate_shard, up_shard = join_columns(moved_mix, 2, planes, of_hidden, "join_hidden")
    qkv_sum = after(qkv_sum, normed_grad)
    if striped:
        own = width // planes
        moved_qkv = [qkv_sum[:own].reshape(members, -1, 3 * model), qkv_sum[own:][:, None]]
        moved_qkv = jnp.concatenate(moved_qkv, axis=1)
        moved_qkv = lax.all_to_all(moved_qkv, "ctx", 0, 0, tiled=True)
        bias_shard = moved_qkv[:, -1, :heads].astype(f32).T.reshape(-1)
        moved_qkv = moved_qkv[:, :-1]
    else:
        moved_qkv = trade(qkv_sum)
        bias_rows = jnp.dot(bias_own.T, pick.T, precision=lax.Precision.HIGHEST).reshape(-1)
        bias_shard = lax.psum_scatter(bias_rows, ("fsdp", "ctx"), scatter_dimension=0, tiled=True)
    first_back = jax.vjp(lambda v: rms_scale(v, gain_first), source)[1]
    input_grad = (residual_grad + first_back(normed_grad)[0]).astype(bf16)

    def gain_grad(gain, pairs):
        return sum(jnp.sum(own_rows(w).astype(f32) * g, axis=1) for w, g in pairs) / own_rows(
            gain
        ).astype(f32)

    down_shard = down_sum.astype(f32)
    ff_gain_shard = gain_grad(gain_ff, ((w_gate, gate_shard), (w_up, up_shard)))
    query_shard, key_shard, value_shard = join_columns(
        moved_qkv, 3, head_pieces, of_heads, "join_heads"
    )
    attn_gain_shard = gain_grad(
        gain_attn, ((w_query, query_shard), (w_key, key_shard), (w_value, value_shard))
    )
    if striped:
        out_shard = after(sum_planes(out_weight_grad), attn_gain_shard).astype(f32)
    else:
        placed = jnp.zeros((H * DH, width), f32)
        placed = lax.dynamic_update_slice_in_dim(placed, out_weight_grad.astype(f32), me * model, 0)
        out_shard = lax.psum_scatter(placed, ("fsdp", "ctx"), scatter_dimension=0, tiled=True)
    return (
        output,
        input_grad,
        attn_gain_shard,
        ff_gain_shard,
        query_shard,
        key_shard,
        value_shard,
        out_shard,
        bias_shard,
        gate_shard,
        up_shard,
        down_shard,
    )


def solution(mesh):
    rows = P(("fsdp", "ctx"), None)
    vector = P(("fsdp", "ctx"))
    weight = P("fsdp", None)
    return jax.shard_map(
        per_device,
        mesh=mesh,
        in_specs=(
            rows,
            P("fsdp", None),
            P("fsdp"),
            weight,
            weight,
            weight,
            weight,
            P(),
            P("fsdp"),
            weight,
            weight,
            weight,
            rows,
        ),
        out_specs=(rows, rows, vector, vector, rows, rows, rows, rows, vector, rows, rows, rows),
        check_vma=False,
    )
```

```python
import functools

import jax
import jax.numpy as jnp
from jax import lax
from jax.experimental import pallas as pl
from jax.experimental.pallas import tpu as pltpu
from jax.sharding import PartitionSpec as P

H = 32
DH = 64
BUCKETS = 32
TILE = 128
PAIR = 2
CLASSES = 5

epsilon = 1e-06
score_masked_rows = -1000000000.0
bucket_edges = (12, 16, 23, 32, 46, 64, 91)
f32 = jnp.float32
bf16 = jnp.bfloat16
NT = (((1,), (1,)), ((), ()))
VMEM_BYTES = 56 * 1024 * 1024


def bucket_index(offset):
    distance = jnp.abs(offset)
    far_bucket = BUCKETS // 4 + sum(
        ((distance >= boundary).astype(jnp.int32) for boundary in bucket_edges)
    )
    within = jnp.where(distance < BUCKETS // 4, distance, far_bucket)
    return within + BUCKETS // 2 * (offset > 0).astype(jnp.int32)


def rms_scale(values, gain_row):
    mean_square = jnp.mean(values * values, axis=-1, keepdims=True)
    return values * lax.rsqrt(mean_square + epsilon) * gain_row


def gated_mix(gate_part, up_part):
    return jax.nn.gelu(gate_part, approximate=True) * up_part


def segment_table(doc_row, total_rows):
    doc_ends = jnp.cumsum(doc_row)
    positions = jnp.arange(total_rows, dtype=jnp.int32)
    return jnp.sum((positions[:, None] >= doc_ends[None, :]).astype(jnp.int32), axis=1)


def dot(left, right, contract=((1,), (0,))):
    return lax.dot_general(left, right, (contract, ((), ())), preferred_element_type=f32)


def swap(block, mask):
    return lax.ppermute(block, "ctx", [(i, i ^ mask) for i in range(lax.axis_size("ctx"))])


def by_exchange():
    return lax.axis_size("ctx") == 8


def plane_gather(block):
    if not by_exchange():
        return lax.all_gather(block, "ctx", axis=0, tiled=True)
    half = block.shape[0] // 2
    from_x, from_y, from_core = swap(block, 2), swap(block, 4), swap(block, 1)
    diagonal = jnp.concatenate([swap(from_x[:half], 4), swap(from_y[half:], 2)], axis=0)
    x_core, y_core = swap(from_x, 1), swap(from_y, 1)
    return jnp.concatenate(
        [block, from_core, from_x, x_core, from_y, y_core, diagonal, swap(diagonal, 1)], axis=0
    )


def scatter_chips(partial):
    if not by_exchange():
        return partial
    rows = partial.shape[0] // 8

    def chip(m):
        mine, other = partial[m * rows : (m + 1) * rows], partial[(m + 1) * rows : (m + 2) * rows]
        return mine.astype(f32) + swap(other, 1).astype(f32)

    diagonal = chip(6).astype(bf16)
    return [chip(0), chip(2), chip(4), diagonal]


def scatter_corner(sums):
    if not by_exchange():
        return sums
    own, x_sum, y_sum, diagonal = sums
    half = own.shape[0] // 2
    via_x, via_y = swap(diagonal[:half], 2), swap(diagonal[half:], 4)
    y_sum = jnp.concatenate([y_sum[:half] + via_x.astype(f32), y_sum[half:]], axis=0)
    x_sum = jnp.concatenate([x_sum[:half], x_sum[half:] + via_y.astype(f32)], axis=0)
    return [own, x_sum.astype(bf16), y_sum.astype(bf16)]


def scatter_sides(sums):
    if not by_exchange():
        return lax.psum_scatter(sums, "ctx", scatter_dimension=0, tiled=True).astype(f32)
    own, x_sum, y_sum = sums
    return own + swap(x_sum, 2).astype(f32) + swap(y_sum, 4).astype(f32)


def plane_scatter(partial):
    return scatter_sides(scatter_corner(scatter_chips(partial)))


def line_gather(small):
    parts = lax.axis_size("fsdp")
    own = lax.axis_index("fsdp")
    whole = jnp.zeros((parts,) + small.shape, small.dtype)
    for step in range(parts):
        piece = (
            small
            if step == 0
            else lax.ppermute(small, "fsdp", [(i, (i + step) % parts) for i in range(parts)])
        )
        whole = lax.dynamic_update_index_in_dim(whole, piece, (own - step) % parts, 0)
    return jnp.transpose(whole, (1, 0, 2)).reshape(small.shape[0], -1)


def cut_plan(cut, members):
    window = max(-(-((cut * p) % TILE + cut) // TILE) for p in range(members))
    return window, members * cut // TILE - window


def cut_kernel(start_ref, *refs, pieces, window, cut, moves, along):
    out_ref = refs[-1]
    if along:
        rows_ref = refs[-2]
        count, groups = rows_ref.shape[0], rows_ref.shape[1] // along
        for group in range(groups):
            part = rows_ref[:, group * along : (group + 1) * along]
            out_ref[group * count : (group + 1) * count, out_ref.shape[1] - along :] = part
    shift = start_ref[1]
    held = {}
    for source, piece, first, length, target in moves:
        if (source, piece) not in held:
            at = (source * pieces + piece) * window
            span = jnp.concatenate([r[...].astype(f32) for r in refs[at : at + window]], axis=1)
            held[source, piece] = pltpu.roll(span, shift, 1)
        part = held[source, piece][:, first : first + length]
        out_ref[:, target : target + length] = part.astype(bf16)


def cut_columns(weights, pieces, me, members, moves, name, along=None):
    rows, width = weights[0].shape
    cut = width // (pieces * members)
    window, most = cut_plan(cut, members)
    blocks = width // pieces // TILE
    start = jnp.minimum(cut * me // TILE, most)
    shift = (window * TILE - (cut * me - start * TILE)) % (window * TILE)
    step = min(rows, 256)
    specs = []
    for _ in weights:
        for piece in range(pieces):
            for w in range(window):
                place = piece * blocks + w
                specs.append(pl.BlockSpec((step, TILE), lambda r, s, place=place: (r, place + s[0])))
    columns = sum(move[3] for move in moves)
    operands = [w for w in weights for _ in range(pieces * window)]
    extra = 0
    if along is not None:
        count = along.shape[0] // members
        extra = count * along.shape[1] // rows
        columns += extra
        specs.append(pl.BlockSpec((count, step // count * extra), lambda r, s: (s[2], r)))
        operands.append(along)
    return pl.pallas_call(
        functools.partial(
            cut_kernel, pieces=pieces, window=window, cut=cut, moves=moves, along=extra
        ),
        grid_spec=pltpu.PrefetchScalarGridSpec(
            num_scalar_prefetch=1,
            grid=(rows // step,),
            in_specs=specs,
            out_specs=pl.BlockSpec((step, columns), lambda r, s: (r, 0)),
        ),
        out_shape=jax.ShapeDtypeStruct((rows, columns), bf16),
        name=name,
    )(jnp.stack([start, shift, me]).astype(jnp.int32), *operands)


def cut_heads_kernel(
    q_ref, k_ref, v_ref, rows_ref, out_ref, held, held_rows, made, sems, out_sems, *, pieces, members
):
    me = lax.axis_index("ctx")
    tiles = members * DH // TILE
    weights = (q_ref, k_ref, v_ref)
    count = held_rows.shape[0]
    copies = []
    for source, weight in enumerate(weights):
        for piece in range(pieces):
            first = pl.multiple_of((piece * tiles + me * DH // TILE) * TILE, TILE)
            at = source * pieces + piece
            copies.append(
                pltpu.make_async_copy(weight.at[:, pl.ds(first, TILE)], held.at[at], sems.at[at])
            )
    first = pl.multiple_of(me * count, count)
    copies.append(
        pltpu.make_async_copy(
            rows_ref.at[pl.ds(first, count), :], held_rows, sems.at[len(weights) * pieces]
        )
    )
    for copy in copies:
        copy.start()
    sent = []

    def send(first, columns, values):
        made[:, first : first + columns] = values
        part = (slice(None), slice(first, first + columns))
        copy = pltpu.make_async_copy(made.at[part], out_ref.at[part], out_sems.at[len(sent)])
        copy.start()
        sent.append(copy)

    row = lax.broadcasted_iota(jnp.int32, (TILE, TILE), 0)
    column = lax.broadcasted_iota(jnp.int32, (TILE, TILE), 1)
    same = row - lax.rem(me * DH, TILE) == lax.rem(column, DH)
    pick = [(same & (column // DH == side)).astype(bf16) for side in range(2)]
    for source in range(len(weights)):
        for pair in range(pieces // 2):
            at = source * pieces + 2 * pair
            copies[at].wait()
            copies[at + 1].wait()
            both = jnp.dot(held[at], pick[0], preferred_element_type=f32)
            both = both + jnp.dot(held[at + 1], pick[1], preferred_element_type=f32)
            send((pair * 3 + source) * TILE, TILE, both.astype(bf16))
    copies[-1].wait()
    first = len(weights) * pieces * DH
    along = made.shape[1] - first
    parts = [
        held_rows[:, group * along : (group + 1) * along]
        for group in range(held_rows.shape[1] // along)
    ]
    send(first, along, jnp.concatenate(parts, axis=0))
    for copy in sent:
        copy.wait()


def cut_heads_at_once(w_query, w_key, w_value, w_out, pieces, members):
    rows, width = w_query.shape
    count = w_out.shape[0] // members
    columns = 3 * pieces * DH + count * width // rows
    return pl.pallas_call(
        functools.partial(cut_heads_kernel, pieces=pieces, members=members),
        out_shape=jax.ShapeDtypeStruct((rows, columns), bf16),
        in_specs=[pl.BlockSpec(memory_space=pl.ANY)] * 4,
        out_specs=pl.BlockSpec(memory_space=pl.ANY),
        scratch_shapes=[
            pltpu.VMEM((3 * pieces, rows, TILE), bf16),
            pltpu.VMEM((count, width), bf16),
            pltpu.VMEM((rows, columns), bf16),
            pltpu.SemaphoreType.DMA((3 * pieces + 1,)),
            pltpu.SemaphoreType.DMA((3 * pieces // 2 + 1,)),
        ],
        compiler_params=pltpu.CompilerParams(vmem_limit_bytes=VMEM_BYTES),
        name="cut_heads",
    )(w_query, w_key, w_value, w_out)


def join_kernel(in_ref, *out_refs, pieces, cut, moves):
    members = in_ref.shape[0]
    for kind, piece, first, length, source in moves:
        for p in range(members):
            target = (piece * members + p) * cut + first
            out_refs[kind][:, target : target + length] = in_ref[p, :, source : source + length].astype(f32)


def join_columns(moved, kinds, pieces, moves, name):
    members, rows, columns = moved.shape
    cut = columns // (kinds * pieces)
    step = min(rows, 32)
    width = members * pieces * cut
    return pl.pallas_call(
        functools.partial(join_kernel, pieces=pieces, cut=cut, moves=moves),
        grid=(rows // step,),
        out_shape=[jax.ShapeDtypeStruct((rows, width), f32)] * kinds,
        in_specs=[pl.BlockSpec((members, step, columns), lambda r: (0, r, 0))],
        out_specs=[pl.BlockSpec((step, width), lambda r: (r, 0))] * kinds,
        name=name,
    )(moved)


def head_moves(pieces, heads):
    each = heads // pieces
    return [
        (kind, t // each, t % each * DH, DH, (t // PAIR * 3 + kind) * PAIR * DH + t % PAIR * DH)
        for t in range(heads)
        for kind in range(3)
    ]


def block_moves(kinds, pieces, cut):
    return [
        (kind, piece, 0, cut, (kind * pieces + piece) * cut)
        for kind in range(kinds)
        for piece in range(pieces)
    ]


def after_all(values, *others):
    return lax.optimization_barrier((values,) + others)[0]


def after(value, *others):
    return lax.optimization_barrier((value,) + others)[0]


def tiles_kernel(table_ref, out_ref):
    heads = out_ref.shape[0]
    row = lax.broadcasted_iota(jnp.int32, (TILE, TILE), 0)
    column = lax.broadcasted_iota(jnp.int32, (TILE, TILE), 1)

    def one_head(h, _):
        for kind in range(CLASSES):
            bucket = bucket_index(row - column + (kind - 2) * TILE)
            first, last = (0, BUCKETS // 2) if kind < 2 else (BUCKETS // 2, BUCKETS)
            if kind == 2:
                first = 0
            tile = jnp.zeros((TILE, TILE), f32)
            for b in range(first, last):
                tile = jnp.where(bucket == b, table_ref[b, h], tile)
            out_ref[h, kind] = tile
        return 0

    lax.fori_loop(0, heads, one_head, 0)


def bias_tiles(table):
    heads = table.shape[1]
    return pl.pallas_call(
        tiles_kernel,
        out_shape=jax.ShapeDtypeStruct((heads, CLASSES, TILE, TILE), f32),
        in_specs=[pl.BlockSpec(memory_space=pltpu.SMEM)],
        out_specs=pl.BlockSpec(memory_space=pltpu.VMEM),
        name="bias_tiles",
    )(table)


def fold(tile, reduce):
    return reduce(tile.reshape(TILE // 8, 8, TILE), axis=0)


def tile_class(base, key_slot, query_slot):
    difference = lax.bitwise_xor(base, key_slot) - lax.bitwise_xor(base, query_slot)
    return jnp.clip(difference, -2, 2) + 2


def score_tile(base, h, a, i, q_i, k_ref, seg_keys, seg_i, tiles_ref):
    s = lax.dot_general(
        k_ref[a * TILE : (a + 1) * TILE, h * DH : (h + 1) * DH], q_i, NT, preferred_element_type=f32
    )
    kind = tile_class(base, jnp.int32(a), i)
    s = s + tiles_ref[h, kind]
    return jnp.where(seg_keys[a * TILE : (a + 1) * TILE, :] == seg_i, s, score_masked_rows), kind


def forward_kernel(base_ref, q_ref, k_ref, v_ref, segk_ref, segq_ref, tiles_ref, ctx_ref, log_ref, s_scr, p_scr):
    blocks = q_ref.shape[0] // TILE
    base = base_ref[0]
    for h in range(PAIR):
        v_t = v_ref[:, h * DH : (h + 1) * DH].astype(f32).T.astype(bf16)

        def one_block(i, _, h=h, v_t=v_t):
            start = pl.multiple_of(i * TILE, TILE)
            q_i = q_ref[pl.ds(start, TILE), h * DH : (h + 1) * DH]
            seg_i = segq_ref[pl.ds(i, 1), :]
            top = jnp.full((8, TILE), -jnp.inf, f32)
            for a in range(blocks):
                s, _ = score_tile(base, h, a, i, q_i, k_ref, segk_ref, seg_i, tiles_ref)
                s_scr[a * TILE : (a + 1) * TILE, :] = s
                top = jnp.maximum(top, fold(s, jnp.max))
            top = jnp.max(top, axis=0, keepdims=True)
            total = jnp.zeros((8, TILE), f32)
            for a in range(blocks):
                e = jnp.exp(s_scr[a * TILE : (a + 1) * TILE, :] - top)
                p_scr[a * TILE : (a + 1) * TILE, :] = e.astype(bf16)
                total = total + fold(e, jnp.sum)
            total = jnp.sum(total, axis=0, keepdims=True)
            context = lax.dot_general(
                v_t, p_scr[...], (((1,), (0,)), ((), ())), preferred_element_type=f32
            )
            ctx_ref[h * DH : (h + 1) * DH, pl.ds(start, TILE)] = (context / total).astype(bf16)
            log_ref[0, h, pl.ds(i, 1), :] = top + jnp.log(total)
            return 0

        lax.fori_loop(0, blocks, one_block, 0)


def of_pair(rows, kind):
    return pl.BlockSpec((rows, PAIR * DH), lambda j: (0, 3 * j + kind))


def attend(base, qkv, seg_keys, seg_queries, tiles):
    rows, width = qkv.shape[0], qkv.shape[1] // 3
    pairs, blocks = width // (PAIR * DH), rows // TILE
    return pl.pallas_call(
        forward_kernel,
        grid=(pairs,),
        out_shape=(
            jax.ShapeDtypeStruct((width, rows), bf16),
            jax.ShapeDtypeStruct((pairs, PAIR, blocks, TILE), f32),
        ),
        in_specs=[
            pl.BlockSpec(memory_space=pltpu.SMEM),
            of_pair(rows, 0),
            of_pair(rows, 1),
            of_pair(rows, 2),
            pl.BlockSpec((rows, TILE), lambda j: (0, 0)),
            pl.BlockSpec((blocks, TILE), lambda j: (0, 0)),
            pl.BlockSpec((PAIR, CLASSES, TILE, TILE), lambda j: (j, 0, 0, 0)),
        ],
        out_specs=(
            pl.BlockSpec((PAIR * DH, rows), lambda j: (j, 0)),
            pl.BlockSpec((1, PAIR, blocks, TILE), lambda j: (j, 0, 0, 0)),
        ),
        scratch_shapes=[pltpu.VMEM((rows, TILE), f32), pltpu.VMEM((rows, TILE), bf16)],
        compiler_params=pltpu.CompilerParams(vmem_limit_bytes=VMEM_BYTES),
        name="attend_forward",
    )(base, qkv, qkv, qkv, seg_keys, seg_queries, tiles)


def backward_kernel(
    base_ref, q_ref, k_ref, v_ref, do_ref, log_ref, segk_ref, segq_ref, tiles_ref,
    *rest, kept,
):
    grad_ref, bias_ref, p_scr, dp_scr, p_all, ds_all, near = rest[kept:]
    rows = q_ref.shape[0]
    blocks = rows // TILE
    base = base_ref[0]
    row = lax.broadcasted_iota(jnp.int32, (TILE, TILE), 0)
    column = lax.broadcasted_iota(jnp.int32, (TILE, TILE), 1)
    for h in range(PAIR):
        lanes = slice(h * DH, (h + 1) * DH)
        near[...] = jnp.zeros_like(near)

        def one_block(i, _, h=h, lanes=lanes):
            start = pl.multiple_of(i * TILE, TILE)
            q_i = q_ref[pl.ds(start, TILE), lanes]
            do_i = do_ref[pl.ds(start, TILE), lanes]
            seg_i = segq_ref[pl.ds(i, 1), :]
            log_i = log_ref[0, h, pl.ds(i, 1), :]
            delta = jnp.zeros((8, TILE), f32)
            for a in range(blocks):
                here = slice(a * TILE, (a + 1) * TILE)
                s, _ = score_tile(base, h, a, i, q_i, k_ref, segk_ref, seg_i, tiles_ref)
                p = jnp.exp(s - log_i)
                dp = lax.dot_general(v_ref[here, lanes], do_i, NT, preferred_element_type=f32)
                delta = delta + fold(p * dp, jnp.sum)
                p_scr[here, :] = p
                dp_scr[here, :] = dp
                p_all[here, pl.ds(start, TILE)] = p.astype(bf16)
            delta = jnp.sum(delta, axis=0, keepdims=True)
            for a in range(blocks):
                here = slice(a * TILE, (a + 1) * TILE)
                ds = (p_scr[here, :] * (dp_scr[here, :] - delta)).astype(bf16)
                ds_all[here, pl.ds(start, TILE)] = ds
                kind = tile_class(base, jnp.int32(a), i)
                near[kind] = near[kind] + ds.astype(f32)
            return 0

        lax.fori_loop(0, blocks, one_block, 0)
        q_h, do_h = q_ref[:, lanes], do_ref[:, lanes]
        k_t = k_ref[:, lanes].astype(f32).T.astype(bf16)

        def products(a, _, lanes=lanes, q_h=q_h, do_h=do_h, k_t=k_t, h=h):
            here = pl.ds(pl.multiple_of(a * 2 * TILE, 2 * TILE), 2 * TILE)
            dv = jnp.dot(p_all[here, :], do_h, preferred_element_type=f32)
            dk = jnp.dot(ds_all[here, :], q_h, preferred_element_type=f32)
            dq = jnp.dot(k_t, ds_all[:, here], preferred_element_type=f32).T
            for kind, grad in enumerate((dq, dk, dv)):
                first = kind * PAIR * DH + h * DH
                grad_ref[here, first : first + DH] = grad.astype(bf16)
            return 0

        lax.fori_loop(0, blocks // 2, products, 0)
        for b in range(BUCKETS):
            part = jnp.zeros((8, TILE), f32)
            low = b < BUCKETS // 2
            for kind in (1, 2) if low else (2, 3):
                bucket = bucket_index(row - column + (kind - 2) * TILE)
                part = part + fold(jnp.where(bucket == b, near[kind], 0.0), jnp.sum)
            if b == BUCKETS // 2 - 1:
                part = part + fold(near[0], jnp.sum)
            if b == BUCKETS - 1:
                part = part + fold(near[4], jnp.sum)
            bias_ref[h, b] = part


def attend_back(base, pair, qkv, context_grad, log_total, seg_keys, seg_queries, tiles, earlier=None):
    rows, width = context_grad.shape
    blocks = rows // TILE

    def part(kind):
        return pl.BlockSpec((rows, PAIR * DH), lambda j: (0, 3 * pair + kind))

    specs = [
        pl.BlockSpec(memory_space=pltpu.SMEM),
        part(0),
        part(1),
        part(2),
        pl.BlockSpec((rows, PAIR * DH), lambda j: (0, pair)),
        pl.BlockSpec((1, PAIR, blocks, TILE), lambda j: (pair, 0, 0, 0)),
        pl.BlockSpec((rows, TILE), lambda j: (0, 0)),
        pl.BlockSpec((blocks, TILE), lambda j: (0, 0)),
        pl.BlockSpec((PAIR, CLASSES, TILE, TILE), lambda j: (pair, 0, 0, 0)),
    ]
    operands = [base, qkv, qkv, qkv, context_grad, log_total, seg_keys, seg_queries, tiles]
    aliases = {}
    if earlier is not None:
        specs.append(pl.BlockSpec(memory_space=pl.ANY))
        operands.append(earlier)
        aliases = {len(operands) - 1: 0}
    return pl.pallas_call(
        functools.partial(backward_kernel, kept=len(aliases)),
        grid=(1,),
        out_shape=(
            jax.ShapeDtypeStruct((rows, 3 * width), bf16),
            jax.ShapeDtypeStruct((PAIR, BUCKETS, 8, TILE), f32),
        ),
        in_specs=specs,
        out_specs=(
            pl.BlockSpec((rows, 3 * PAIR * DH), lambda j: (0, pair)),
            pl.BlockSpec((PAIR, BUCKETS, 8, TILE), lambda j: (0, 0, 0, 0)),
        ),
        scratch_shapes=[
            pltpu.VMEM((rows, TILE), f32),
            pltpu.VMEM((rows, TILE), f32),
            pltpu.VMEM((rows, rows), bf16),
            pltpu.VMEM((rows, rows), bf16),
            pltpu.VMEM((CLASSES, TILE, TILE), f32),
        ],
        input_output_aliases=aliases,
        compiler_params=pltpu.CompilerParams(vmem_limit_bytes=VMEM_BYTES),
        name="attend_backward",
    )(*operands)


def per_device(
    inputs,
    doc_lengths,
    gain_attn,
    w_query,
    w_key,
    w_value,
    w_out,
    bias_table,
    gain_ff,
    w_gate,
    w_up,
    w_down,
    cotangent,
):
    rows, width = inputs.shape
    planes, members = lax.axis_size("fsdp"), lax.axis_size("ctx")
    me = lax.axis_index("ctx")
    length = rows * members
    heads = H // members
    hidden = w_gate.shape[1] // members
    model = heads * DH
    striped = H == planes * members == BUCKETS

    def own_rows(weight):
        count = weight.shape[0] // members
        return lax.dynamic_slice_in_dim(weight, me * count, count, 0)

    def over_planes(weight):
        return lax.all_gather(weight, "fsdp", axis=0, tiled=True)

    def sum_planes(partial):
        return lax.psum_scatter(partial, "fsdp", scatter_dimension=0, tiled=True)

    def trade(summed):
        moved = summed.reshape(members, -1, summed.shape[1])
        return lax.all_to_all(moved, "ctx", 0, 0, tiled=True)

    head_pieces = planes if striped else 1
    of_heads = head_moves(head_pieces, heads)
    of_hidden = block_moves(2, planes, hidden // planes)
    if striped:
        own_qkv = cut_heads_at_once(w_query, w_key, w_value, w_out, planes, members)
    else:
        own_qkv = cut_columns(
            [w_query, w_key, w_value], head_pieces, me, members, of_heads, "cut_heads"
        )
    if striped:
        gathered = over_planes(own_qkv)
        w_qkv = gathered[:, : 3 * model]
        lanes = gathered.shape[1] - 3 * model
        out_rows = gathered[:, 3 * model :].reshape(planes, width // lanes, -1, lanes)
        out_rows = jnp.transpose(out_rows, (0, 2, 1, 3)).reshape(model, width)
    else:
        w_qkv = over_planes(own_qkv)
        out_rows = lax.dynamic_slice_in_dim(over_planes(w_out), me * model, model, 0)
    w_mix = over_planes(cut_columns([w_gate, w_up], planes, me, members, of_hidden, "cut_hidden"))
    down_rows = over_planes(own_rows(w_down))
    gains = line_gather(after(jnp.stack([gain_attn, gain_ff]), own_qkv)).astype(f32)
    gain_first, gain_second = gains[0], gains[1]

    base = me if by_exchange() else jnp.zeros_like(me)
    slots = jnp.arange(members, dtype=jnp.int32)
    segments = segment_table(doc_lengths[0], length).reshape(members, rows)
    seg_queries = jnp.take(segments, lax.bitwise_xor(base, slots), axis=0)
    seg_queries = seg_queries.reshape(length // TILE, TILE)
    seg_keys = jnp.broadcast_to(seg_queries.reshape(length, 1), (length, TILE))
    base_block = jnp.reshape(base, (1,)).astype(jnp.int32)
    if striped:
        unit = H // (planes * members)
        order = jnp.arange(heads, dtype=jnp.int32)
        own_heads = order // unit * (H // planes) + me * unit + order % unit
    else:
        own_heads = me * heads + jnp.arange(heads, dtype=jnp.int32)
    pick = (jnp.arange(H, dtype=jnp.int32)[:, None] == own_heads[None, :]).astype(f32)
    table = jnp.dot(bias_table.astype(f32), pick, precision=lax.Precision.HIGHEST)
    tiles = bias_tiles(table)

    inputs, cotangent = lax.optimization_barrier((inputs, cotangent, own_qkv))[:2]
    source_all = plane_gather(inputs)
    normed = rms_scale(source_all.astype(f32), gain_first).astype(bf16)
    grad_all = plane_gather(after(cotangent, source_all))
    normed = after(normed, grad_all, tiles)
    qkv = dot(normed, w_qkv).astype(bf16)
    context_t, log_total = attend(base_block, qkv, seg_keys, seg_queries, tiles)
    source = inputs.astype(f32)
    residual = source + plane_scatter(dot(context_t, out_rows, ((0,), (0,))).astype(bf16))

    normed_ff = plane_gather(rms_scale(residual, gain_second).astype(bf16))
    mix = dot(normed_ff, w_mix)
    gate_pre, up_pre = mix[:, :hidden], mix[:, hidden:]
    active_f, mix_back = jax.vjp(gated_mix, gate_pre, up_pre)
    active = active_f.astype(bf16)
    down_grad = dot(active, grad_all, ((0,), (0,))).astype(bf16)
    down_sum = sum_planes(down_grad)
    active_grad = dot(after(grad_all, down_grad), down_rows, ((1,), (1,)))
    gate_grad, up_grad = mix_back(active_grad)
    mix_grad = jnp.concatenate([gate_grad.astype(bf16), up_grad.astype(bf16)], axis=1)
    normed_ff_part = dot(mix_grad, w_mix, ((1,), (1,))).astype(bf16)
    normed_ff_grad = plane_scatter(normed_ff_part)
    mix_grad = after(mix_grad, normed_ff_part)
    mix_weight_grad = dot(normed_ff, mix_grad, ((0,), (0,))).astype(bf16)
    mix_sum = sum_planes(mix_weight_grad)
    norm_back = jax.vjp(lambda v: rms_scale(v, gain_second), residual)[1]
    residual_grad = cotangent.astype(f32) + norm_back(normed_ff_grad)[0]

    residual_low = plane_gather(after(residual_grad.astype(bf16), down_sum, mix_weight_grad))
    output_part = dot(after(active, mix_weight_grad), down_rows).astype(bf16)
    context_grad = dot(after(residual_low, output_part), out_rows, ((1,), (1,))).astype(bf16)
    output_sums = scatter_chips(after(output_part, residual_low))

    def back(pair, grad, earlier=None):
        return attend_back(
            base_block, pair, qkv, grad, log_total, seg_keys, seg_queries, tiles, earlier
        )

    qkv_grad, bias_parts = back(0, context_grad)
    bias_parts = [bias_parts]
    for pair in range(1, heads // PAIR):
        context_grad = after(context_grad, qkv_grad, output_sums)
        qkv_grad, more = back(pair, context_grad, qkv_grad)
        bias_parts.append(more)
    bias_parts = jnp.concatenate(bias_parts, axis=0)
    qkv_weight_grad = dot(normed, qkv_grad, ((0,), (0,))).astype(bf16)
    bias_own = jnp.sum(bias_parts, axis=(2, 3))
    qkv_sent = qkv_weight_grad
    if striped:
        bias_own = bias_own.T.astype(bf16).reshape(planes, members, heads)
        bias_own = jnp.pad(bias_own, ((0, 0), (0, 0), (0, 3 * model - heads)))
        qkv_sent = qkv_sent.reshape(planes, -1, 3 * model)
        qkv_sent = jnp.concatenate([qkv_sent, bias_own], axis=1).reshape(-1, 3 * model)
    qkv_sum = sum_planes(qkv_sent)
    normed_part = dot(after(qkv_grad, qkv_weight_grad), w_qkv, ((1,), (1,))).astype(bf16)
    normed_sums, mix_sum, output_sums = lax.optimization_barrier(
        (scatter_corner(scatter_chips(normed_part)), mix_sum, scatter_corner(output_sums))
    )
    out_weight_grad = dot(context_t, after_all((residual_low,), normed_sums)[0]).astype(bf16)
    moved_mix = trade(mix_sum)
    normed_grad, moved_mix, output_sum = lax.optimization_barrier(
        (scatter_sides(normed_sums), moved_mix, scatter_sides(output_sums))
    )
    output = (residual + output_sum).astype(bf16)
    gate_shard, up_shard = join_columns(moved_mix, 2, planes, of_hidden, "join_hidden")
    qkv_sum = after(qkv_sum, normed_grad)
    if striped:
        own = width // planes
        moved_qkv = [qkv_sum[:own].reshape(members, -1, 3 * model), qkv_sum[own:][:, None]]
        moved_qkv = jnp.concatenate(moved_qkv, axis=1)
        moved_qkv = lax.all_to_all(moved_qkv, "ctx", 0, 0, tiled=True)
        bias_shard = moved_qkv[:, -1, :heads].astype(f32).T.reshape(-1)
        moved_qkv = moved_qkv[:, :-1]
    else:
        moved_qkv = trade(qkv_sum)
        bias_rows = jnp.dot(bias_own.T, pick.T, precision=lax.Precision.HIGHEST).reshape(-1)
        bias_shard = lax.psum_scatter(bias_rows, ("fsdp", "ctx"), scatter_dimension=0, tiled=True)
    first_back = jax.vjp(lambda v: rms_scale(v, gain_first), source)[1]
    input_grad = (residual_grad + first_back(normed_grad)[0]).astype(bf16)

    def gain_grad(gain, pairs):
        return sum(jnp.sum(own_rows(w).astype(f32) * g, axis=1) for w, g in pairs) / own_rows(
            gain
        ).astype(f32)

    down_shard = down_sum.astype(f32)
    ff_gain_shard = gain_grad(gain_ff, ((w_gate, gate_shard), (w_up, up_shard)))
    query_shard, key_shard, value_shard = join_columns(
        moved_qkv, 3, head_pieces, of_heads, "join_heads"
    )
    attn_gain_shard = gain_grad(
        gain_attn, ((w_query, query_shard), (w_key, key_shard), (w_value, value_shard))
    )
    if striped:
        out_shard = after(sum_planes(out_weight_grad), attn_gain_shard).astype(f32)
    else:
        placed = jnp.zeros((H * DH, width), f32)
        placed = lax.dynamic_update_slice_in_dim(placed, out_weight_grad.astype(f32), me * model, 0)
        out_shard = lax.psum_scatter(placed, ("fsdp", "ctx"), scatter_dimension=0, tiled=True)
    return (
        output,
        input_grad,
        attn_gain_shard,
        ff_gain_shard,
        query_shard,
        key_shard,
        value_shard,
        out_shard,
        bias_shard,
        gate_shard,
        up_shard,
        down_shard,
    )


def solution(mesh):
    rows = P(("fsdp", "ctx"), None)
    vector = P(("fsdp", "ctx"))
    weight = P("fsdp", None)
    return jax.shard_map(
        per_device,
        mesh=mesh,
        in_specs=(
            rows,
            P("fsdp", None),
            P("fsdp"),
            weight,
            weight,
            weight,
            weight,
            P(),
            P("fsdp"),
            weight,
            weight,
            weight,
            rows,
        ),
        out_specs=(rows, rows, vector, vector, rows, rows, rows, rows, vector, rows, rows, rows),
        check_vma=False,
    )
```

```python
import functools

import jax
import jax.numpy as jnp
from jax import lax
from jax.experimental import pallas as pl
from jax.experimental.pallas import tpu as pltpu
from jax.sharding import PartitionSpec as P

H = 32
DH = 64
BUCKETS = 32
TILE = 128
PAIR = 2
CLASSES = 5

epsilon = 1e-06
score_masked_rows = -1000000000.0
bucket_edges = (12, 16, 23, 32, 46, 64, 91)
f32 = jnp.float32
bf16 = jnp.bfloat16
NT = (((1,), (1,)), ((), ()))
VMEM_BYTES = 56 * 1024 * 1024


def bucket_index(offset):
    distance = jnp.abs(offset)
    far_bucket = BUCKETS // 4 + sum(
        ((distance >= boundary).astype(jnp.int32) for boundary in bucket_edges)
    )
    within = jnp.where(distance < BUCKETS // 4, distance, far_bucket)
    return within + BUCKETS // 2 * (offset > 0).astype(jnp.int32)


def rms_scale(values, gain_row):
    mean_square = jnp.mean(values * values, axis=-1, keepdims=True)
    return values * lax.rsqrt(mean_square + epsilon) * gain_row


def gated_mix(gate_part, up_part):
    return jax.nn.gelu(gate_part, approximate=True) * up_part


def segment_table(doc_row, total_rows):
    doc_ends = jnp.cumsum(doc_row)
    positions = jnp.arange(total_rows, dtype=jnp.int32)
    return jnp.sum((positions[:, None] >= doc_ends[None, :]).astype(jnp.int32), axis=1)


def dot(left, right, contract=((1,), (0,))):
    return lax.dot_general(left, right, (contract, ((), ())), preferred_element_type=f32)


def swap(block, mask):
    return lax.ppermute(block, "ctx", [(i, i ^ mask) for i in range(lax.axis_size("ctx"))])


def by_exchange():
    return lax.axis_size("ctx") == 8


def plane_gather(block):
    if not by_exchange():
        return lax.all_gather(block, "ctx", axis=0, tiled=True)
    half = block.shape[0] // 2
    from_x, from_y, from_core = swap(block, 2), swap(block, 4), swap(block, 1)
    diagonal = jnp.concatenate([swap(from_x[:half], 4), swap(from_y[half:], 2)], axis=0)
    x_core, y_core = swap(from_x, 1), swap(from_y, 1)
    return jnp.concatenate(
        [block, from_core, from_x, x_core, from_y, y_core, diagonal, swap(diagonal, 1)], axis=0
    )


def scatter_chips(partial):
    if not by_exchange():
        return partial
    rows = partial.shape[0] // 8

    def chip(m):
        mine, other = partial[m * rows : (m + 1) * rows], partial[(m + 1) * rows : (m + 2) * rows]
        return mine.astype(f32) + swap(other, 1).astype(f32)

    diagonal = chip(6).astype(bf16)
    return [chip(0), chip(2), chip(4), diagonal]


def scatter_corner(sums):
    if not by_exchange():
        return sums
    own, x_sum, y_sum, diagonal = sums
    half = own.shape[0] // 2
    via_x, via_y = swap(diagonal[:half], 2), swap(diagonal[half:], 4)
    y_sum = jnp.concatenate([y_sum[:half] + via_x.astype(f32), y_sum[half:]], axis=0)
    x_sum = jnp.concatenate([x_sum[:half], x_sum[half:] + via_y.astype(f32)], axis=0)
    return [own, x_sum.astype(bf16), y_sum.astype(bf16)]


def scatter_sides(sums):
    if not by_exchange():
        return lax.psum_scatter(sums, "ctx", scatter_dimension=0, tiled=True).astype(f32)
    own, x_sum, y_sum = sums
    return own + swap(x_sum, 2).astype(f32) + swap(y_sum, 4).astype(f32)


def plane_scatter(partial):
    return scatter_sides(scatter_corner(scatter_chips(partial)))


def line_gather(small):
    parts = lax.axis_size("fsdp")
    own = lax.axis_index("fsdp")
    whole = jnp.zeros((parts,) + small.shape, small.dtype)
    for step in range(parts):
        piece = (
            small
            if step == 0
            else lax.ppermute(small, "fsdp", [(i, (i + step) % parts) for i in range(parts)])
        )
        whole = lax.dynamic_update_index_in_dim(whole, piece, (own - step) % parts, 0)
    return jnp.transpose(whole, (1, 0, 2)).reshape(small.shape[0], -1)


def cut_plan(cut, members):
    window = max(-(-((cut * p) % TILE + cut) // TILE) for p in range(members))
    return window, members * cut // TILE - window


def cut_kernel(start_ref, *refs, pieces, window, cut, moves, along):
    out_ref = refs[-1]
    if along:
        rows_ref = refs[-2]
        count, groups = rows_ref.shape[0], rows_ref.shape[1] // along
        for group in range(groups):
            part = rows_ref[:, group * along : (group + 1) * along]
            out_ref[group * count : (group + 1) * count, out_ref.shape[1] - along :] = part
    shift = start_ref[1]
    held = {}
    for source, piece, first, length, target in moves:
        if (source, piece) not in held:
            at = (source * pieces + piece) * window
            span = jnp.concatenate([r[...].astype(f32) for r in refs[at : at + window]], axis=1)
            held[source, piece] = pltpu.roll(span, shift, 1)
        part = held[source, piece][:, first : first + length]
        out_ref[:, target : target + length] = part.astype(bf16)


def cut_columns(weights, pieces, me, members, moves, name, along=None):
    rows, width = weights[0].shape
    cut = width // (pieces * members)
    window, most = cut_plan(cut, members)
    blocks = width // pieces // TILE
    start = jnp.minimum(cut * me // TILE, most)
    shift = (window * TILE - (cut * me - start * TILE)) % (window * TILE)
    step = min(rows, 256)
    specs = []
    for _ in weights:
        for piece in range(pieces):
            for w in range(window):
                place = piece * blocks + w
                specs.append(pl.BlockSpec((step, TILE), lambda r, s, place=place: (r, place + s[0])))
    columns = sum(move[3] for move in moves)
    operands = [w for w in weights for _ in range(pieces * window)]
    extra = 0
    if along is not None:
        count = along.shape[0] // members
        extra = count * along.shape[1] // rows
        columns += extra
        specs.append(pl.BlockSpec((count, step // count * extra), lambda r, s: (s[2], r)))
        operands.append(along)
    return pl.pallas_call(
        functools.partial(
            cut_kernel, pieces=pieces, window=window, cut=cut, moves=moves, along=extra
        ),
        grid_spec=pltpu.PrefetchScalarGridSpec(
            num_scalar_prefetch=1,
            grid=(rows // step,),
            in_specs=specs,
            out_specs=pl.BlockSpec((step, columns), lambda r, s: (r, 0)),
        ),
        out_shape=jax.ShapeDtypeStruct((rows, columns), bf16),
        name=name,
    )(jnp.stack([start, shift, me]).astype(jnp.int32), *operands)


def cut_heads_kernel(q_ref, k_ref, v_ref, rows_ref, out_ref, held, held_rows, sems, *, pieces, members):
    me = lax.axis_index("ctx")
    tiles = members * DH // TILE
    weights = (q_ref, k_ref, v_ref)
    count = held_rows.shape[0]
    copies = []
    for source, weight in enumerate(weights):
        for piece in range(pieces):
            first = pl.multiple_of((piece * tiles + me * DH // TILE) * TILE, TILE)
            at = source * pieces + piece
            copies.append(
                pltpu.make_async_copy(weight.at[:, pl.ds(first, TILE)], held.at[at], sems.at[at])
            )
    first = pl.multiple_of(me * count, count)
    copies.append(
        pltpu.make_async_copy(
            rows_ref.at[pl.ds(first, count), :], held_rows, sems.at[len(weights) * pieces]
        )
    )
    for copy in copies:
        copy.start()
    row = lax.broadcasted_iota(jnp.int32, (TILE, TILE), 0)
    column = lax.broadcasted_iota(jnp.int32, (TILE, TILE), 1)
    same = row - lax.rem(me * DH, TILE) == lax.rem(column, DH)
    pick = [(same & (column // DH == side)).astype(bf16) for side in range(2)]
    for source in range(len(weights)):
        for pair in range(pieces // 2):
            at = source * pieces + 2 * pair
            copies[at].wait()
            copies[at + 1].wait()
            both = jnp.dot(held[at], pick[0], preferred_element_type=f32)
            both = both + jnp.dot(held[at + 1], pick[1], preferred_element_type=f32)
            target = (pair * 3 + source) * TILE
            out_ref[:, target : target + TILE] = both.astype(bf16)
    copies[-1].wait()
    along = out_ref.shape[1] - len(weights) * pieces * DH
    for group in range(held_rows.shape[1] // along):
        part = held_rows[:, group * along : (group + 1) * along]
        out_ref[group * count : (group + 1) * count, out_ref.shape[1] - along :] = part


def cut_heads_at_once(w_query, w_key, w_value, w_out, pieces, members):
    rows, width = w_query.shape
    count = w_out.shape[0] // members
    columns = 3 * pieces * DH + count * width // rows
    return pl.pallas_call(
        functools.partial(cut_heads_kernel, pieces=pieces, members=members),
        out_shape=jax.ShapeDtypeStruct((rows, columns), bf16),
        in_specs=[pl.BlockSpec(memory_space=pl.ANY)] * 4,
        out_specs=pl.BlockSpec(memory_space=pltpu.VMEM),
        scratch_shapes=[
            pltpu.VMEM((3 * pieces, rows, TILE), bf16),
            pltpu.VMEM((count, width), bf16),
            pltpu.SemaphoreType.DMA((3 * pieces + 1,)),
        ],
        compiler_params=pltpu.CompilerParams(vmem_limit_bytes=VMEM_BYTES),
        name="cut_heads",
    )(w_query, w_key, w_value, w_out)


def join_kernel(in_ref, *out_refs, pieces, cut, moves):
    members = in_ref.shape[0]
    for kind, piece, first, length, source in moves:
        for p in range(members):
            target = (piece * members + p) * cut + first
            out_refs[kind][:, target : target + length] = in_ref[p, :, source : source + length].astype(f32)


def join_columns(moved, kinds, pieces, moves, name):
    members, rows, columns = moved.shape
    cut = columns // (kinds * pieces)
    step = min(rows, 32)
    width = members * pieces * cut
    return pl.pallas_call(
        functools.partial(join_kernel, pieces=pieces, cut=cut, moves=moves),
        grid=(rows // step,),
        out_shape=[jax.ShapeDtypeStruct((rows, width), f32)] * kinds,
        in_specs=[pl.BlockSpec((members, step, columns), lambda r: (0, r, 0))],
        out_specs=[pl.BlockSpec((step, width), lambda r: (r, 0))] * kinds,
        name=name,
    )(moved)


def head_moves(pieces, heads):
    each = heads // pieces
    return [
        (kind, t // each, t % each * DH, DH, (t // PAIR * 3 + kind) * PAIR * DH + t % PAIR * DH)
        for t in range(heads)
        for kind in range(3)
    ]


def block_moves(kinds, pieces, cut):
    return [
        (kind, piece, 0, cut, (kind * pieces + piece) * cut)
        for kind in range(kinds)
        for piece in range(pieces)
    ]


def after_all(values, *others):
    return lax.optimization_barrier((values,) + others)[0]


def after(value, *others):
    return lax.optimization_barrier((value,) + others)[0]


def tiles_kernel(table_ref, out_ref):
    heads = out_ref.shape[0]
    row = lax.broadcasted_iota(jnp.int32, (TILE, TILE), 0)
    column = lax.broadcasted_iota(jnp.int32, (TILE, TILE), 1)

    def one_head(h, _):
        for kind in range(CLASSES):
            bucket = bucket_index(row - column + (kind - 2) * TILE)
            first, last = (0, BUCKETS // 2) if kind < 2 else (BUCKETS // 2, BUCKETS)
            if kind == 2:
                first = 0
            tile = jnp.zeros((TILE, TILE), f32)
            for b in range(first, last):
                tile = jnp.where(bucket == b, table_ref[b, h], tile)
            out_ref[h, kind] = tile
        return 0

    lax.fori_loop(0, heads, one_head, 0)


def bias_tiles(table):
    heads = table.shape[1]
    return pl.pallas_call(
        tiles_kernel,
        out_shape=jax.ShapeDtypeStruct((heads, CLASSES, TILE, TILE), f32),
        in_specs=[pl.BlockSpec(memory_space=pltpu.SMEM)],
        out_specs=pl.BlockSpec(memory_space=pltpu.VMEM),
        name="bias_tiles",
    )(table)


def fold(tile, reduce):
    return reduce(tile.reshape(TILE // 8, 8, TILE), axis=0)


def tile_class(base, key_slot, query_slot):
    difference = lax.bitwise_xor(base, key_slot) - lax.bitwise_xor(base, query_slot)
    return jnp.clip(difference, -2, 2) + 2


def score_tile(base, h, a, i, q_i, k_ref, seg_keys, seg_i, tiles_ref):
    s = lax.dot_general(
        k_ref[a * TILE : (a + 1) * TILE, h * DH : (h + 1) * DH], q_i, NT, preferred_element_type=f32
    )
    kind = tile_class(base, jnp.int32(a), i)
    s = s + tiles_ref[h, kind]
    return jnp.where(seg_keys[a * TILE : (a + 1) * TILE, :] == seg_i, s, score_masked_rows), kind


def forward_kernel(base_ref, q_ref, k_ref, v_ref, segk_ref, segq_ref, tiles_ref, ctx_ref, log_ref, s_scr, p_scr):
    blocks = q_ref.shape[0] // TILE
    base = base_ref[0]
    for h in range(PAIR):
        v_t = v_ref[:, h * DH : (h + 1) * DH].astype(f32).T.astype(bf16)

        def one_block(i, _, h=h, v_t=v_t):
            start = pl.multiple_of(i * TILE, TILE)
            q_i = q_ref[pl.ds(start, TILE), h * DH : (h + 1) * DH]
            seg_i = segq_ref[pl.ds(i, 1), :]
            top = jnp.full((8, TILE), -jnp.inf, f32)
            for a in range(blocks):
                s, _ = score_tile(base, h, a, i, q_i, k_ref, segk_ref, seg_i, tiles_ref)
                s_scr[a * TILE : (a + 1) * TILE, :] = s
                top = jnp.maximum(top, fold(s, jnp.max))
            top = jnp.max(top, axis=0, keepdims=True)
            total = jnp.zeros((8, TILE), f32)
            for a in range(blocks):
                e = jnp.exp(s_scr[a * TILE : (a + 1) * TILE, :] - top)
                p_scr[a * TILE : (a + 1) * TILE, :] = e.astype(bf16)
                total = total + fold(e, jnp.sum)
            total = jnp.sum(total, axis=0, keepdims=True)
            context = lax.dot_general(
                v_t, p_scr[...], (((1,), (0,)), ((), ())), preferred_element_type=f32
            )
            ctx_ref[h * DH : (h + 1) * DH, pl.ds(start, TILE)] = (context / total).astype(bf16)
            log_ref[0, h, pl.ds(i, 1), :] = top + jnp.log(total)
            return 0

        lax.fori_loop(0, blocks, one_block, 0)


def of_pair(rows, kind):
    return pl.BlockSpec((rows, PAIR * DH), lambda j: (0, 3 * j + kind))


def attend(base, qkv, seg_keys, seg_queries, tiles):
    rows, width = qkv.shape[0], qkv.shape[1] // 3
    pairs, blocks = width // (PAIR * DH), rows // TILE
    return pl.pallas_call(
        forward_kernel,
        grid=(pairs,),
        out_shape=(
            jax.ShapeDtypeStruct((width, rows), bf16),
            jax.ShapeDtypeStruct((pairs, PAIR, blocks, TILE), f32),
        ),
        in_specs=[
            pl.BlockSpec(memory_space=pltpu.SMEM),
            of_pair(rows, 0),
            of_pair(rows, 1),
            of_pair(rows, 2),
            pl.BlockSpec((rows, TILE), lambda j: (0, 0)),
            pl.BlockSpec((blocks, TILE), lambda j: (0, 0)),
            pl.BlockSpec((PAIR, CLASSES, TILE, TILE), lambda j: (j, 0, 0, 0)),
        ],
        out_specs=(
            pl.BlockSpec((PAIR * DH, rows), lambda j: (j, 0)),
            pl.BlockSpec((1, PAIR, blocks, TILE), lambda j: (j, 0, 0, 0)),
        ),
        scratch_shapes=[pltpu.VMEM((rows, TILE), f32), pltpu.VMEM((rows, TILE), bf16)],
        compiler_params=pltpu.CompilerParams(vmem_limit_bytes=VMEM_BYTES),
        name="attend_forward",
    )(base, qkv, qkv, qkv, seg_keys, seg_queries, tiles)


def backward_kernel(
    base_ref, q_ref, k_ref, v_ref, do_ref, log_ref, segk_ref, segq_ref, tiles_ref,
    *rest, kept,
):
    grad_ref, bias_ref, p_scr, dp_scr, p_all, ds_all, near = rest[kept:]
    rows = q_ref.shape[0]
    blocks = rows // TILE
    base = base_ref[0]
    row = lax.broadcasted_iota(jnp.int32, (TILE, TILE), 0)
    column = lax.broadcasted_iota(jnp.int32, (TILE, TILE), 1)
    for h in range(PAIR):
        lanes = slice(h * DH, (h + 1) * DH)
        near[...] = jnp.zeros_like(near)

        def one_block(i, _, h=h, lanes=lanes):
            start = pl.multiple_of(i * TILE, TILE)
            q_i = q_ref[pl.ds(start, TILE), lanes]
            do_i = do_ref[pl.ds(start, TILE), lanes]
            seg_i = segq_ref[pl.ds(i, 1), :]
            log_i = log_ref[0, h, pl.ds(i, 1), :]
            delta = jnp.zeros((8, TILE), f32)
            for a in range(blocks):
                here = slice(a * TILE, (a + 1) * TILE)
                s, _ = score_tile(base, h, a, i, q_i, k_ref, segk_ref, seg_i, tiles_ref)
                p = jnp.exp(s - log_i)
                dp = lax.dot_general(v_ref[here, lanes], do_i, NT, preferred_element_type=f32)
                delta = delta + fold(p * dp, jnp.sum)
                p_scr[here, :] = p
                dp_scr[here, :] = dp
                p_all[here, pl.ds(start, TILE)] = p.astype(bf16)
            delta = jnp.sum(delta, axis=0, keepdims=True)
            for a in range(blocks):
                here = slice(a * TILE, (a + 1) * TILE)
                ds = (p_scr[here, :] * (dp_scr[here, :] - delta)).astype(bf16)
                ds_all[here, pl.ds(start, TILE)] = ds
                kind = tile_class(base, jnp.int32(a), i)
                near[kind] = near[kind] + ds.astype(f32)
            return 0

        lax.fori_loop(0, blocks, one_block, 0)
        q_h, do_h = q_ref[:, lanes], do_ref[:, lanes]
        k_t = k_ref[:, lanes].astype(f32).T.astype(bf16)

        def products(a, _, lanes=lanes, q_h=q_h, do_h=do_h, k_t=k_t, h=h):
            here = pl.ds(pl.multiple_of(a * 2 * TILE, 2 * TILE), 2 * TILE)
            dv = jnp.dot(p_all[here, :], do_h, preferred_element_type=f32)
            dk = jnp.dot(ds_all[here, :], q_h, preferred_element_type=f32)
            dq = jnp.dot(k_t, ds_all[:, here], preferred_element_type=f32).T
            for kind, grad in enumerate((dq, dk, dv)):
                first = kind * PAIR * DH + h * DH
                grad_ref[here, first : first + DH] = grad.astype(bf16)
            return 0

        lax.fori_loop(0, blocks // 2, products, 0)
        for b in range(BUCKETS):
            part = jnp.zeros((8, TILE), f32)
            low = b < BUCKETS // 2
            for kind in (1, 2) if low else (2, 3):
                bucket = bucket_index(row - column + (kind - 2) * TILE)
                part = part + fold(jnp.where(bucket == b, near[kind], 0.0), jnp.sum)
            if b == BUCKETS // 2 - 1:
                part = part + fold(near[0], jnp.sum)
            if b == BUCKETS - 1:
                part = part + fold(near[4], jnp.sum)
            bias_ref[h, b] = part


def attend_back(base, pair, qkv, context_grad, log_total, seg_keys, seg_queries, tiles, earlier=None):
    rows, width = context_grad.shape
    blocks = rows // TILE

    def part(kind):
        return pl.BlockSpec((rows, PAIR * DH), lambda j: (0, 3 * pair + kind))

    specs = [
        pl.BlockSpec(memory_space=pltpu.SMEM),
        part(0),
        part(1),
        part(2),
        pl.BlockSpec((rows, PAIR * DH), lambda j: (0, pair)),
        pl.BlockSpec((1, PAIR, blocks, TILE), lambda j: (pair, 0, 0, 0)),
        pl.BlockSpec((rows, TILE), lambda j: (0, 0)),
        pl.BlockSpec((blocks, TILE), lambda j: (0, 0)),
        pl.BlockSpec((PAIR, CLASSES, TILE, TILE), lambda j: (pair, 0, 0, 0)),
    ]
    operands = [base, qkv, qkv, qkv, context_grad, log_total, seg_keys, seg_queries, tiles]
    aliases = {}
    if earlier is not None:
        specs.append(pl.BlockSpec(memory_space=pl.ANY))
        operands.append(earlier)
        aliases = {len(operands) - 1: 0}
    return pl.pallas_call(
        functools.partial(backward_kernel, kept=len(aliases)),
        grid=(1,),
        out_shape=(
            jax.ShapeDtypeStruct((rows, 3 * width), bf16),
            jax.ShapeDtypeStruct((PAIR, BUCKETS, 8, TILE), f32),
        ),
        in_specs=specs,
        out_specs=(
            pl.BlockSpec((rows, 3 * PAIR * DH), lambda j: (0, pair)),
            pl.BlockSpec((PAIR, BUCKETS, 8, TILE), lambda j: (0, 0, 0, 0)),
        ),
        scratch_shapes=[
            pltpu.VMEM((rows, TILE), f32),
            pltpu.VMEM((rows, TILE), f32),
            pltpu.VMEM((rows, rows), bf16),
            pltpu.VMEM((rows, rows), bf16),
            pltpu.VMEM((CLASSES, TILE, TILE), f32),
        ],
        input_output_aliases=aliases,
        compiler_params=pltpu.CompilerParams(vmem_limit_bytes=VMEM_BYTES),
        name="attend_backward",
    )(*operands)


def per_device(
    inputs,
    doc_lengths,
    gain_attn,
    w_query,
    w_key,
    w_value,
    w_out,
    bias_table,
    gain_ff,
    w_gate,
    w_up,
    w_down,
    cotangent,
):
    rows, width = inputs.shape
    planes, members = lax.axis_size("fsdp"), lax.axis_size("ctx")
    me = lax.axis_index("ctx")
    length = rows * members
    heads = H // members
    hidden = w_gate.shape[1] // members
    model = heads * DH
    striped = H == planes * members == BUCKETS

    def own_rows(weight):
        count = weight.shape[0] // members
        return lax.dynamic_slice_in_dim(weight, me * count, count, 0)

    def over_planes(weight):
        return lax.all_gather(weight, "fsdp", axis=0, tiled=True)

    def sum_planes(partial):
        return lax.psum_scatter(partial, "fsdp", scatter_dimension=0, tiled=True)

    def trade(summed):
        moved = summed.reshape(members, -1, summed.shape[1])
        return lax.all_to_all(moved, "ctx", 0, 0, tiled=True)

    head_pieces = planes if striped else 1
    of_heads = head_moves(head_pieces, heads)
    of_hidden = block_moves(2, planes, hidden // planes)
    if striped:
        own_qkv = cut_heads_at_once(w_query, w_key, w_value, w_out, planes, members)
    else:
        own_qkv = cut_columns(
            [w_query, w_key, w_value], head_pieces, me, members, of_heads, "cut_heads"
        )
    if striped:
        gathered = over_planes(own_qkv)
        w_qkv = gathered[:, : 3 * model]
        lanes = gathered.shape[1] - 3 * model
        out_rows = gathered[:, 3 * model :].reshape(planes, width // lanes, -1, lanes)
        out_rows = jnp.transpose(out_rows, (0, 2, 1, 3)).reshape(model, width)
    else:
        w_qkv = over_planes(own_qkv)
        out_rows = lax.dynamic_slice_in_dim(over_planes(w_out), me * model, model, 0)
    w_mix = over_planes(cut_columns([w_gate, w_up], planes, me, members, of_hidden, "cut_hidden"))
    down_rows = over_planes(own_rows(w_down))
    gains = line_gather(after(jnp.stack([gain_attn, gain_ff]), own_qkv)).astype(f32)
    gain_first, gain_second = gains[0], gains[1]

    base = me if by_exchange() else jnp.zeros_like(me)
    slots = jnp.arange(members, dtype=jnp.int32)
    segments = segment_table(doc_lengths[0], length).reshape(members, rows)
    seg_queries = jnp.take(segments, lax.bitwise_xor(base, slots), axis=0)
    seg_queries = seg_queries.reshape(length // TILE, TILE)
    seg_keys = jnp.broadcast_to(seg_queries.reshape(length, 1), (length, TILE))
    base_block = jnp.reshape(base, (1,)).astype(jnp.int32)
    if striped:
        unit = H // (planes * members)
        order = jnp.arange(heads, dtype=jnp.int32)
        own_heads = order // unit * (H // planes) + me * unit + order % unit
    else:
        own_heads = me * heads + jnp.arange(heads, dtype=jnp.int32)
    pick = (jnp.arange(H, dtype=jnp.int32)[:, None] == own_heads[None, :]).astype(f32)
    table = jnp.dot(bias_table.astype(f32), pick, precision=lax.Precision.HIGHEST)
    tiles = bias_tiles(table)

    inputs, cotangent = lax.optimization_barrier((inputs, cotangent, own_qkv))[:2]
    source_all = plane_gather(inputs)
    normed = rms_scale(source_all.astype(f32), gain_first).astype(bf16)
    grad_all = plane_gather(after(cotangent, source_all))
    normed = after(normed, grad_all, tiles)
    qkv = dot(normed, w_qkv).astype(bf16)
    context_t, log_total = attend(base_block, qkv, seg_keys, seg_queries, tiles)
    source = inputs.astype(f32)
    residual = source + plane_scatter(dot(context_t, out_rows, ((0,), (0,))).astype(bf16))

    normed_ff = plane_gather(rms_scale(residual, gain_second).astype(bf16))
    mix = dot(normed_ff, w_mix)
    gate_pre, up_pre = mix[:, :hidden], mix[:, hidden:]
    active_f, mix_back = jax.vjp(gated_mix, gate_pre, up_pre)
    active = active_f.astype(bf16)
    down_grad = dot(active, grad_all, ((0,), (0,))).astype(bf16)
    down_sum = sum_planes(down_grad)
    active_grad = dot(after(grad_all, down_grad), down_rows, ((1,), (1,)))
    gate_grad, up_grad = mix_back(active_grad)
    mix_grad = jnp.concatenate([gate_grad.astype(bf16), up_grad.astype(bf16)], axis=1)
    normed_ff_part = dot(mix_grad, w_mix, ((1,), (1,))).astype(bf16)
    normed_ff_grad = plane_scatter(normed_ff_part)
    mix_grad = after(mix_grad, normed_ff_part)
    mix_weight_grad = dot(normed_ff, mix_grad, ((0,), (0,))).astype(bf16)
    mix_sum = sum_planes(mix_weight_grad)
    norm_back = jax.vjp(lambda v: rms_scale(v, gain_second), residual)[1]
    residual_grad = cotangent.astype(f32) + norm_back(normed_ff_grad)[0]

    residual_low = plane_gather(after(residual_grad.astype(bf16), down_sum, mix_weight_grad))
    output_part = dot(after(active, mix_weight_grad), down_rows).astype(bf16)
    context_grad = dot(after(residual_low, output_part), out_rows, ((1,), (1,))).astype(bf16)
    output_sums = scatter_chips(after(output_part, residual_low))

    def back(pair, grad, earlier=None):
        return attend_back(
            base_block, pair, qkv, grad, log_total, seg_keys, seg_queries, tiles, earlier
        )

    qkv_grad, bias_parts = back(0, context_grad)
    bias_parts = [bias_parts]
    for pair in range(1, heads // PAIR):
        context_grad = after(context_grad, qkv_grad, output_sums)
        qkv_grad, more = back(pair, context_grad, qkv_grad)
        bias_parts.append(more)
    bias_parts = jnp.concatenate(bias_parts, axis=0)
    qkv_weight_grad = dot(normed, qkv_grad, ((0,), (0,))).astype(bf16)
    bias_own = jnp.sum(bias_parts, axis=(2, 3))
    qkv_sent = qkv_weight_grad
    if striped:
        bias_own = bias_own.T.astype(bf16).reshape(planes, members, heads)
        bias_own = jnp.pad(bias_own, ((0, 0), (0, 0), (0, 3 * model - heads)))
        qkv_sent = qkv_sent.reshape(planes, -1, 3 * model)
        qkv_sent = jnp.concatenate([qkv_sent, bias_own], axis=1).reshape(-1, 3 * model)
    qkv_sum = sum_planes(qkv_sent)
    normed_part = dot(after(qkv_grad, qkv_weight_grad), w_qkv, ((1,), (1,))).astype(bf16)
    normed_sums, mix_sum, output_sums = lax.optimization_barrier(
        (scatter_corner(scatter_chips(normed_part)), mix_sum, scatter_corner(output_sums))
    )
    out_weight_grad = dot(context_t, after_all((residual_low,), normed_sums)[0]).astype(bf16)
    moved_mix = trade(mix_sum)
    normed_grad, moved_mix, output_sum = lax.optimization_barrier(
        (scatter_sides(normed_sums), moved_mix, scatter_sides(output_sums))
    )
    output = (residual + output_sum).astype(bf16)
    gate_shard, up_shard = join_columns(moved_mix, 2, planes, of_hidden, "join_hidden")
    qkv_sum = after(qkv_sum, normed_grad)
    if striped:
        own = width // planes
        moved_qkv = [qkv_sum[:own].reshape(members, -1, 3 * model), qkv_sum[own:][:, None]]
        moved_qkv = jnp.concatenate(moved_qkv, axis=1)
        moved_qkv = lax.all_to_all(moved_qkv, "ctx", 0, 0, tiled=True)
        bias_shard = moved_qkv[:, -1, :heads].astype(f32).T.reshape(-1)
        moved_qkv = moved_qkv[:, :-1]
    else:
        moved_qkv = trade(qkv_sum)
        bias_rows = jnp.dot(bias_own.T, pick.T, precision=lax.Precision.HIGHEST).reshape(-1)
        bias_shard = lax.psum_scatter(bias_rows, ("fsdp", "ctx"), scatter_dimension=0, tiled=True)
    first_back = jax.vjp(lambda v: rms_scale(v, gain_first), source)[1]
    input_grad = (residual_grad + first_back(normed_grad)[0]).astype(bf16)

    def gain_grad(gain, pairs):
        products = sum(own_rows(w).astype(f32) * g for w, g in pairs)
        return jnp.sum(products, axis=1) / own_rows(gain).astype(f32)

    down_shard = down_sum.astype(f32)
    ff_gain_shard = gain_grad(gain_ff, ((w_gate, gate_shard), (w_up, up_shard)))
    query_shard, key_shard, value_shard = join_columns(
        moved_qkv, 3, head_pieces, of_heads, "join_heads"
    )
    attn_gain_shard = gain_grad(
        gain_attn, ((w_query, query_shard), (w_key, key_shard), (w_value, value_shard))
    )
    if striped:
        out_shard = after(sum_planes(out_weight_grad), attn_gain_shard).astype(f32)
    else:
        placed = jnp.zeros((H * DH, width), f32)
        placed = lax.dynamic_update_slice_in_dim(placed, out_weight_grad.astype(f32), me * model, 0)
        out_shard = lax.psum_scatter(placed, ("fsdp", "ctx"), scatter_dimension=0, tiled=True)
    return (
        output,
        input_grad,
        attn_gain_shard,
        ff_gain_shard,
        query_shard,
        key_shard,
        value_shard,
        out_shard,
        bias_shard,
        gate_shard,
        up_shard,
        down_shard,
    )


def solution(mesh):
    rows = P(("fsdp", "ctx"), None)
    vector = P(("fsdp", "ctx"))
    weight = P("fsdp", None)
    return jax.shard_map(
        per_device,
        mesh=mesh,
        in_specs=(
            rows,
            P("fsdp", None),
            P("fsdp"),
            weight,
            weight,
            weight,
            weight,
            P(),
            P("fsdp"),
            weight,
            weight,
            weight,
            rows,
        ),
        out_specs=(rows, rows, vector, vector, rows, rows, rows, rows, vector, rows, rows, rows),
        check_vma=False,
    )
```

```python
import functools

import jax
import jax.numpy as jnp
from jax import lax
from jax.experimental import pallas as pl
from jax.experimental.pallas import tpu as pltpu
from jax.sharding import PartitionSpec as P

H = 32
DH = 64
BUCKETS = 32
TILE = 128
PAIR = 2
CLASSES = 5

epsilon = 1e-06
score_masked_rows = -1000000000.0
bucket_edges = (12, 16, 23, 32, 46, 64, 91)
f32 = jnp.float32
bf16 = jnp.bfloat16
NT = (((1,), (1,)), ((), ()))
VMEM_BYTES = 56 * 1024 * 1024


def bucket_index(offset):
    distance = jnp.abs(offset)
    far_bucket = BUCKETS // 4 + sum(
        ((distance >= boundary).astype(jnp.int32) for boundary in bucket_edges)
    )
    within = jnp.where(distance < BUCKETS // 4, distance, far_bucket)
    return within + BUCKETS // 2 * (offset > 0).astype(jnp.int32)


def rms_scale(values, gain_row):
    mean_square = jnp.mean(values * values, axis=-1, keepdims=True)
    return values * lax.rsqrt(mean_square + epsilon) * gain_row


def gated_mix(gate_part, up_part):
    return jax.nn.gelu(gate_part, approximate=True) * up_part


def segment_table(doc_row, total_rows):
    doc_ends = jnp.cumsum(doc_row)
    positions = jnp.arange(total_rows, dtype=jnp.int32)
    return jnp.sum((positions[:, None] >= doc_ends[None, :]).astype(jnp.int32), axis=1)


def dot(left, right, contract=((1,), (0,))):
    return lax.dot_general(left, right, (contract, ((), ())), preferred_element_type=f32)


def swap(block, mask):
    return lax.ppermute(block, "ctx", [(i, i ^ mask) for i in range(lax.axis_size("ctx"))])


def by_exchange():
    return lax.axis_size("ctx") == 8


def plane_gather(block):
    if not by_exchange():
        return lax.all_gather(block, "ctx", axis=0, tiled=True)
    half = block.shape[0] // 2
    from_x, from_y, from_core = swap(block, 2), swap(block, 4), swap(block, 1)
    diagonal = jnp.concatenate([swap(from_x[:half], 4), swap(from_y[half:], 2)], axis=0)
    x_core, y_core = swap(from_x, 1), swap(from_y, 1)
    return jnp.concatenate(
        [block, from_core, from_x, x_core, from_y, y_core, diagonal, swap(diagonal, 1)], axis=0
    )


def scatter_chips(partial):
    if not by_exchange():
        return partial
    rows = partial.shape[0] // 8

    def chip(m):
        mine, other = partial[m * rows : (m + 1) * rows], partial[(m + 1) * rows : (m + 2) * rows]
        return mine.astype(f32) + swap(other, 1).astype(f32)

    diagonal = chip(6).astype(bf16)
    return [chip(0), chip(2), chip(4), diagonal]


def scatter_corner(sums):
    if not by_exchange():
        return sums
    own, x_sum, y_sum, diagonal = sums
    half = own.shape[0] // 2
    via_x, via_y = swap(diagonal[:half], 2), swap(diagonal[half:], 4)
    y_sum = jnp.concatenate([y_sum[:half] + via_x.astype(f32), y_sum[half:]], axis=0)
    x_sum = jnp.concatenate([x_sum[:half], x_sum[half:] + via_y.astype(f32)], axis=0)
    return [own, x_sum.astype(bf16), y_sum.astype(bf16)]


def scatter_sides(sums):
    if not by_exchange():
        return lax.psum_scatter(sums, "ctx", scatter_dimension=0, tiled=True).astype(f32)
    own, x_sum, y_sum = sums
    return own + swap(x_sum, 2).astype(f32) + swap(y_sum, 4).astype(f32)


def plane_scatter(partial):
    return scatter_sides(scatter_corner(scatter_chips(partial)))


def line_gather(small):
    parts = lax.axis_size("fsdp")
    own = lax.axis_index("fsdp")
    whole = jnp.zeros((parts,) + small.shape, small.dtype)
    for step in range(parts):
        piece = (
            small
            if step == 0
            else lax.ppermute(small, "fsdp", [(i, (i + step) % parts) for i in range(parts)])
        )
        whole = lax.dynamic_update_index_in_dim(whole, piece, (own - step) % parts, 0)
    return jnp.transpose(whole, (1, 0, 2)).reshape(small.shape[0], -1)


def cut_plan(cut, members):
    window = max(-(-((cut * p) % TILE + cut) // TILE) for p in range(members))
    return window, members * cut // TILE - window


def cut_kernel(start_ref, *refs, pieces, window, cut, moves, along):
    out_ref = refs[-1]
    if along:
        rows_ref = refs[-2]
        count, groups = rows_ref.shape[0], rows_ref.shape[1] // along
        for group in range(groups):
            part = rows_ref[:, group * along : (group + 1) * along]
            out_ref[group * count : (group + 1) * count, out_ref.shape[1] - along :] = part
    shift = start_ref[1]
    held = {}
    for source, piece, first, length, target in moves:
        if (source, piece) not in held:
            at = (source * pieces + piece) * window
            span = jnp.concatenate([r[...].astype(f32) for r in refs[at : at + window]], axis=1)
            held[source, piece] = pltpu.roll(span, shift, 1)
        part = held[source, piece][:, first : first + length]
        out_ref[:, target : target + length] = part.astype(bf16)


def cut_columns(weights, pieces, me, members, moves, name, along=None):
    rows, width = weights[0].shape
    cut = width // (pieces * members)
    window, most = cut_plan(cut, members)
    blocks = width // pieces // TILE
    start = jnp.minimum(cut * me // TILE, most)
    shift = (window * TILE - (cut * me - start * TILE)) % (window * TILE)
    step = min(rows, 256)
    specs = []
    for _ in weights:
        for piece in range(pieces):
            for w in range(window):
                place = piece * blocks + w
                specs.append(pl.BlockSpec((step, TILE), lambda r, s, place=place: (r, place + s[0])))
    columns = sum(move[3] for move in moves)
    operands = [w for w in weights for _ in range(pieces * window)]
    extra = 0
    if along is not None:
        count = along.shape[0] // members
        extra = count * along.shape[1] // rows
        columns += extra
        specs.append(pl.BlockSpec((count, step // count * extra), lambda r, s: (s[2], r)))
        operands.append(along)
    return pl.pallas_call(
        functools.partial(
            cut_kernel, pieces=pieces, window=window, cut=cut, moves=moves, along=extra
        ),
        grid_spec=pltpu.PrefetchScalarGridSpec(
            num_scalar_prefetch=1,
            grid=(rows // step,),
            in_specs=specs,
            out_specs=pl.BlockSpec((step, columns), lambda r, s: (r, 0)),
        ),
        out_shape=jax.ShapeDtypeStruct((rows, columns), bf16),
        name=name,
    )(jnp.stack([start, shift, me]).astype(jnp.int32), *operands)


def cut_heads_kernel(
    q_ref, k_ref, v_ref, rows_ref, out_ref, held, held_rows, made, sems, out_sems, *, pieces, members
):
    me = lax.axis_index("ctx")
    tiles = members * DH // TILE
    weights = (q_ref, k_ref, v_ref)
    count = held_rows.shape[0]
    copies = []
    for source, weight in enumerate(weights):
        for piece in range(pieces):
            first = pl.multiple_of((piece * tiles + me * DH // TILE) * TILE, TILE)
            at = source * pieces + piece
            copies.append(
                pltpu.make_async_copy(weight.at[:, pl.ds(first, TILE)], held.at[at], sems.at[at])
            )
    first = pl.multiple_of(me * count, count)
    copies.append(
        pltpu.make_async_copy(
            rows_ref.at[pl.ds(first, count), :], held_rows, sems.at[len(weights) * pieces]
        )
    )
    for copy in copies:
        copy.start()
    sent = []

    def send(first, columns, values):
        made[:, first : first + columns] = values
        part = (slice(None), slice(first, first + columns))
        copy = pltpu.make_async_copy(made.at[part], out_ref.at[part], out_sems.at[len(sent)])
        copy.start()
        sent.append(copy)

    row = lax.broadcasted_iota(jnp.int32, (TILE, TILE), 0)
    column = lax.broadcasted_iota(jnp.int32, (TILE, TILE), 1)
    same = row - lax.rem(me * DH, TILE) == lax.rem(column, DH)
    pick = [(same & (column // DH == side)).astype(bf16) for side in range(2)]
    for source in range(len(weights)):
        for pair in range(pieces // 2):
            at = source * pieces + 2 * pair
            copies[at].wait()
            copies[at + 1].wait()
            both = jnp.dot(held[at], pick[0], preferred_element_type=f32)
            both = both + jnp.dot(held[at + 1], pick[1], preferred_element_type=f32)
            send((pair * 3 + source) * TILE, TILE, both.astype(bf16))
    copies[-1].wait()
    first = len(weights) * pieces * DH
    along = made.shape[1] - first
    parts = [
        held_rows[:, group * along : (group + 1) * along]
        for group in range(held_rows.shape[1] // along)
    ]
    send(first, along, jnp.concatenate(parts, axis=0))
    for copy in sent:
        copy.wait()


def cut_heads_at_once(w_query, w_key, w_value, w_out, pieces, members):
    rows, width = w_query.shape
    count = w_out.shape[0] // members
    columns = 3 * pieces * DH + count * width // rows
    return pl.pallas_call(
        functools.partial(cut_heads_kernel, pieces=pieces, members=members),
        out_shape=jax.ShapeDtypeStruct((rows, columns), bf16),
        in_specs=[pl.BlockSpec(memory_space=pl.ANY)] * 4,
        out_specs=pl.BlockSpec(memory_space=pl.ANY),
        scratch_shapes=[
            pltpu.VMEM((3 * pieces, rows, TILE), bf16),
            pltpu.VMEM((count, width), bf16),
            pltpu.VMEM((rows, columns), bf16),
            pltpu.SemaphoreType.DMA((3 * pieces + 1,)),
            pltpu.SemaphoreType.DMA((3 * pieces // 2 + 1,)),
        ],
        compiler_params=pltpu.CompilerParams(vmem_limit_bytes=VMEM_BYTES),
        name="cut_heads",
    )(w_query, w_key, w_value, w_out)


def join_kernel(in_ref, *out_refs, pieces, cut, moves):
    members = in_ref.shape[0]
    for kind, piece, first, length, source in moves:
        for p in range(members):
            target = (piece * members + p) * cut + first
            out_refs[kind][:, target : target + length] = in_ref[p, :, source : source + length].astype(f32)


def join_columns(moved, kinds, pieces, moves, name):
    members, rows, columns = moved.shape
    cut = columns // (kinds * pieces)
    step = min(rows, 32)
    width = members * pieces * cut
    return pl.pallas_call(
        functools.partial(join_kernel, pieces=pieces, cut=cut, moves=moves),
        grid=(rows // step,),
        out_shape=[jax.ShapeDtypeStruct((rows, width), f32)] * kinds,
        in_specs=[pl.BlockSpec((members, step, columns), lambda r: (0, r, 0))],
        out_specs=[pl.BlockSpec((step, width), lambda r: (r, 0))] * kinds,
        name=name,
    )(moved)


def head_moves(pieces, heads):
    each = heads // pieces
    return [
        (kind, t // each, t % each * DH, DH, (t // PAIR * 3 + kind) * PAIR * DH + t % PAIR * DH)
        for t in range(heads)
        for kind in range(3)
    ]


def block_moves(kinds, pieces, cut):
    return [
        (kind, piece, 0, cut, (kind * pieces + piece) * cut)
        for kind in range(kinds)
        for piece in range(pieces)
    ]


def after_all(values, *others):
    return lax.optimization_barrier((values,) + others)[0]


def after(value, *others):
    return lax.optimization_barrier((value,) + others)[0]


def tiles_kernel(table_ref, out_ref):
    heads = out_ref.shape[0]
    row = lax.broadcasted_iota(jnp.int32, (TILE, TILE), 0)
    column = lax.broadcasted_iota(jnp.int32, (TILE, TILE), 1)

    def one_head(h, _):
        for kind in range(CLASSES):
            bucket = bucket_index(row - column + (kind - 2) * TILE)
            first, last = (0, BUCKETS // 2) if kind < 2 else (BUCKETS // 2, BUCKETS)
            if kind == 2:
                first = 0
            tile = jnp.zeros((TILE, TILE), f32)
            for b in range(first, last):
                tile = jnp.where(bucket == b, table_ref[b, h], tile)
            out_ref[h, kind] = tile
        return 0

    lax.fori_loop(0, heads, one_head, 0)


def bias_tiles(table):
    heads = table.shape[1]
    return pl.pallas_call(
        tiles_kernel,
        out_shape=jax.ShapeDtypeStruct((heads, CLASSES, TILE, TILE), f32),
        in_specs=[pl.BlockSpec(memory_space=pltpu.SMEM)],
        out_specs=pl.BlockSpec(memory_space=pltpu.VMEM),
        name="bias_tiles",
    )(table)


def fold(tile, reduce):
    return reduce(tile.reshape(TILE // 8, 8, TILE), axis=0)


def tile_class(base, key_slot, query_slot):
    difference = lax.bitwise_xor(base, key_slot) - lax.bitwise_xor(base, query_slot)
    return jnp.clip(difference, -2, 2) + 2


def score_tile(base, h, a, i, q_i, k_ref, seg_keys, seg_i, tiles_ref):
    s = lax.dot_general(
        k_ref[a * TILE : (a + 1) * TILE, h * DH : (h + 1) * DH], q_i, NT, preferred_element_type=f32
    )
    kind = tile_class(base, jnp.int32(a), i)
    s = s + tiles_ref[h, kind]
    return jnp.where(seg_keys[a * TILE : (a + 1) * TILE, :] == seg_i, s, score_masked_rows), kind


def forward_kernel(base_ref, q_ref, k_ref, v_ref, segk_ref, segq_ref, tiles_ref, ctx_ref, log_ref, s_scr, p_scr):
    blocks = q_ref.shape[0] // TILE
    base = base_ref[0]
    for h in range(PAIR):
        v_t = v_ref[:, h * DH : (h + 1) * DH].astype(f32).T.astype(bf16)

        def one_block(i, _, h=h, v_t=v_t):
            start = pl.multiple_of(i * TILE, TILE)
            q_i = q_ref[pl.ds(start, TILE), h * DH : (h + 1) * DH]
            seg_i = segq_ref[pl.ds(i, 1), :]
            top = jnp.full((8, TILE), -jnp.inf, f32)
            for a in range(blocks):
                s, _ = score_tile(base, h, a, i, q_i, k_ref, segk_ref, seg_i, tiles_ref)
                s_scr[a * TILE : (a + 1) * TILE, :] = s
                top = jnp.maximum(top, fold(s, jnp.max))
            top = jnp.max(top, axis=0, keepdims=True)
            total = jnp.zeros((8, TILE), f32)
            for a in range(blocks):
                e = jnp.exp(s_scr[a * TILE : (a + 1) * TILE, :] - top)
                p_scr[a * TILE : (a + 1) * TILE, :] = e.astype(bf16)
                total = total + fold(e, jnp.sum)
            total = jnp.sum(total, axis=0, keepdims=True)
            context = lax.dot_general(
                v_t, p_scr[...], (((1,), (0,)), ((), ())), preferred_element_type=f32
            )
            ctx_ref[h * DH : (h + 1) * DH, pl.ds(start, TILE)] = (context / total).astype(bf16)
            log_ref[0, h, pl.ds(i, 1), :] = top + jnp.log(total)
            return 0

        lax.fori_loop(0, blocks, one_block, 0)


def of_pair(rows, kind):
    return pl.BlockSpec((rows, PAIR * DH), lambda j: (0, 3 * j + kind))


def attend(base, qkv, seg_keys, seg_queries, tiles):
    rows, width = qkv.shape[0], qkv.shape[1] // 3
    pairs, blocks = width // (PAIR * DH), rows // TILE
    return pl.pallas_call(
        forward_kernel,
        grid=(pairs,),
        out_shape=(
            jax.ShapeDtypeStruct((width, rows), bf16),
            jax.ShapeDtypeStruct((pairs, PAIR, blocks, TILE), f32),
        ),
        in_specs=[
            pl.BlockSpec(memory_space=pltpu.SMEM),
            of_pair(rows, 0),
            of_pair(rows, 1),
            of_pair(rows, 2),
            pl.BlockSpec((rows, TILE), lambda j: (0, 0)),
            pl.BlockSpec((blocks, TILE), lambda j: (0, 0)),
            pl.BlockSpec((PAIR, CLASSES, TILE, TILE), lambda j: (j, 0, 0, 0)),
        ],
        out_specs=(
            pl.BlockSpec((PAIR * DH, rows), lambda j: (j, 0)),
            pl.BlockSpec((1, PAIR, blocks, TILE), lambda j: (j, 0, 0, 0)),
        ),
        scratch_shapes=[pltpu.VMEM((rows, TILE), f32), pltpu.VMEM((rows, TILE), bf16)],
        compiler_params=pltpu.CompilerParams(vmem_limit_bytes=VMEM_BYTES),
        name="attend_forward",
    )(base, qkv, qkv, qkv, seg_keys, seg_queries, tiles)


def backward_kernel(
    base_ref, q_ref, k_ref, v_ref, do_ref, log_ref, segk_ref, segq_ref, tiles_ref,
    *rest, kept,
):
    grad_ref, bias_ref, p_scr, dp_scr, p_all, ds_all, near = rest[kept:]
    rows = q_ref.shape[0]
    blocks = rows // TILE
    base = base_ref[0]
    row = lax.broadcasted_iota(jnp.int32, (TILE, TILE), 0)
    column = lax.broadcasted_iota(jnp.int32, (TILE, TILE), 1)
    for h in range(PAIR):
        lanes = slice(h * DH, (h + 1) * DH)
        near[...] = jnp.zeros_like(near)

        def one_block(i, _, h=h, lanes=lanes):
            start = pl.multiple_of(i * TILE, TILE)
            q_i = q_ref[pl.ds(start, TILE), lanes]
            do_i = do_ref[pl.ds(start, TILE), lanes]
            seg_i = segq_ref[pl.ds(i, 1), :]
            log_i = log_ref[0, h, pl.ds(i, 1), :]
            delta = jnp.zeros((8, TILE), f32)
            for a in range(blocks):
                here = slice(a * TILE, (a + 1) * TILE)
                s, _ = score_tile(base, h, a, i, q_i, k_ref, segk_ref, seg_i, tiles_ref)
                p = jnp.exp(s - log_i)
                dp = lax.dot_general(v_ref[here, lanes], do_i, NT, preferred_element_type=f32)
                delta = delta + fold(p * dp, jnp.sum)
                p_scr[here, :] = p
                dp_scr[here, :] = dp
                p_all[here, pl.ds(start, TILE)] = p.astype(bf16)
            delta = jnp.sum(delta, axis=0, keepdims=True)
            for a in range(blocks):
                here = slice(a * TILE, (a + 1) * TILE)
                ds = (p_scr[here, :] * (dp_scr[here, :] - delta)).astype(bf16)
                ds_all[here, pl.ds(start, TILE)] = ds
                kind = tile_class(base, jnp.int32(a), i)
                near[kind] = near[kind] + ds.astype(f32)
            return 0

        lax.fori_loop(0, blocks, one_block, 0)
        q_h, do_h = q_ref[:, lanes], do_ref[:, lanes]
        k_t = k_ref[:, lanes].astype(f32).T.astype(bf16)

        def products(a, _, lanes=lanes, q_h=q_h, do_h=do_h, k_t=k_t, h=h):
            here = pl.ds(pl.multiple_of(a * 2 * TILE, 2 * TILE), 2 * TILE)
            dv = jnp.dot(p_all[here, :], do_h, preferred_element_type=f32)
            dk = jnp.dot(ds_all[here, :], q_h, preferred_element_type=f32)
            dq = jnp.dot(k_t, ds_all[:, here], preferred_element_type=f32).T
            for kind, grad in enumerate((dq, dk, dv)):
                first = kind * PAIR * DH + h * DH
                grad_ref[here, first : first + DH] = grad.astype(bf16)
            return 0

        lax.fori_loop(0, blocks // 2, products, 0)
        for b in range(BUCKETS):
            part = jnp.zeros((8, TILE), f32)
            low = b < BUCKETS // 2
            for kind in (1, 2) if low else (2, 3):
                bucket = bucket_index(row - column + (kind - 2) * TILE)
                part = part + fold(jnp.where(bucket == b, near[kind], 0.0), jnp.sum)
            if b == BUCKETS // 2 - 1:
                part = part + fold(near[0], jnp.sum)
            if b == BUCKETS - 1:
                part = part + fold(near[4], jnp.sum)
            bias_ref[h, b] = part


def attend_back(base, pair, qkv, context_grad, log_total, seg_keys, seg_queries, tiles, earlier=None):
    rows, width = context_grad.shape
    blocks = rows // TILE

    def part(kind):
        return pl.BlockSpec((rows, PAIR * DH), lambda j: (0, 3 * pair + kind))

    specs = [
        pl.BlockSpec(memory_space=pltpu.SMEM),
        part(0),
        part(1),
        part(2),
        pl.BlockSpec((rows, PAIR * DH), lambda j: (0, pair)),
        pl.BlockSpec((1, PAIR, blocks, TILE), lambda j: (pair, 0, 0, 0)),
        pl.BlockSpec((rows, TILE), lambda j: (0, 0)),
        pl.BlockSpec((blocks, TILE), lambda j: (0, 0)),
        pl.BlockSpec((PAIR, CLASSES, TILE, TILE), lambda j: (pair, 0, 0, 0)),
    ]
    operands = [base, qkv, qkv, qkv, context_grad, log_total, seg_keys, seg_queries, tiles]
    aliases = {}
    if earlier is not None:
        specs.append(pl.BlockSpec(memory_space=pl.ANY))
        operands.append(earlier)
        aliases = {len(operands) - 1: 0}
    return pl.pallas_call(
        functools.partial(backward_kernel, kept=len(aliases)),
        grid=(1,),
        out_shape=(
            jax.ShapeDtypeStruct((rows, 3 * width), bf16),
            jax.ShapeDtypeStruct((PAIR, BUCKETS, 8, TILE), f32),
        ),
        in_specs=specs,
        out_specs=(
            pl.BlockSpec((rows, 3 * PAIR * DH), lambda j: (0, pair)),
            pl.BlockSpec((PAIR, BUCKETS, 8, TILE), lambda j: (0, 0, 0, 0)),
        ),
        scratch_shapes=[
            pltpu.VMEM((rows, TILE), f32),
            pltpu.VMEM((rows, TILE), f32),
            pltpu.VMEM((rows, rows), bf16),
            pltpu.VMEM((rows, rows), bf16),
            pltpu.VMEM((CLASSES, TILE, TILE), f32),
        ],
        input_output_aliases=aliases,
        compiler_params=pltpu.CompilerParams(vmem_limit_bytes=VMEM_BYTES),
        name="attend_backward",
    )(*operands)


def per_device(
    inputs,
    doc_lengths,
    gain_attn,
    w_query,
    w_key,
    w_value,
    w_out,
    bias_table,
    gain_ff,
    w_gate,
    w_up,
    w_down,
    cotangent,
):
    rows, width = inputs.shape
    planes, members = lax.axis_size("fsdp"), lax.axis_size("ctx")
    me = lax.axis_index("ctx")
    length = rows * members
    heads = H // members
    hidden = w_gate.shape[1] // members
    model = heads * DH
    striped = H == planes * members == BUCKETS

    def own_rows(weight):
        count = weight.shape[0] // members
        return lax.dynamic_slice_in_dim(weight, me * count, count, 0)

    def over_planes(weight):
        return lax.all_gather(weight, "fsdp", axis=0, tiled=True)

    def sum_planes(partial):
        return lax.psum_scatter(partial, "fsdp", scatter_dimension=0, tiled=True)

    def trade(summed):
        moved = summed.reshape(members, -1, summed.shape[1])
        return lax.all_to_all(moved, "ctx", 0, 0, tiled=True)

    head_pieces = planes if striped else 1
    of_heads = head_moves(head_pieces, heads)
    of_hidden = block_moves(2, planes, hidden // planes)
    if striped:
        own_qkv = cut_heads_at_once(w_query, w_key, w_value, w_out, planes, members)
    else:
        own_qkv = cut_columns(
            [w_query, w_key, w_value], head_pieces, me, members, of_heads, "cut_heads"
        )
    if striped:
        gathered = over_planes(own_qkv)
        w_qkv = gathered[:, : 3 * model]
        lanes = gathered.shape[1] - 3 * model
        out_rows = gathered[:, 3 * model :].reshape(planes, width // lanes, -1, lanes)
        out_rows = jnp.transpose(out_rows, (0, 2, 1, 3)).reshape(model, width)
    else:
        w_qkv = over_planes(own_qkv)
        out_rows = lax.dynamic_slice_in_dim(over_planes(w_out), me * model, model, 0)
    w_mix = over_planes(cut_columns([w_gate, w_up], planes, me, members, of_hidden, "cut_hidden"))
    down_rows = over_planes(own_rows(w_down))
    gains = line_gather(after(jnp.stack([gain_attn, gain_ff]), own_qkv)).astype(f32)
    gain_first, gain_second = gains[0], gains[1]

    base = me if by_exchange() else jnp.zeros_like(me)
    slots = jnp.arange(members, dtype=jnp.int32)
    segments = segment_table(doc_lengths[0], length).reshape(members, rows)
    seg_queries = jnp.take(segments, lax.bitwise_xor(base, slots), axis=0)
    seg_queries = seg_queries.reshape(length // TILE, TILE)
    seg_keys = jnp.broadcast_to(seg_queries.reshape(length, 1), (length, TILE))
    base_block = jnp.reshape(base, (1,)).astype(jnp.int32)
    if striped:
        unit = H // (planes * members)
        order = jnp.arange(heads, dtype=jnp.int32)
        own_heads = order // unit * (H // planes) + me * unit + order % unit
    else:
        own_heads = me * heads + jnp.arange(heads, dtype=jnp.int32)
    pick = (jnp.arange(H, dtype=jnp.int32)[:, None] == own_heads[None, :]).astype(f32)
    table = jnp.dot(bias_table.astype(f32), pick, precision=lax.Precision.HIGHEST)
    tiles = bias_tiles(table)

    inputs, cotangent = lax.optimization_barrier((inputs, cotangent, own_qkv))[:2]
    source_all = plane_gather(inputs)
    normed = rms_scale(source_all.astype(f32), gain_first).astype(bf16)
    grad_all = plane_gather(after(cotangent, source_all))
    normed = after(normed, grad_all, tiles)
    qkv = dot(normed, w_qkv).astype(bf16)
    context_t, log_total = attend(base_block, qkv, seg_keys, seg_queries, tiles)
    source = inputs.astype(f32)
    residual = source + plane_scatter(dot(context_t, out_rows, ((0,), (0,))).astype(bf16))

    normed_ff = plane_gather(rms_scale(residual, gain_second).astype(bf16))
    mix = dot(normed_ff, w_mix)
    gate_pre, up_pre = mix[:, :hidden], mix[:, hidden:]
    active_f, mix_back = jax.vjp(gated_mix, gate_pre, up_pre)
    active = active_f.astype(bf16)
    down_grad = dot(active, grad_all, ((0,), (0,))).astype(bf16)
    down_sum = sum_planes(down_grad)
    active_grad = dot(after(grad_all, down_grad), down_rows, ((1,), (1,)))
    gate_grad, up_grad = mix_back(active_grad)
    mix_grad = jnp.concatenate([gate_grad.astype(bf16), up_grad.astype(bf16)], axis=1)
    normed_ff_part = dot(mix_grad, w_mix, ((1,), (1,))).astype(bf16)
    normed_ff_grad = plane_scatter(normed_ff_part)
    mix_grad = after(mix_grad, normed_ff_part)
    mix_weight_grad = dot(normed_ff, mix_grad, ((0,), (0,))).astype(bf16)
    mix_sum = sum_planes(mix_weight_grad)
    norm_back = jax.vjp(lambda v: rms_scale(v, gain_second), residual)[1]
    residual_grad = cotangent.astype(f32) + norm_back(normed_ff_grad)[0]

    residual_low = plane_gather(after(residual_grad.astype(bf16), down_sum, mix_weight_grad))
    output_part = dot(after(active, mix_weight_grad), down_rows).astype(bf16)
    context_grad = dot(after(residual_low, output_part), out_rows, ((1,), (1,))).astype(bf16)
    output_sums = scatter_chips(after(output_part, residual_low))

    def back(pair, grad, earlier=None):
        return attend_back(
            base_block, pair, qkv, grad, log_total, seg_keys, seg_queries, tiles, earlier
        )

    qkv_grad, bias_parts = back(0, context_grad)
    bias_parts = [bias_parts]
    for pair in range(1, heads // PAIR):
        context_grad = after(context_grad, qkv_grad, output_sums)
        qkv_grad, more = back(pair, context_grad, qkv_grad)
        bias_parts.append(more)
    bias_parts = jnp.concatenate(bias_parts, axis=0)
    qkv_weight_grad = dot(normed, qkv_grad, ((0,), (0,))).astype(bf16)
    bias_own = jnp.sum(bias_parts, axis=(2, 3))
    qkv_sent = qkv_weight_grad
    if striped:
        bias_own = bias_own.T.astype(bf16).reshape(planes, members, heads)
        bias_own = jnp.pad(bias_own, ((0, 0), (0, 0), (0, 3 * model - heads)))
        qkv_sent = qkv_sent.reshape(planes, -1, 3 * model)
        qkv_sent = jnp.concatenate([qkv_sent, bias_own], axis=1).reshape(-1, 3 * model)
    qkv_sum = sum_planes(qkv_sent)
    normed_part = dot(after(qkv_grad, qkv_weight_grad), w_qkv, ((1,), (1,))).astype(bf16)
    normed_sums, mix_sum, output_sums = lax.optimization_barrier(
        (scatter_corner(scatter_chips(normed_part)), mix_sum, scatter_corner(output_sums))
    )
    out_weight_grad = dot(context_t, after_all((residual_low,), normed_sums)[0]).astype(bf16)
    moved_mix = trade(mix_sum)
    normed_grad, moved_mix, output_sum = lax.optimization_barrier(
        (scatter_sides(normed_sums), moved_mix, scatter_sides(output_sums))
    )
    output = (residual + output_sum).astype(bf16)
    gate_shard, up_shard = join_columns(moved_mix, 2, planes, of_hidden, "join_hidden")
    qkv_sum = after(qkv_sum, normed_grad)
    if striped:
        own = width // planes
        moved_qkv = [qkv_sum[:own].reshape(members, -1, 3 * model), qkv_sum[own:][:, None]]
        moved_qkv = jnp.concatenate(moved_qkv, axis=1)
        moved_qkv = lax.all_to_all(moved_qkv, "ctx", 0, 0, tiled=True)
        bias_shard = moved_qkv[:, -1, :heads].astype(f32).T.reshape(-1)
        moved_qkv = moved_qkv[:, :-1]
    else:
        moved_qkv = trade(qkv_sum)
        bias_rows = jnp.dot(bias_own.T, pick.T, precision=lax.Precision.HIGHEST).reshape(-1)
        bias_shard = lax.psum_scatter(bias_rows, ("fsdp", "ctx"), scatter_dimension=0, tiled=True)
    first_back = jax.vjp(lambda v: rms_scale(v, gain_first), source)[1]
    input_grad = (residual_grad + first_back(normed_grad)[0]).astype(bf16)

    def gain_grad(gain, pairs):
        products = sum(own_rows(w).astype(f32) * g for w, g in pairs)
        return jnp.sum(products, axis=1) / own_rows(gain).astype(f32)

    down_shard = down_sum.astype(f32)
    ff_gain_shard = gain_grad(gain_ff, ((w_gate, gate_shard), (w_up, up_shard)))
    query_shard, key_shard, value_shard = join_columns(
        moved_qkv, 3, head_pieces, of_heads, "join_heads"
    )
    attn_gain_shard = gain_grad(
        gain_attn, ((w_query, query_shard), (w_key, key_shard), (w_value, value_shard))
    )
    if striped:
        out_shard = after(sum_planes(out_weight_grad), attn_gain_shard).astype(f32)
    else:
        placed = jnp.zeros((H * DH, width), f32)
        placed = lax.dynamic_update_slice_in_dim(placed, out_weight_grad.astype(f32), me * model, 0)
        out_shard = lax.psum_scatter(placed, ("fsdp", "ctx"), scatter_dimension=0, tiled=True)
    return (
        output,
        input_grad,
        attn_gain_shard,
        ff_gain_shard,
        query_shard,
        key_shard,
        value_shard,
        out_shard,
        bias_shard,
        gate_shard,
        up_shard,
        down_shard,
    )


def solution(mesh):
    rows = P(("fsdp", "ctx"), None)
    vector = P(("fsdp", "ctx"))
    weight = P("fsdp", None)
    return jax.shard_map(
        per_device,
        mesh=mesh,
        in_specs=(
            rows,
            P("fsdp", None),
            P("fsdp"),
            weight,
            weight,
            weight,
            weight,
            P(),
            P("fsdp"),
            weight,
            weight,
            weight,
            rows,
        ),
        out_specs=(rows, rows, vector, vector, rows, rows, rows, rows, vector, rows, rows, rows),
        check_vma=False,
    )
```
